256 devices in a mesh: dp: 32 (over z_hi, x, y), tensor: 8 (over z_lo, core).
Axes of the slice: x: 4, y: 4, z: 8 (z_hi: 2, z_lo: 4; z = z_hi * 4 + z_lo), core: 2. Of those that a mesh axis runs over, the one named last changes fastest.
Arguments:
- hidden: bfloat16 [1024, 8192], P('tensor'), may hold values from -6 to 6
- norm_gain: float32 [8192], replicated, may hold values from 0.1 to 1.9
- gate_pre: bfloat16 [1024, 28672], P('tensor', 'dp'), may hold values from -6 to 6
- out_grad: bfloat16 [1024, 28672], P('tensor', 'dp'), may hold values from -6 to 6
- grad_basis: bfloat16 [28672, 14336], P('dp', 'tensor'), may hold values from -0.03125 to 0.03125
- act_basis: bfloat16 [8192, 4096], P('dp'), may hold values from -0.125 to 0.125
Outputs:
- correction: float32 [14336, 4096], P('tensor', 'dp')
The draws below stay inside these ranges and needn't reach their ends.
All inputs are finite; a program needn't handle non-finite values.
Results may differ from the reference program's by a relative error of at most 0.00091.
Values may be sent and summed in bfloat16 or wider, within the bound.
No kernel may reach another device: no remote copies, remote signals or barrier semaphores. Data moves between devices by JAX's collectives and lax.ppermute only.
A program may use at most 128 MiB of HBM per device.

```python
import jax
import jax.numpy as jnp
from jax import lax

D = 8192
FF = 28672
D_WIN = 4096
FF_WIN = 14336
TOKENS = 1024


def strengthened(drawn, own_key, source, target, parts, factor):
    owner, partner = [(jnp.arange(drawn.shape[dim]) // (drawn.shape[dim] // parts)).reshape([-1 if axis == dim else 1 for axis in range(drawn.ndim)]) for dim in (source, target)]
    chosen = jax.random.permutation(own_key, parts)[partner]
    strong = (owner == chosen) | (owner == (partner + parts // 2) % parts)
    return jnp.where(strong, factor * drawn, drawn)


def block_scale(key, shape, split, least, largest):
    def one(position, parts):
        heights = jax.random.uniform(jax.random.fold_in(jax.random.fold_in(key, 6), position), (parts,), jnp.float32, least / len(split), largest / len(split))
        return jnp.repeat(jnp.exp(heights), shape[position] // parts).reshape((-1,) + (1,) * (len(shape) - position - 1))

    gain = one(*split[0])
    for cut in split[1:]:
        gain = gain * one(*cut)
    return gain


def scatter_about(own_key, extent, deviation, most, split=(), kind=jnp.bfloat16):
    array = jax.random.normal(own_key, extent, jnp.float32) * deviation
    if len(split) > 0:
        array = block_scale(own_key, extent, split, -0.22, 0.18) * array
    return jnp.clip(array, min=-most, max=most).astype(kind)


def gaussian_with(stream_key, shape, spread, limit, pieces, heavy, held_as=jnp.bfloat16):
    drawn = spread * jax.random.normal(stream_key, shape, jnp.float32)
    if pieces:
        drawn = drawn * block_scale(stream_key, shape, pieces, -0.22, 0.18)
    return jnp.clip(strengthened(drawn, jax.random.fold_in(stream_key, 3), *heavy), -limit, limit).astype(held_as)


def setup_inputs(seed: int = 0) -> dict:
    key_list = jax.random.split(jax.random.key(seed), 7)
    hidden = scatter_about(key_list[0], (TOKENS, D), 1.0, 6.0, ((0, 8),))
    norm_gain = jnp.clip(1.0 + 0.18 * jax.random.normal(key_list[1], (D,), jnp.float32), 0.1, 1.9)
    gate_pre = scatter_about(key_list[2], (TOKENS, FF), 1.0, 6.0, ((0, 8), (1, 32)))
    out_grad = scatter_about(key_list[3], (TOKENS, FF), 1.0, 6.0, ((0, 8), (1, 32)))
    grad_basis = scatter_about(key_list[4], (FF, FF_WIN), FF ** -0.5, 0.03125, ((0, 32), (1, 8)))
    act_basis = gaussian_with(key_list[5], (D, D_WIN), D ** -0.5, 0.125, ((0, 32),), (0, 1, 32, 2.75))
    return dict(hidden=hidden, norm_gain=norm_gain, gate_pre=gate_pre, out_grad=out_grad, grad_basis=grad_basis, act_basis=act_basis)


def reference(hidden, norm_gain, gate_pre, out_grad, grad_basis, act_basis):
    wide = hidden.astype(jnp.float32)
    stat = lax.optimization_barrier(jnp.mean(wide * wide, axis=-1, keepdims=True))
    normed = (wide * jax.lax.rsqrt(stat + 1e-05) * norm_gain).astype(jnp.bfloat16)
    act_proj = jnp.dot(normed, act_basis, preferred_element_type=jnp.float32)
    act_sq = (act_proj * act_proj).astype(jnp.bfloat16)
    up_grad = (out_grad.astype(jnp.float32) * jax.nn.silu(gate_pre.astype(jnp.float32))).astype(jnp.bfloat16)
    grad_proj = jnp.dot(up_grad, grad_basis, preferred_element_type=jnp.float32)
    grad_sq = (grad_proj * grad_proj).astype(jnp.bfloat16)
    total = jax.lax.dot_general(grad_sq, act_sq, (((0,), (0,)), ((), ())), preferred_element_type=jnp.float32)
    return total / jnp.float32(TOKENS)
```

```python
import jax
import jax.numpy as jnp
from jax import lax
from jax.sharding import Mesh
from jax.sharding import PartitionSpec as P

AXES = ("z_hi", "x", "y", "z_lo", "core")
SIZES = (2, 4, 4, 4, 2)
DP = ("z_hi", "x", "y")
TENSOR = ("z_lo", "core")


def shifted(value, axis, step):
    size = SIZES[AXES.index(axis)]
    return lax.ppermute(value, axis, [(i, (i + step) % size) for i in range(size)])


def act_squares(hidden, norm_gain, act_basis):
    wide = hidden.astype(jnp.float32)
    stat = jnp.mean(wide * wide, axis=-1, keepdims=True)
    width = act_basis.shape[0]
    start = lax.axis_index(DP) * width
    part = lax.dynamic_slice_in_dim(hidden, start, width, 1).astype(jnp.float32)
    gain = lax.dynamic_slice_in_dim(norm_gain, start, width, 0)
    normed = (part * lax.rsqrt(stat + 1e-05) * gain).astype(jnp.bfloat16)
    partial = jnp.dot(normed, act_basis, preferred_element_type=jnp.float32).astype(jnp.bfloat16)
    tokens, columns = partial.shape
    block = columns // 32
    pieces = partial.reshape(tokens, 2, 4, 4, block).transpose(3, 2, 0, 1, 4)
    pieces = pieces.reshape(16, tokens, 2 * block)
    got = lax.all_to_all(pieces, ("y", "x"), 0, 0, tiled=True)
    summed = jnp.sum(got.astype(jnp.float32), axis=0).reshape(tokens, 2, block)
    z_hi = lax.axis_index("z_hi")
    kept = lax.dynamic_index_in_dim(summed, z_hi, 1, keepdims=False)
    given = lax.dynamic_index_in_dim(summed, 1 - z_hi, 1, keepdims=False)
    total = kept + shifted(given.astype(jnp.bfloat16), "z_hi", 1).astype(jnp.float32)
    square = (total * total).astype(jnp.bfloat16)
    spread = lax.all_gather(square, ("x",) + TENSOR, axis=0, tiled=False)
    return spread.reshape(4, 4, 2 * tokens, block)


def per_device(hidden, norm_gain, gate_pre, out_grad, grad_basis, act_basis):
    up_grad = (out_grad.astype(jnp.float32) * jax.nn.silu(gate_pre.astype(jnp.float32))).astype(
        jnp.bfloat16
    )
    moved = [up_grad] + [shifted(up_grad, "z_lo", step) for step in (1, 2, 3)]
    act_sq = act_squares(hidden, norm_gain, act_basis)
    first = lax.axis_index("core") == 0
    partials = []
    for own in moved:
        other = shifted(own, "core", 1)
        rows = jnp.concatenate(
            [jnp.where(first, own, other), jnp.where(first, other, own)], axis=0
        )
        partials.append(
            lax.dot_general(
                grad_basis, rows, (((0,), (1,)), ((), ())), preferred_element_type=jnp.float32
            ).astype(jnp.bfloat16)
        )
    columns, quarter = partials[0].shape
    pieces = jnp.concatenate(partials, axis=0).reshape(16, columns // 4, quarter)
    got = lax.all_to_all(pieces, ("y", "x"), 0, 0, tiled=True)
    summed = jnp.sum(got.astype(jnp.float32), axis=0)
    total = summed + shifted(summed.astype(jnp.bfloat16), "z_hi", 1).astype(jnp.float32)
    square = (total * total).astype(jnp.bfloat16)
    grad_sq = lax.all_to_all(
        jnp.broadcast_to(square[None], (4,) + square.shape), "y", 0, 0, tiled=True
    )
    z_lo = lax.axis_index("z_lo")
    act_by_step = jnp.stack(
        [
            lax.dynamic_index_in_dim(act_sq, lax.rem(z_lo + 4 - step, 4), 1, keepdims=False)
            for step in range(4)
        ]
    )
    out = jnp.einsum("snt,sxtm->xnm", grad_sq, act_by_step, preferred_element_type=jnp.float32)
    out = out / jnp.float32(4 * quarter)
    out = lax.all_to_all(out, "x", 0, 0, tiled=True)
    return out.reshape(columns, -1)


def solution(mesh):
    fine = Mesh(mesh.devices.reshape(SIZES), AXES)
    placed = (
        P(TENSOR, None),
        P(),
        P(TENSOR, DP),
        P(TENSOR, DP),
        P(DP, TENSOR),
        P(DP, None),
    )
    return jax.shard_map(
        per_device, mesh=fine, in_specs=placed, out_specs=P(TENSOR, DP), check_vma=False
    )
```

```python
import jax
import jax.numpy as jnp
from jax import lax
from jax.experimental import pallas as pl
from jax.experimental.pallas import tpu as pltpu
from jax.sharding import Mesh
from jax.sharding import PartitionSpec as P

AXES = ("z_hi", "x", "y", "z_lo", "core")
SIZES = (2, 4, 4, 4, 2)
DP = ("z_hi", "x", "y")
TENSOR = ("z_lo", "core")
VMEM_LIMIT = 48 * 1024 * 1024
SMEM = pl.BlockSpec(memory_space=pltpu.SMEM)
VMEM = pl.BlockSpec(memory_space=pltpu.VMEM)


def shifted(value, axis, step):
    size = SIZES[AXES.index(axis)]
    return lax.ppermute(value, axis, [(i, (i + step) % size) for i in range(size)])


def act_kernel(place, hidden, gain, basis, out):
    tokens, features = hidden.shape
    depth = basis.shape[0]
    squares = jnp.zeros((tokens, 128), jnp.float32)
    for at in range(0, features, 128):
        wide = hidden[:, at : at + 128].astype(jnp.float32)
        squares += wide * wide
    stat = jnp.sum(squares, axis=-1, keepdims=True) / features
    mine = pl.ds(pl.multiple_of(place[0] * depth, depth), depth)
    scaled = hidden[:, mine].astype(jnp.float32) * lax.rsqrt(stat + 1e-05)
    normed = (scaled * gain[:, mine]).astype(jnp.bfloat16)
    block = out.shape[2] // 2
    for z_hi in range(2):
        for x in range(4):
            at = (z_hi * 16 + x * 4) * block
            part = jnp.dot(
                normed, basis[:, at : at + 4 * block], preferred_element_type=jnp.float32
            )
            for y in range(4):
                out[x * 4 + y, :, z_hi * block : (z_hi + 1) * block] = part[
                    :, y * block : (y + 1) * block
                ].astype(jnp.bfloat16)


def grad_kernel(*refs):
    *rows, basis, out = refs
    together = jnp.concatenate([part[...] for part in rows], axis=0)
    for at in range(0, basis.shape[1], 256):
        part = jnp.dot(together, basis[:, at : at + 256], preferred_element_type=jnp.float32)
        out[at : at + 256, :] = part.T.astype(jnp.bfloat16)


def correct_kernel(steps, tokens, *refs):
    place, grad_sq, act_sq, *before, out, act = refs
    block = act_sq.shape[3]
    at = 0
    for step in steps:
        chip = lax.rem(place[0] + 4 - step, 4)
        for flip in range(2):
            core = lax.rem(place[1] + flip, 2)
            for x in range(4):
                act[at : at + block, x * 128 : (x + 1) * 128] = act_sq[chip, core, x]
            at += block
    rows = grad_sq.shape[1]
    for y in range(4):
        part = jnp.dot(grad_sq[y], act[...], preferred_element_type=jnp.float32)
        part = part * (1.0 / tokens)
        for x in range(4):
            here = part[:, x * 128 : (x + 1) * 128]
            if before:
                here = before[0][x, y * rows : (y + 1) * rows, :] + here
            out[x, y * rows : (y + 1) * rows, :] = here


def act_squares(hidden, norm_gain, act_basis):
    tokens = hidden.shape[0]
    columns = act_basis.shape[1]
    block = columns // 32
    place = lax.axis_index(DP).astype(jnp.int32).reshape(1)
    pieces = pl.pallas_call(
        act_kernel,
        out_shape=jax.ShapeDtypeStruct((16, tokens, 2 * block), jnp.bfloat16),
        in_specs=[SMEM, VMEM, VMEM, VMEM],
        out_specs=VMEM,
        compiler_params=pltpu.CompilerParams(vmem_limit_bytes=VMEM_LIMIT),
        name="act",
    )(place, hidden, norm_gain.reshape(1, -1), act_basis)
    got = lax.all_to_all(pieces, ("x", "y"), 0, 0, tiled=True)
    summed = jnp.sum(got.astype(jnp.float32), axis=0).reshape(tokens, 2, block)
    z_hi = lax.axis_index("z_hi")
    kept = lax.dynamic_index_in_dim(summed, z_hi, 1, keepdims=False)
    given = lax.dynamic_index_in_dim(summed, 1 - z_hi, 1, keepdims=False)
    total = kept + shifted(given, "z_hi", 1)
    square = (total * total).astype(jnp.bfloat16)
    row = lax.all_gather(square, "x", axis=0, tiled=False)
    spread = lax.all_gather(row, TENSOR, axis=0, tiled=False)
    return spread.reshape(4, 2, 4, tokens, block)


def grad_squares(rows, basis):
    tokens = sum(part.shape[0] for part in rows)
    columns = basis.shape[1]
    partial = pl.pallas_call(
        grad_kernel,
        out_shape=jax.ShapeDtypeStruct((columns, tokens), jnp.bfloat16),
        in_specs=[VMEM] * (len(rows) + 1),
        out_specs=VMEM,
        compiler_params=pltpu.CompilerParams(vmem_limit_bytes=VMEM_LIMIT),
        name="grad",
    )(*rows, basis)
    got = lax.all_to_all(partial.reshape(16, columns // 16, tokens), ("x", "y"), 0, 0, tiled=True)
    summed = jnp.sum(got.astype(jnp.float32), axis=0)
    total = summed + shifted(summed.astype(jnp.bfloat16), "z_hi", 1).astype(jnp.float32)
    square = (total * total).astype(jnp.bfloat16)
    return lax.all_to_all(
        jnp.broadcast_to(square[None], (4,) + square.shape), "y", 0, 0, tiled=True
    )


def corrected(steps, place, grad_sq, act_sq, tokens, *before):
    _, rows, here = grad_sq.shape
    block = act_sq.shape[4]
    return pl.pallas_call(
        lambda *refs: correct_kernel(steps, tokens, *refs),
        out_shape=jax.ShapeDtypeStruct((4, 4 * rows, block), jnp.float32),
        in_specs=[SMEM] + [VMEM] * (2 + len(before)),
        out_specs=VMEM,
        scratch_shapes=[pltpu.VMEM((here, 4 * block), jnp.bfloat16)],
        compiler_params=pltpu.CompilerParams(vmem_limit_bytes=VMEM_LIMIT),
        name="correct",
    )(place, grad_sq, act_sq, *before)


def per_device(hidden, norm_gain, gate_pre, out_grad, grad_basis, act_basis):
    up_grad = (out_grad.astype(jnp.float32) * jax.nn.silu(gate_pre.astype(jnp.float32))).astype(
        jnp.bfloat16
    )
    moved = [up_grad] + [shifted(up_grad, "z_lo", step) for step in (1, 2, 3)]
    act_sq = act_squares(hidden, norm_gain, act_basis)
    both = [(own, shifted(own, "core", 1)) for own in moved]
    place = jnp.stack([lax.axis_index("z_lo"), lax.axis_index("core")]).astype(jnp.int32)
    tokens = 8 * hidden.shape[0]
    out = []
    for steps in ((0, 1), (2, 3)):
        rows = [part for step in steps for part in both[step]]
        grad_sq = grad_squares(rows, grad_basis)
        out = [corrected(steps, place, grad_sq, act_sq, tokens, *out)]
    out = lax.all_to_all(out[0], "x", 0, 0, tiled=True)
    return out.reshape(grad_basis.shape[1], -1)


def solution(mesh):
    fine = Mesh(mesh.devices.reshape(SIZES), AXES)
    placed = (
        P(TENSOR, None),
        P(),
        P(TENSOR, DP),
        P(TENSOR, DP),
        P(DP, TENSOR),
        P(DP, None),
    )
    return jax.shard_map(
        per_device, mesh=fine, in_specs=placed, out_specs=P(TENSOR, DP), check_vma=False
    )
```

```python
import jax
import jax.numpy as jnp
from jax import lax
from jax.experimental import pallas as pl
from jax.experimental.pallas import tpu as pltpu
from jax.sharding import Mesh
from jax.sharding import PartitionSpec as P

AXES = ("z_hi", "x", "y", "z_lo", "core")
SIZES = (2, 4, 4, 4, 2)
DP = ("z_hi", "x", "y")
TENSOR = ("z_lo", "core")
SMEM = pl.BlockSpec(memory_space=pltpu.SMEM)
VMEM = pl.BlockSpec(memory_space=pltpu.VMEM)
HBM = pl.BlockSpec(memory_space=pl.ANY)
PARAMS = pltpu.CompilerParams(vmem_limit_bytes=48 * 1024 * 1024)


def shifted(value, axis, step):
    size = SIZES[AXES.index(axis)]
    return lax.ppermute(value, axis, [(i, (i + step) % size) for i in range(size)])


def first_kernel(place, gain, own, other, hidden_at, act_at, grad_at, out_at,
                 hidden, act_basis, grad_basis, rows, out, sems):
    loads = [
        pltpu.make_async_copy(src, dst, sems.at[i])
        for i, (src, dst) in enumerate(
            ((hidden_at, hidden), (act_at, act_basis), (grad_at, grad_basis))
        )
    ]
    for load in loads:
        load.start()
    tokens, features = hidden.shape
    depth = act_basis.shape[0]
    rows[:tokens, :] = own[...]
    rows[tokens:, :] = other[...]
    loads[0].wait()
    squares = jnp.zeros((tokens, 128), jnp.float32)
    for at in range(0, features, 128):
        wide = hidden[:, at : at + 128].astype(jnp.float32)
        squares += wide * wide
    stat = jnp.sum(squares, axis=-1, keepdims=True) / features
    mine = pl.ds(pl.multiple_of(place[0] * depth, depth), depth)
    scaled = hidden[:, mine].astype(jnp.float32) * lax.rsqrt(stat + 1e-05)
    normed = (scaled * gain[:, mine]).astype(jnp.bfloat16)
    loads[1].wait()
    block = act_basis.shape[1] // 32
    for z_hi in range(2):
        for x in range(4):
            at = (z_hi * 16 + x * 4) * block
            part = jnp.dot(
                normed, act_basis[:, at : at + 4 * block], preferred_element_type=jnp.float32
            )
            for y in range(4):
                out[x * 4 + y, :tokens, z_hi * block : (z_hi + 1) * block] = part[
                    :, y * block : (y + 1) * block
                ].astype(jnp.bfloat16)
    act_rows = pl.ds(0, tokens)
    act_store = pltpu.make_async_copy(out.at[:, act_rows], out_at.at[:, act_rows], sems.at[3])
    act_store.start()
    loads[2].wait()
    columns = grad_basis.shape[1]
    share = columns // 16
    for at in range(0, columns, 256):
        part = jnp.dot(rows[...], grad_basis[:, at : at + 256], preferred_element_type=jnp.float32)
        part = part.T.astype(jnp.bfloat16)
        for owner in range(at // share, (at + 255) // share + 1):
            low, high = max(at, owner * share), min(at + 256, (owner + 1) * share)
            to = tokens + low - owner * share
            out[owner, to : to + high - low, :] = part[low - at : high - at, :]
    grad_rows = pl.ds(tokens, share)
    grad_store = pltpu.make_async_copy(out.at[:, grad_rows], out_at.at[:, grad_rows], sems.at[4])
    grad_store.start()
    act_store.wait()
    grad_store.wait()


def first_partials(hidden, norm_gain, act_basis, grad_basis, own, other):
    tokens, features = hidden.shape
    shape = (16, tokens + grad_basis.shape[1] // 16, 2 * tokens)
    place = lax.axis_index(DP).astype(jnp.int32).reshape(1)
    return pl.pallas_call(
        first_kernel,
        out_shape=jax.ShapeDtypeStruct(shape, jnp.bfloat16),
        in_specs=[SMEM, VMEM, VMEM, VMEM, HBM, HBM, HBM],
        out_specs=HBM,
        scratch_shapes=[
            pltpu.VMEM(hidden.shape, jnp.bfloat16),
            pltpu.VMEM(act_basis.shape, jnp.bfloat16),
            pltpu.VMEM(grad_basis.shape, jnp.bfloat16),
            pltpu.VMEM((2 * tokens, own.shape[1]), jnp.bfloat16),
            pltpu.VMEM(shape, jnp.bfloat16),
            pltpu.SemaphoreType.DMA((5,)),
        ],
        compiler_params=PARAMS,
        name="first",
    )(place, norm_gain.reshape(1, -1), own, other, hidden, act_basis, grad_basis)


def grad_kernel(count, *refs):
    parts, basis, out, rows = refs[:count], refs[count], refs[-2], refs[-1]

    @pl.when(pl.program_id(0) == 0)
    def _():
        at = 0
        for part in parts:
            rows[at : at + part.shape[0], :] = part[...]
            at += part.shape[0]

    part = jnp.dot(rows[...], basis[...], preferred_element_type=jnp.float32)
    out[...] = part.T.astype(jnp.bfloat16)


def grad_partials(parts, basis, *after):
    depth, columns = basis.shape
    tokens = sum(part.shape[0] for part in parts)
    whole = pl.BlockSpec(parts[0].shape, lambda i: (0, 0))
    return pl.pallas_call(
        lambda *refs: grad_kernel(len(parts), *refs),
        grid=(columns // 256,),
        out_shape=jax.ShapeDtypeStruct((columns, tokens), jnp.bfloat16),
        in_specs=[whole] * len(parts)
        + [pl.BlockSpec((depth, 256), lambda i: (0, i))]
        + [HBM] * len(after),
        out_specs=pl.BlockSpec((256, tokens), lambda i: (i, 0)),
        scratch_shapes=[pltpu.VMEM((tokens, depth), jnp.bfloat16)],
        compiler_params=PARAMS,
        name="grad",
    )(*parts, basis, *after)


def spread_sum_kernel(place, got, kept, grad, given):
    tokens = kept.shape[0]
    half = tokens // 2
    act = jnp.zeros((tokens, 2 * kept.shape[1]), jnp.float32)
    for source in range(got.shape[0]):
        act += got[source, :tokens, :].astype(jnp.float32)
    low, high = act[:, : kept.shape[1]], act[:, kept.shape[1] :]
    first = place[0] == 0
    kept[...] = jnp.where(first, low, high)
    away = jnp.where(first, high, low).astype(jnp.bfloat16)
    given[:half, : kept.shape[1]] = away[:half]
    given[:half, kept.shape[1] :] = away[half:]
    total = jnp.zeros(grad.shape, jnp.float32)
    for source in range(got.shape[0]):
        total += got[source, tokens:, :].astype(jnp.float32)
    grad[...] = total
    given[half:, :] = total.astype(jnp.bfloat16)


def square_kernel(kept, grad, got, act_sq, grad_sq):
    tokens, block = kept.shape
    half = tokens // 2
    for part in range(2):
        rows = slice(part * half, (part + 1) * half)
        total = kept[rows, :] + got[:half, part * block : (part + 1) * block].astype(jnp.float32)
        act_sq[rows, :] = (total * total).astype(jnp.bfloat16)
    total = grad[...] + got[half:, :].astype(jnp.float32)
    grad_sq[...] = (total * total).astype(jnp.bfloat16)


def first_squares(got, tokens):
    share = got.shape[1] - tokens
    wide = got.shape[2]
    block = wide // 2
    place = lax.axis_index("z_hi").astype(jnp.int32).reshape(1)
    kept, grad, given = pl.pallas_call(
        spread_sum_kernel,
        out_shape=(
            jax.ShapeDtypeStruct((tokens, block), jnp.float32),
            jax.ShapeDtypeStruct((share, wide), jnp.float32),
            jax.ShapeDtypeStruct((tokens // 2 + share, wide), jnp.bfloat16),
        ),
        in_specs=[SMEM, VMEM],
        out_specs=(VMEM, VMEM, VMEM),
        compiler_params=PARAMS,
        name="spread_sum",
    )(place, got)
    return pl.pallas_call(
        square_kernel,
        out_shape=(
            jax.ShapeDtypeStruct((tokens, block), jnp.bfloat16),
            jax.ShapeDtypeStruct((share, wide), jnp.bfloat16),
        ),
        in_specs=[VMEM] * 3,
        out_specs=(VMEM, VMEM),
        compiler_params=PARAMS,
        name="square",
    )(kept, grad, shifted(given, "z_hi", 1))


def exchanged(partial):
    columns, tokens = partial.shape
    return lax.all_to_all(partial.reshape(16, columns // 16, tokens), ("x", "y"), 0, 0, tiled=True)


def squared(got):
    summed = jnp.sum(got.astype(jnp.float32), axis=0)
    total = summed + shifted(summed.astype(jnp.bfloat16), "z_hi", 1).astype(jnp.float32)
    return (total * total).astype(jnp.bfloat16)


def correct_kernel(steps, *refs):
    place, *pieces, act_sq, out, act = refs
    pieces, before = pieces[:4], pieces[4:]
    tokens, block = act_sq.shape[2:]
    for i, step in enumerate(steps):
        chip = lax.rem(place[0] + 4 - step, 4)
        for x in range(4):
            act[i * tokens : (i + 1) * tokens, x * block : (x + 1) * block] = act_sq[x, chip]
    rows = pieces[0].shape[0]
    for piece, behind in zip(pieces, (0, 1, 2, 3)):
        part = jnp.dot(piece[...], act[...], preferred_element_type=jnp.float32)
        part = part * (1.0 / (4 * tokens))
        at = pl.ds(pl.multiple_of(lax.rem(place[1] + 4 - behind, 4) * rows, rows), rows)
        for x in range(4):
            here = part[:, x * block : (x + 1) * block]
            if before:
                here = before[0][x, at, :] + here
            out[x, at, :] = here


def corrected(steps, grad_sq, act_sq, *before):
    rows, tokens = grad_sq.shape
    block = act_sq.shape[3]
    place = jnp.stack([lax.axis_index("z_lo"), lax.axis_index("y")]).astype(jnp.int32)
    pieces = [grad_sq] + [shifted(grad_sq, "y", step) for step in (1, 2, 3)]
    return pl.pallas_call(
        lambda *refs: correct_kernel(steps, *refs),
        out_shape=jax.ShapeDtypeStruct((4, 4 * rows, block), jnp.float32),
        in_specs=[SMEM] + [VMEM] * (5 + len(before)),
        out_specs=VMEM,
        scratch_shapes=[pltpu.VMEM((tokens, 4 * block), jnp.bfloat16)],
        compiler_params=PARAMS,
        name="correct",
    )(place, *pieces, *before, act_sq)


def per_device(hidden, norm_gain, gate_pre, out_grad, grad_basis, act_basis):
    tokens = hidden.shape[0]
    up_grad = (out_grad.astype(jnp.float32) * jax.nn.silu(gate_pre.astype(jnp.float32))).astype(
        jnp.bfloat16
    )
    moved = [up_grad] + [shifted(up_grad, "z_lo", step) for step in (1, 2, 3)]
    both = [(own, shifted(own, "core", 1)) for own in moved]
    first = first_partials(hidden, norm_gain, act_basis, grad_basis, *both[0])
    got_first = lax.all_to_all(first, ("x", "y"), 0, 0, tiled=True)
    got_middle = exchanged(grad_partials(both[1] + both[2], grad_basis))
    act_own, grad_first = first_squares(got_first, tokens)
    act_chip = jnp.concatenate([act_own, shifted(act_own, "core", 1)], axis=0)
    act_sq = lax.all_gather(act_chip, ("x", "z_lo"), axis=0, tiled=False)
    act_sq = act_sq.reshape(4, 4, 2 * tokens, -1)
    got_last = exchanged(grad_partials(both[3], grad_basis, act_chip))
    grad_most = jnp.concatenate([grad_first, squared(got_middle)], axis=1)
    most = corrected((0, 1, 2), grad_most, act_sq)
    out = corrected((3,), squared(got_last), act_sq, most)
    out = lax.all_to_all(out, "x", 0, 0, tiled=True)
    return out.reshape(grad_basis.shape[1], -1)


def solution(mesh):
    fine = Mesh(mesh.devices.reshape(SIZES), AXES)
    placed = (
        P(TENSOR, None),
        P(),
        P(TENSOR, DP),
        P(TENSOR, DP),
        P(DP, TENSOR),
        P(DP, None),
    )
    return jax.shard_map(
        per_device, mesh=fine, in_specs=placed, out_specs=P(TENSOR, DP), check_vma=False
    )
```

```python
import jax
import jax.numpy as jnp
from jax import lax
from jax.experimental import pallas as pl
from jax.experimental.pallas import tpu as pltpu
from jax.sharding import Mesh
from jax.sharding import PartitionSpec as P

AXES = ("z_hi", "x", "y", "z_lo", "core")
SIZES = (2, 4, 4, 4, 2)
DP = ("z_hi", "x", "y")
TENSOR = ("z_lo", "core")
SMEM = pl.BlockSpec(memory_space=pltpu.SMEM)
VMEM = pl.BlockSpec(memory_space=pltpu.VMEM)
ANY = pl.BlockSpec(memory_space=pl.ANY)
PARAMS = pltpu.CompilerParams(vmem_limit_bytes=32 * 1024 * 1024)
WHOLE = pltpu.CompilerParams(vmem_limit_bytes=60 * 1024 * 1024)


def shifted(value, axis, step):
    size = SIZES[AXES.index(axis)]
    return lax.ppermute(value, axis, [(i, (i + step) % size) for i in range(size)])


def act_kernel(place, gain, hidden_at, basis_at, out_at, hidden, basis, out, sems):
    tokens, features = hidden.shape
    depth = basis.shape[0]
    strip = tokens // 4
    loads = [
        pltpu.make_async_copy(hidden_at.at[here], hidden.at[here], sems.at[i])
        for i, here in enumerate(pl.ds(at, strip) for at in range(0, tokens, strip))
    ]
    load_basis = pltpu.make_async_copy(basis_at, basis, sems.at[4])
    for load in loads:
        load.start()
    load_basis.start()
    stats = []
    for i, load in enumerate(loads):
        load.wait()
        squares = jnp.zeros((strip, 128), jnp.float32)
        for at in range(0, features, 128):
            wide = hidden[i * strip : (i + 1) * strip, at : at + 128].astype(jnp.float32)
            squares += wide * wide
        stats.append(jnp.sum(squares, axis=-1, keepdims=True) / features)
    stat = jnp.concatenate(stats, axis=0)
    mine = pl.ds(pl.multiple_of(place[0] * depth, depth), depth)
    scaled = hidden[:, mine].astype(jnp.float32) * lax.rsqrt(stat + 1e-05)
    normed = (scaled * gain[:, mine]).astype(jnp.bfloat16)
    load_basis.wait()
    block = basis.shape[1] // 32
    stores = []
    for x in range(4):
        for z_hi in range(2):
            at = (z_hi * 16 + x * 4) * block
            part = jnp.dot(
                normed, basis[:, at : at + 4 * block], preferred_element_type=jnp.float32
            )
            for y in range(4):
                here = part[:, y * block : (y + 1) * block]
                to = slice(z_hi * block, (z_hi + 1) * block)
                out[x * 4 + y, :, to] = here.astype(jnp.bfloat16)
        here = pl.ds(x * 4, 4)
        stores.append(pltpu.make_async_copy(out.at[here], out_at.at[here], sems.at[5 + x]))
        stores[-1].start()
    for store in stores:
        store.wait()


def act_partials(hidden, norm_gain, act_basis):
    tokens = hidden.shape[0]
    shape = (16, tokens, act_basis.shape[1] // 16)
    place = lax.axis_index(DP).astype(jnp.int32).reshape(1)
    return pl.pallas_call(
        act_kernel,
        out_shape=pltpu.HBM(shape, jnp.bfloat16),
        in_specs=[SMEM, VMEM, ANY, ANY],
        out_specs=ANY,
        scratch_shapes=[
            pltpu.VMEM(hidden.shape, jnp.bfloat16),
            pltpu.VMEM(act_basis.shape, jnp.bfloat16),
            pltpu.VMEM(shape, jnp.bfloat16),
            pltpu.SemaphoreType.DMA((9,)),
        ],
        compiler_params=WHOLE,
        name="act",
    )(place, norm_gain.reshape(1, -1), hidden, act_basis)


def grad_kernel(count, *refs):
    parts, basis, out_at, rows, out, sem = refs[:count], refs[count], *refs[-4:]
    at = 0
    for part in parts:
        rows[at : at + part.shape[0], :] = part[...]
        at += part.shape[0]
    stores = []
    for at in range(0, basis.shape[1], 256):
        here = pl.ds(at, 256)
        part = jnp.dot(rows[...], basis[:, here], preferred_element_type=jnp.float32)
        out[here, :] = part.T.astype(jnp.bfloat16)
        stores.append(
            pltpu.make_async_copy(out.at[here], out_at.at[here], sem.at[at // 256])
        )
        stores[-1].start()
    for store in stores:
        store.wait()


def grad_partials(parts, basis, *after):
    depth, columns = basis.shape
    tokens = sum(part.shape[0] for part in parts)
    shape = (columns, tokens)
    return pl.pallas_call(
        lambda *refs: grad_kernel(len(parts), *refs),
        out_shape=pltpu.HBM(shape, jnp.bfloat16),
        in_specs=[VMEM] * (len(parts) + 1) + [ANY] * len(after),
        out_specs=ANY,
        scratch_shapes=[
            pltpu.VMEM((tokens, depth), jnp.bfloat16),
            pltpu.VMEM(shape, jnp.bfloat16),
            pltpu.SemaphoreType.DMA((columns // 256,)),
        ],
        compiler_params=PARAMS,
        name="grad",
    )(*parts, basis, *after)


def act_sum_kernel(place, got, kept, given):
    total = got[0].astype(jnp.float32)
    for source in range(1, got.shape[0]):
        total += got[source].astype(jnp.float32)
    low, high = total[:, : kept.shape[1]], total[:, kept.shape[1] :]
    first = place[0] == 0
    kept[...] = jnp.where(first, low, high)
    given[...] = jnp.where(first, high, low)


def act_squares(partials):
    got = lax.all_to_all(partials, ("x", "y"), 0, 0, tiled=True)
    _, tokens, wide = got.shape
    half = jax.ShapeDtypeStruct((tokens, wide // 2), jnp.float32)
    place = lax.axis_index("z_hi").astype(jnp.int32).reshape(1)
    kept, given = pl.pallas_call(
        act_sum_kernel,
        out_shape=(half, half),
        in_specs=[SMEM, VMEM],
        out_specs=(VMEM, VMEM),
        compiler_params=PARAMS,
        name="act_sum",
    )(place, got)
    total = kept + shifted(given, "z_hi", 1)
    square = (total * total).astype(jnp.bfloat16)
    row = [square] + [shifted(square, "x", step) for step in (1, 2, 3)]
    spread = lax.all_gather(jnp.stack(row), TENSOR, axis=0, tiled=False)
    return row, spread.reshape(4, 2, 4, tokens, wide // 2)


def gate_kernel(*refs):
    del refs


def gated(value, *after):
    return pl.pallas_call(
        gate_kernel,
        out_shape=pltpu.HBM(value.shape, value.dtype),
        in_specs=[ANY] * (1 + len(after)),
        out_specs=ANY,
        input_output_aliases={0: 0},
        compiler_params=PARAMS,
        name="gate",
    )(value, *after)


def exchanged(partial):
    columns, tokens = partial.shape
    return lax.all_to_all(partial.reshape(16, columns // 16, tokens), ("x", "y"), 0, 0, tiled=True)


def squared(got):
    summed = jnp.sum(got.astype(jnp.float32), axis=0)
    total = summed + shifted(summed.astype(jnp.bfloat16), "z_hi", 1).astype(jnp.float32)
    return (total * total).astype(jnp.bfloat16)


def correct_kernel(steps, *refs):
    place, *pieces, act_sq, out, act = refs
    pieces, before = pieces[:4], pieces[4:]
    tokens, block = act_sq.shape[3:]
    at = 0
    for step in steps:
        chip = lax.rem(place[0] + 4 - step, 4)
        for flip in range(2):
            core = lax.rem(place[1] + flip, 2)
            for behind in range(4):
                to = slice(behind * block, (behind + 1) * block)
                act[at : at + tokens, to] = act_sq[chip, core, behind]
            at += tokens
    rows = pieces[0].shape[0]
    for y_behind, piece in enumerate(pieces):
        part = jnp.dot(piece[...], act[...], preferred_element_type=jnp.float32)
        part = part * (1.0 / (8 * tokens))
        at = pl.ds(pl.multiple_of(lax.rem(place[3] + 4 - y_behind, 4) * rows, rows), rows)
        for behind in range(4):
            x = lax.rem(place[2] + 4 - behind, 4)
            here = part[:, behind * block : (behind + 1) * block]
            if before:
                here = before[0][x, at, :] + here
            out[x, at, :] = here


def corrected(steps, grad_sq, act_sq, *before):
    rows, tokens = grad_sq.shape
    block = act_sq.shape[4]
    place = jnp.stack([lax.axis_index(a) for a in ("z_lo", "core", "x", "y")]).astype(jnp.int32)
    pieces = [grad_sq] + [shifted(grad_sq, "y", step) for step in (1, 2, 3)]
    return pl.pallas_call(
        lambda *refs: correct_kernel(steps, *refs),
        out_shape=jax.ShapeDtypeStruct((4, 4 * rows, block), jnp.float32),
        in_specs=[SMEM] + [VMEM] * (5 + len(before)),
        out_specs=VMEM,
        scratch_shapes=[pltpu.VMEM((tokens, 4 * block), jnp.bfloat16)],
        compiler_params=PARAMS,
        name="correct",
    )(place, *pieces, *before, act_sq)


CHUNKS = ((0, 1), (2, 3))


def per_device(hidden, norm_gain, gate_pre, out_grad, grad_basis, act_basis):
    up_grad = (out_grad.astype(jnp.float32) * jax.nn.silu(gate_pre.astype(jnp.float32))).astype(
        jnp.bfloat16
    )
    moved = [up_grad] + [shifted(up_grad, "z_lo", step) for step in (1, 2, 3)]
    both = [(own, shifted(own, "core", 1)) for own in moved]
    act_row, act_sq = act_squares(act_partials(hidden, norm_gain, act_basis))
    grad_got = []
    for chunk, steps in enumerate(CHUNKS):
        partial = grad_partials([part for step in steps for part in both[step]], grad_basis)
        if chunk:
            partial = gated(partial, *act_row)
        grad_got.append(exchanged(partial))
    out = []
    for steps, got in zip(CHUNKS, grad_got):
        out = [corrected(steps, squared(got), act_sq, *out)]
    out = lax.all_to_all(out[0], "x", 0, 0, tiled=True)
    return out.reshape(grad_basis.shape[1], -1)


def solution(mesh):
    fine = Mesh(mesh.devices.reshape(SIZES), AXES)
    placed = (
        P(TENSOR, None),
        P(),
        P(TENSOR, DP),
        P(TENSOR, DP),
        P(DP, TENSOR),
        P(DP, None),
    )
    return jax.shard_map(
        per_device, mesh=fine, in_specs=placed, out_specs=P(TENSOR, DP), check_vma=False
    )
```

```python
import jax
import jax.numpy as jnp
from jax import lax
from jax.experimental import pallas as pl
from jax.experimental.pallas import tpu as pltpu
from jax.sharding import Mesh
from jax.sharding import PartitionSpec as P

AXES = ("z_hi", "x", "y", "z_lo", "core")
SIZES = (2, 4, 4, 4, 2)
DP = ("z_hi", "x", "y")
TENSOR = ("z_lo", "core")
SMEM = pl.BlockSpec(memory_space=pltpu.SMEM)
VMEM = pl.BlockSpec(memory_space=pltpu.VMEM)
ANY = pl.BlockSpec(memory_space=pl.ANY)
PARAMS = pltpu.CompilerParams(vmem_limit_bytes=32 * 1024 * 1024)
WHOLE = pltpu.CompilerParams(vmem_limit_bytes=60 * 1024 * 1024)


def shifted(value, axis, step):
    size = SIZES[AXES.index(axis)]
    return lax.ppermute(value, axis, [(i, (i + step) % size) for i in range(size)])


def first_kernel(place, gain, gate_at, grad_at, hidden_at, basis_at, out_at, up_at,
                 gate, grad, hidden, basis, out, up, sems):
    tokens, features = hidden.shape
    depth = basis.shape[0]
    strip = tokens // 4
    load_gate = pltpu.make_async_copy(gate_at, gate, sems.at[9])
    load_grad = pltpu.make_async_copy(grad_at, grad, sems.at[10])
    loads = [
        pltpu.make_async_copy(hidden_at.at[here], hidden.at[here], sems.at[i])
        for i, here in enumerate(pl.ds(at, strip) for at in range(0, tokens, strip))
    ]
    load_basis = pltpu.make_async_copy(basis_at, basis, sems.at[4])
    for load in (load_gate, load_grad, *loads, load_basis):
        load.start()
    load_gate.wait()
    load_grad.wait()
    for at in range(0, tokens, 32):
        here = slice(at, at + 32)
        wide = gate[here, :].astype(jnp.float32)
        wide = grad[here, :].astype(jnp.float32) * (wide / (1.0 + jnp.exp(-wide)))
        up[here, :] = wide.astype(jnp.bfloat16)
    store_up = pltpu.make_async_copy(up, up_at, sems.at[11])
    store_up.start()
    stats = []
    for i, load in enumerate(loads):
        load.wait()
        squares = jnp.zeros((strip, 128), jnp.float32)
        for at in range(0, features, 128):
            wide = hidden[i * strip : (i + 1) * strip, at : at + 128].astype(jnp.float32)
            squares += wide * wide
        stats.append(jnp.sum(squares, axis=-1, keepdims=True) / features)
    stat = jnp.concatenate(stats, axis=0)
    mine = pl.ds(pl.multiple_of(place[0] * depth, depth), depth)
    scaled = hidden[:, mine].astype(jnp.float32) * lax.rsqrt(stat + 1e-05)
    normed = (scaled * gain[:, mine]).astype(jnp.bfloat16)
    load_basis.wait()
    block = basis.shape[1] // 32
    stores = [store_up]
    for x in range(4):
        for z_hi in range(2):
            at = (z_hi * 16 + x * 4) * block
            part = jnp.dot(
                normed, basis[:, at : at + 4 * block], preferred_element_type=jnp.float32
            )
            for y in range(4):
                here = part[:, y * block : (y + 1) * block]
                to = slice(z_hi * block, (z_hi + 1) * block)
                out[x * 4 + y, :, to] = here.astype(jnp.bfloat16)
        here = pl.ds(x * 4, 4)
        stores.append(pltpu.make_async_copy(out.at[here], out_at.at[here], sems.at[5 + x]))
        stores[-1].start()
    for store in stores:
        store.wait()


def first_partials(hidden, norm_gain, gate_pre, out_grad, act_basis):
    tokens = hidden.shape[0]
    shape = (16, tokens, act_basis.shape[1] // 16)
    place = lax.axis_index(DP).astype(jnp.int32).reshape(1)
    return pl.pallas_call(
        first_kernel,
        out_shape=(pltpu.HBM(shape, jnp.bfloat16), pltpu.HBM(out_grad.shape, jnp.bfloat16)),
        in_specs=[SMEM, VMEM, ANY, ANY, ANY, ANY],
        out_specs=(ANY, ANY),
        scratch_shapes=[
            pltpu.VMEM(gate_pre.shape, jnp.bfloat16),
            pltpu.VMEM(out_grad.shape, jnp.bfloat16),
            pltpu.VMEM(hidden.shape, jnp.bfloat16),
            pltpu.VMEM(act_basis.shape, jnp.bfloat16),
            pltpu.VMEM(shape, jnp.bfloat16),
            pltpu.VMEM(out_grad.shape, jnp.bfloat16),
            pltpu.SemaphoreType.DMA((12,)),
        ],
        compiler_params=WHOLE,
        name="first",
    )(place, norm_gain.reshape(1, -1), gate_pre, out_grad, hidden, act_basis)


def grad_kernel(picks, *refs):
    place, *parts, basis, out_at, rows, out, sem = refs
    tokens = parts[0].shape[-2]
    if picks:
        chips = [lax.rem(place[0] + 4 - step, 4) for step in picks]
        cores = [lax.rem(place[1] + flip, 2) for flip in range(2)]
        parts = [parts[0].at[chip, core] for chip in chips for core in cores]
    for at, part in enumerate(parts):
        rows[at * tokens : (at + 1) * tokens, :] = part[...]
    stores = []
    for at in range(0, basis.shape[1], 256):
        here = pl.ds(at, 256)
        part = jnp.dot(rows[...], basis[:, here], preferred_element_type=jnp.float32)
        out[here, :] = part.T.astype(jnp.bfloat16)
        stores.append(
            pltpu.make_async_copy(out.at[here], out_at.at[here], sem.at[at // 256])
        )
        stores[-1].start()
    for store in stores:
        store.wait()


def grad_partials(place, parts, basis, picks=()):
    depth, columns = basis.shape
    tokens = parts[0].shape[-2] * (2 * len(picks) if picks else len(parts))
    shape = (columns, tokens)
    return pl.pallas_call(
        lambda *refs: grad_kernel(picks, *refs),
        out_shape=pltpu.HBM(shape, jnp.bfloat16),
        in_specs=[SMEM] + [VMEM] * (len(parts) + 1),
        out_specs=ANY,
        scratch_shapes=[
            pltpu.VMEM((tokens, depth), jnp.bfloat16),
            pltpu.VMEM(shape, jnp.bfloat16),
            pltpu.SemaphoreType.DMA((columns // 256,)),
        ],
        compiler_params=PARAMS,
        name="grad",
    )(place, *parts, basis)


def act_sum_kernel(place, got, kept, given):
    total = got[0].astype(jnp.float32)
    for source in range(1, got.shape[0]):
        total += got[source].astype(jnp.float32)
    low, high = total[:, : kept.shape[1]], total[:, kept.shape[1] :]
    first = place[0] == 0
    kept[...] = jnp.where(first, low, high)
    given[...] = jnp.where(first, high, low)


def act_squares(partials):
    got = lax.all_to_all(partials, ("x", "y"), 0, 0, tiled=True)
    _, tokens, wide = got.shape
    half = jax.ShapeDtypeStruct((tokens, wide // 2), jnp.float32)
    place = lax.axis_index("z_hi").astype(jnp.int32).reshape(1)
    kept, given = pl.pallas_call(
        act_sum_kernel,
        out_shape=(half, half),
        in_specs=[SMEM, VMEM],
        out_specs=(VMEM, VMEM),
        compiler_params=PARAMS,
        name="act_sum",
    )(place, got)
    total = kept + shifted(given, "z_hi", 1)
    square = (total * total).astype(jnp.bfloat16)
    row = [square] + [shifted(square, "x", step) for step in (1, 2, 3)]
    spread = lax.all_gather(jnp.stack(row), TENSOR, axis=0, tiled=False)
    return row, spread.reshape(4, 2, 4, tokens, wide // 2)


def gate_kernel(*refs):
    del refs


def gated(value, *after):
    return pl.pallas_call(
        gate_kernel,
        out_shape=pltpu.HBM(value.shape, value.dtype),
        in_specs=[ANY] * (1 + len(after)),
        out_specs=ANY,
        input_output_aliases={0: 0},
        compiler_params=PARAMS,
        name="gate",
    )(value, *after)


def exchanged(partial):
    columns, tokens = partial.shape
    return lax.all_to_all(partial.reshape(16, columns // 16, tokens), ("x", "y"), 0, 0, tiled=True)


def squared(got):
    summed = jnp.sum(got.astype(jnp.float32), axis=0)
    total = summed + shifted(summed.astype(jnp.bfloat16), "z_hi", 1).astype(jnp.float32)
    return (total * total).astype(jnp.bfloat16)


def correct_kernel(steps, *refs):
    place, *pieces, act_sq, out, act = refs
    pieces, before = pieces[:4], pieces[4:]
    tokens, block = act_sq.shape[3:]
    at = 0
    for step in steps:
        chip = lax.rem(place[0] + 4 - step, 4)
        for flip in range(2):
            core = lax.rem(place[1] + flip, 2)
            for behind in range(4):
                to = slice(behind * block, (behind + 1) * block)
                act[at : at + tokens, to] = act_sq[chip, core, behind]
            at += tokens
    rows = pieces[0].shape[0]
    for y_behind, piece in enumerate(pieces):
        part = jnp.dot(piece[...], act[...], preferred_element_type=jnp.float32)
        part = part * (1.0 / (8 * tokens))
        at = pl.ds(pl.multiple_of(lax.rem(place[3] + 4 - y_behind, 4) * rows, rows), rows)
        for behind in range(4):
            x = lax.rem(place[2] + 4 - behind, 4)
            here = part[:, behind * block : (behind + 1) * block]
            if before:
                here = before[0][x, at, :] + here
            out[x, at, :] = here


def corrected(steps, place, grad_sq, act_sq, *before):
    rows, tokens = grad_sq.shape
    block = act_sq.shape[4]
    pieces = [grad_sq] + [shifted(grad_sq, "y", step) for step in (1, 2, 3)]
    return pl.pallas_call(
        lambda *refs: correct_kernel(steps, *refs),
        out_shape=jax.ShapeDtypeStruct((4, 4 * rows, block), jnp.float32),
        in_specs=[SMEM] + [VMEM] * (5 + len(before)),
        out_specs=VMEM,
        scratch_shapes=[pltpu.VMEM((tokens, 4 * block), jnp.bfloat16)],
        compiler_params=PARAMS,
        name="correct",
    )(place, *pieces, *before, act_sq)


def per_device(hidden, norm_gain, gate_pre, out_grad, grad_basis, act_basis):
    place = jnp.stack([lax.axis_index(a) for a in ("z_lo", "core", "x", "y")]).astype(jnp.int32)
    act_parts, up_grad = first_partials(hidden, norm_gain, gate_pre, out_grad, act_basis)
    near = shifted(up_grad, "z_lo", 1)
    parts = [up_grad, shifted(up_grad, "core", 1), near, shifted(near, "core", 1)]
    every = lax.all_gather(up_grad, TENSOR, axis=0, tiled=False)
    every = every.reshape((4, 2) + up_grad.shape)
    act_row, act_sq = act_squares(act_parts)
    near_got = exchanged(grad_partials(place, parts, grad_basis))
    far_partial = grad_partials(place, [every], grad_basis, (2, 3))
    far_got = exchanged(gated(far_partial, *act_row))
    out = corrected((0, 1), place, squared(near_got), act_sq)
    out = corrected((2, 3), place, squared(far_got), act_sq, out)
    out = lax.all_to_all(out, "x", 0, 0, tiled=True)
    return out.reshape(grad_basis.shape[1], -1)


def solution(mesh):
    fine = Mesh(mesh.devices.reshape(SIZES), AXES)
    placed = (
        P(TENSOR, None),
        P(),
        P(TENSOR, DP),
        P(TENSOR, DP),
        P(DP, TENSOR),
        P(DP, None),
    )
    return jax.shard_map(
        per_device, mesh=fine, in_specs=placed, out_specs=P(TENSOR, DP), check_vma=False
    )
```

```python
import jax
import jax.numpy as jnp
from jax import lax
from jax.experimental import pallas as pl
from jax.experimental.pallas import tpu as pltpu
from jax.sharding import Mesh
from jax.sharding import PartitionSpec as P

AXES = ("z_hi", "x", "y", "z_lo", "core")
SIZES = (2, 4, 4, 4, 2)
DP = ("z_hi", "x", "y")
TENSOR = ("z_lo", "core")
SMEM = pl.BlockSpec(memory_space=pltpu.SMEM)
VMEM = pl.BlockSpec(memory_space=pltpu.VMEM)
ANY = pl.BlockSpec(memory_space=pl.ANY)
PARAMS = pltpu.CompilerParams(vmem_limit_bytes=32 * 1024 * 1024)
WHOLE = pltpu.CompilerParams(vmem_limit_bytes=60 * 1024 * 1024)


def shifted(value, axis, step):
    size = SIZES[AXES.index(axis)]
    return lax.ppermute(value, axis, [(i, (i + step) % size) for i in range(size)])


def first_kernel(place, gain, gate_at, grad_at, hidden_at, basis_at, out_at, up_at,
                 gate, grad, hidden, basis, out, up, sems):
    tokens, features = hidden.shape
    depth = basis.shape[0]
    strip = tokens // 4
    load_gate = pltpu.make_async_copy(gate_at, gate, sems.at[9])
    load_grad = pltpu.make_async_copy(grad_at, grad, sems.at[10])
    loads = [
        pltpu.make_async_copy(hidden_at.at[here], hidden.at[here], sems.at[i])
        for i, here in enumerate(pl.ds(at, strip) for at in range(0, tokens, strip))
    ]
    load_basis = pltpu.make_async_copy(basis_at, basis, sems.at[4])
    for load in (load_gate, load_grad, *loads, load_basis):
        load.start()
    load_gate.wait()
    load_grad.wait()
    for at in range(0, tokens, 32):
        here = slice(at, at + 32)
        wide = gate[here, :].astype(jnp.float32)
        wide = grad[here, :].astype(jnp.float32) * (wide / (1.0 + jnp.exp(-wide)))
        up[here, :] = wide.astype(jnp.bfloat16)
    store_up = pltpu.make_async_copy(up, up_at, sems.at[11])
    store_up.start()
    stats = []
    for i, load in enumerate(loads):
        load.wait()
        squares = jnp.zeros((strip, 128), jnp.float32)
        for at in range(0, features, 128):
            wide = hidden[i * strip : (i + 1) * strip, at : at + 128].astype(jnp.float32)
            squares += wide * wide
        stats.append(jnp.sum(squares, axis=-1, keepdims=True) / features)
    stat = jnp.concatenate(stats, axis=0)
    mine = pl.ds(pl.multiple_of(place[0] * depth, depth), depth)
    scaled = hidden[:, mine].astype(jnp.float32) * lax.rsqrt(stat + 1e-05)
    normed = (scaled * gain[:, mine]).astype(jnp.bfloat16)
    load_basis.wait()
    block = basis.shape[1] // 32
    stores = [store_up]
    for x in range(4):
        for z_hi in range(2):
            at = (z_hi * 16 + x * 4) * block
            part = jnp.dot(
                normed, basis[:, at : at + 4 * block], preferred_element_type=jnp.float32
            )
            for y in range(4):
                here = part[:, y * block : (y + 1) * block]
                to = slice(z_hi * block, (z_hi + 1) * block)
                out[x * 4 + y, :, to] = here.astype(jnp.bfloat16)
        here = pl.ds(x * 4, 4)
        stores.append(pltpu.make_async_copy(out.at[here], out_at.at[here], sems.at[5 + x]))
        stores[-1].start()
    for store in stores:
        store.wait()


def first_partials(hidden, norm_gain, gate_pre, out_grad, act_basis):
    tokens = hidden.shape[0]
    shape = (16, tokens, act_basis.shape[1] // 16)
    place = lax.axis_index(DP).astype(jnp.int32).reshape(1)
    return pl.pallas_call(
        first_kernel,
        out_shape=(pltpu.HBM(shape, jnp.bfloat16), pltpu.HBM(out_grad.shape, jnp.bfloat16)),
        in_specs=[SMEM, VMEM, ANY, ANY, ANY, ANY],
        out_specs=(ANY, ANY),
        scratch_shapes=[
            pltpu.VMEM(gate_pre.shape, jnp.bfloat16),
            pltpu.VMEM(out_grad.shape, jnp.bfloat16),
            pltpu.VMEM(hidden.shape, jnp.bfloat16),
            pltpu.VMEM(act_basis.shape, jnp.bfloat16),
            pltpu.VMEM(shape, jnp.bfloat16),
            pltpu.VMEM(out_grad.shape, jnp.bfloat16),
            pltpu.SemaphoreType.DMA((12,)),
        ],
        compiler_params=WHOLE,
        name="first",
    )(place, norm_gain.reshape(1, -1), gate_pre, out_grad, hidden, act_basis)


def grad_kernel(count, *refs):
    parts, basis, out_at, rows, out, sem = refs[:count], refs[count], *refs[-4:]
    at = 0
    for part in parts:
        rows[at : at + part.shape[0], :] = part[...]
        at += part.shape[0]
    stores = []
    for at in range(0, basis.shape[1], 256):
        here = pl.ds(at, 256)
        part = jnp.dot(rows[...], basis[:, here], preferred_element_type=jnp.float32)
        out[here, :] = part.T.astype(jnp.bfloat16)
        stores.append(
            pltpu.make_async_copy(out.at[here], out_at.at[here], sem.at[at // 256])
        )
        stores[-1].start()
    for store in stores:
        store.wait()


def grad_partials(parts, basis, *after):
    depth, columns = basis.shape
    tokens = sum(part.shape[0] for part in parts)
    shape = (columns, tokens)
    return pl.pallas_call(
        lambda *refs: grad_kernel(len(parts), *refs),
        out_shape=pltpu.HBM(shape, jnp.bfloat16),
        in_specs=[VMEM] * (len(parts) + 1) + [ANY] * len(after),
        out_specs=ANY,
        scratch_shapes=[
            pltpu.VMEM((tokens, depth), jnp.bfloat16),
            pltpu.VMEM(shape, jnp.bfloat16),
            pltpu.SemaphoreType.DMA((columns // 256,)),
        ],
        compiler_params=PARAMS,
        name="grad",
    )(*parts, basis, *after)


def act_sum_kernel(place, got, kept, given):
    total = got[0].astype(jnp.float32)
    for source in range(1, got.shape[0]):
        total += got[source].astype(jnp.float32)
    low, high = total[:, : kept.shape[1]], total[:, kept.shape[1] :]
    first = place[0] == 0
    kept[...] = jnp.where(first, low, high)
    given[...] = jnp.where(first, high, low)


def act_squares(partials):
    got = lax.all_to_all(partials, ("x", "y"), 0, 0, tiled=True)
    _, tokens, wide = got.shape
    half = jax.ShapeDtypeStruct((tokens, wide // 2), jnp.float32)
    place = lax.axis_index("z_hi").astype(jnp.int32).reshape(1)
    kept, given = pl.pallas_call(
        act_sum_kernel,
        out_shape=(half, half),
        in_specs=[SMEM, VMEM],
        out_specs=(VMEM, VMEM),
        compiler_params=PARAMS,
        name="act_sum",
    )(place, got)
    total = kept + shifted(given, "z_hi", 1)
    square = (total * total).astype(jnp.bfloat16)
    return [square] + [shifted(square, "x", step) for step in (1, 2, 3)]


def gate_kernel(*refs):
    del refs


def gated(value, *after):
    return pl.pallas_call(
        gate_kernel,
        out_shape=pltpu.HBM(value.shape, value.dtype),
        in_specs=[ANY] * (1 + len(after)),
        out_specs=ANY,
        input_output_aliases={0: 0},
        compiler_params=PARAMS,
        name="gate",
    )(value, *after)


def exchanged(partial):
    columns, tokens = partial.shape
    return lax.all_to_all(partial.reshape(16, columns // 16, tokens), ("x", "y"), 0, 0, tiled=True)


def squared(got):
    summed = jnp.sum(got.astype(jnp.float32), axis=0)
    total = summed + shifted(summed.astype(jnp.bfloat16), "z_hi", 1).astype(jnp.float32)
    return (total * total).astype(jnp.bfloat16)


def correct_kernel(place, *refs):
    pieces, acts, before, (out, act) = refs[:4], refs[4:8], refs[8:-2], refs[-2:]
    _, tokens, block = acts[0].shape
    for i, part in enumerate(acts):
        for behind in range(4):
            here = slice(i * tokens, (i + 1) * tokens), slice(behind * block, (behind + 1) * block)
            act[here] = part[behind]
    rows = pieces[0].shape[0]
    for y_behind, piece in enumerate(pieces):
        part = jnp.dot(piece[...], act[...], preferred_element_type=jnp.float32)
        part = part * (1.0 / (8 * tokens))
        at = pl.ds(pl.multiple_of(lax.rem(place[1] + 4 - y_behind, 4) * rows, rows), rows)
        for behind in range(4):
            x = lax.rem(place[0] + 4 - behind, 4)
            here = part[:, behind * block : (behind + 1) * block]
            if before:
                here = before[0][x, at, :] + here
            out[x, at, :] = here


def corrected(pieces, acts, *before):
    rows, tokens = pieces[0].shape
    block = acts[0].shape[2]
    place = jnp.stack([lax.axis_index("x"), lax.axis_index("y")]).astype(jnp.int32)
    return pl.pallas_call(
        correct_kernel,
        out_shape=jax.ShapeDtypeStruct((4, 4 * rows, block), jnp.float32),
        in_specs=[SMEM] + [VMEM] * (8 + len(before)),
        out_specs=VMEM,
        scratch_shapes=[pltpu.VMEM((tokens, 4 * block), jnp.bfloat16)],
        compiler_params=PARAMS,
        name="correct",
    )(place, *pieces, *acts, *before)


def per_device(hidden, norm_gain, gate_pre, out_grad, grad_basis, act_basis):
    act_parts, up_grad = first_partials(hidden, norm_gain, gate_pre, out_grad, act_basis)
    rows = []
    for own in [up_grad] + [shifted(up_grad, "z_lo", step) for step in (1, 2, 3)]:
        rows += [own, shifted(own, "core", 1)]
    act_row = act_squares(act_parts)
    near_got = exchanged(grad_partials(rows[:4], grad_basis))
    far_got = exchanged(gated(grad_partials(rows[4:], grad_basis), *act_row))
    act_own = jnp.stack(act_row)
    acts = []
    for own in [act_own] + [shifted(act_own, "z_lo", step) for step in (1, 2, 3)]:
        acts += [own, shifted(own, "core", 1)]
    near_sq = squared(near_got)
    near_pieces = [near_sq] + [shifted(near_sq, "y", step) for step in (1, 2, 3)]
    far_sq = squared(gated(far_got, *near_pieces, *acts))
    far_pieces = [far_sq] + [shifted(far_sq, "y", step) for step in (1, 2, 3)]
    out = corrected(far_pieces, acts[4:], corrected(near_pieces, acts[:4]))
    out = lax.all_to_all(out, "x", 0, 0, tiled=True)
    return out.reshape(grad_basis.shape[1], -1)


def solution(mesh):
    fine = Mesh(mesh.devices.reshape(SIZES), AXES)
    placed = (
        P(TENSOR, None),
        P(),
        P(TENSOR, DP),
        P(TENSOR, DP),
        P(DP, TENSOR),
        P(DP, None),
    )
    return jax.shard_map(
        per_device, mesh=fine, in_specs=placed, out_specs=P(TENSOR, DP), check_vma=False
    )
```

```python
import jax
import jax.numpy as jnp
from jax import lax
from jax.experimental import pallas as pl
from jax.experimental.pallas import tpu as pltpu
from jax.sharding import Mesh
from jax.sharding import PartitionSpec as P

AXES = ("z_hi", "x", "y", "z_lo", "core")
SIZES = (2, 4, 4, 4, 2)
DP = ("z_hi", "x", "y")
TENSOR = ("z_lo", "core")
SMEM = pl.BlockSpec(memory_space=pltpu.SMEM)
VMEM = pl.BlockSpec(memory_space=pltpu.VMEM)
ANY = pl.BlockSpec(memory_space=pl.ANY)
PARAMS = pltpu.CompilerParams(vmem_limit_bytes=32 * 1024 * 1024)
WHOLE = pltpu.CompilerParams(vmem_limit_bytes=60 * 1024 * 1024)


def shifted(value, axis, step):
    size = SIZES[AXES.index(axis)]
    return lax.ppermute(value, axis, [(i, (i + step) % size) for i in range(size)])


def first_kernel(place, gain, gate_at, grad_at, hidden_at, basis_at, out_at, up_at,
                 gate, grad, hidden, basis, out, up, sems):
    tokens, features = hidden.shape
    depth = basis.shape[0]
    strip = tokens // 4
    load_gate = pltpu.make_async_copy(gate_at, gate, sems.at[9])
    load_grad = pltpu.make_async_copy(grad_at, grad, sems.at[10])
    loads = [
        pltpu.make_async_copy(hidden_at.at[here], hidden.at[here], sems.at[i])
        for i, here in enumerate(pl.ds(at, strip) for at in range(0, tokens, strip))
    ]
    load_basis = pltpu.make_async_copy(basis_at, basis, sems.at[4])
    for load in (load_gate, load_grad, *loads, load_basis):
        load.start()
    load_gate.wait()
    load_grad.wait()
    for at in range(0, tokens, 32):
        here = slice(at, at + 32)
        wide = gate[here, :].astype(jnp.float32)
        wide = grad[here, :].astype(jnp.float32) * (wide / (1.0 + jnp.exp(-wide)))
        up[here, :] = wide.astype(jnp.bfloat16)
    store_up = pltpu.make_async_copy(up, up_at, sems.at[11])
    store_up.start()
    stats = []
    for i, load in enumerate(loads):
        load.wait()
        squares = jnp.zeros((strip, 128), jnp.float32)
        for at in range(0, features, 128):
            wide = hidden[i * strip : (i + 1) * strip, at : at + 128].astype(jnp.float32)
            squares += wide * wide
        stats.append(jnp.sum(squares, axis=-1, keepdims=True) / features)
    stat = jnp.concatenate(stats, axis=0)
    mine = pl.ds(pl.multiple_of(place[0] * depth, depth), depth)
    scaled = hidden[:, mine].astype(jnp.float32) * lax.rsqrt(stat + 1e-05)
    normed = (scaled * gain[:, mine]).astype(jnp.bfloat16)
    load_basis.wait()
    block = basis.shape[1] // 32
    stores = [store_up]
    for x in range(4):
        for z_hi in range(2):
            at = (z_hi * 16 + x * 4) * block
            part = jnp.dot(
                normed, basis[:, at : at + 4 * block], preferred_element_type=jnp.float32
            )
            for y in range(4):
                here = part[:, y * block : (y + 1) * block]
                to = slice(z_hi * block, (z_hi + 1) * block)
                out[x * 4 + y, :, to] = here.astype(jnp.bfloat16)
        here = pl.ds(x * 4, 4)
        stores.append(pltpu.make_async_copy(out.at[here], out_at.at[here], sems.at[5 + x]))
        stores[-1].start()
    for store in stores:
        store.wait()


def first_partials(hidden, norm_gain, gate_pre, out_grad, act_basis):
    tokens = hidden.shape[0]
    shape = (16, tokens, act_basis.shape[1] // 16)
    place = lax.axis_index(DP).astype(jnp.int32).reshape(1)
    return pl.pallas_call(
        first_kernel,
        out_shape=(pltpu.HBM(shape, jnp.bfloat16), pltpu.HBM(out_grad.shape, jnp.bfloat16)),
        in_specs=[SMEM, VMEM, ANY, ANY, ANY, ANY],
        out_specs=(ANY, ANY),
        scratch_shapes=[
            pltpu.VMEM(gate_pre.shape, jnp.bfloat16),
            pltpu.VMEM(out_grad.shape, jnp.bfloat16),
            pltpu.VMEM(hidden.shape, jnp.bfloat16),
            pltpu.VMEM(act_basis.shape, jnp.bfloat16),
            pltpu.VMEM(shape, jnp.bfloat16),
            pltpu.VMEM(out_grad.shape, jnp.bfloat16),
            pltpu.SemaphoreType.DMA((12,)),
        ],
        compiler_params=WHOLE,
        name="first",
    )(place, norm_gain.reshape(1, -1), gate_pre, out_grad, hidden, act_basis)


def grad_kernel(count, *refs):
    parts, basis, out_at, rows, out, sem = refs[:count], refs[count], *refs[-4:]
    at = 0
    for part in parts:
        rows[at : at + part.shape[0], :] = part[...]
        at += part.shape[0]
    stores = []
    for at in range(0, basis.shape[1], 256):
        here = pl.ds(at, 256)
        part = jnp.dot(rows[...], basis[:, here], preferred_element_type=jnp.float32)
        out[here, :] = part.T.astype(jnp.bfloat16)
        stores.append(
            pltpu.make_async_copy(out.at[here], out_at.at[here], sem.at[at // 256])
        )
        stores[-1].start()
    for store in stores:
        store.wait()


def grad_partials(parts, basis, *after):
    depth, columns = basis.shape
    tokens = sum(part.shape[0] for part in parts)
    shape = (columns, tokens)
    return pl.pallas_call(
        lambda *refs: grad_kernel(len(parts), *refs),
        out_shape=pltpu.HBM(shape, jnp.bfloat16),
        in_specs=[VMEM] * (len(parts) + 1) + [ANY] * len(after),
        out_specs=ANY,
        scratch_shapes=[
            pltpu.VMEM((tokens, depth), jnp.bfloat16),
            pltpu.VMEM(shape, jnp.bfloat16),
            pltpu.SemaphoreType.DMA((columns // 256,)),
        ],
        compiler_params=PARAMS,
        name="grad",
    )(*parts, basis, *after)


def act_sum_kernel(place, got, kept, given):
    total = got[0].astype(jnp.float32)
    for source in range(1, got.shape[0]):
        total += got[source].astype(jnp.float32)
    low, high = total[:, : kept.shape[1]], total[:, kept.shape[1] :]
    first = place[0] == 0
    kept[...] = jnp.where(first, low, high)
    given[...] = jnp.where(first, high, low)


def act_squares(partials):
    got = lax.all_to_all(partials, ("x", "y"), 0, 0, tiled=True)
    _, tokens, wide = got.shape
    half = jax.ShapeDtypeStruct((tokens, wide // 2), jnp.float32)
    place = lax.axis_index("z_hi").astype(jnp.int32).reshape(1)
    kept, given = pl.pallas_call(
        act_sum_kernel,
        out_shape=(half, half),
        in_specs=[SMEM, VMEM],
        out_specs=(VMEM, VMEM),
        compiler_params=PARAMS,
        name="act_sum",
    )(place, got)
    total = kept + shifted(given, "z_hi", 1)
    square = (total * total).astype(jnp.bfloat16)
    return [square] + [shifted(square, "x", step) for step in (1, 2, 3)]


def gate_kernel(*refs):
    del refs


def gated(value, after, place=pltpu.HBM):
    return pl.pallas_call(
        gate_kernel,
        out_shape=place(value.shape, value.dtype),
        in_specs=[ANY] * (1 + len(after)),
        out_specs=ANY,
        input_output_aliases={0: 0},
        compiler_params=PARAMS,
        name="gate",
    )(value, *after)


def exchanged(partial):
    columns, tokens = partial.shape
    return lax.all_to_all(partial.reshape(16, columns // 16, tokens), ("x", "y"), 0, 0, tiled=True)


def squared(got):
    summed = jnp.sum(got.astype(jnp.float32), axis=0)
    total = summed + shifted(summed.astype(jnp.bfloat16), "z_hi", 1).astype(jnp.float32)
    return (total * total).astype(jnp.bfloat16)


def correct_kernel(place, *refs):
    pieces, acts, before, (out, act) = refs[:4], refs[4:8], refs[8:-2], refs[-2:]
    _, tokens, block = acts[0].shape
    for i, part in enumerate(acts):
        for behind in range(4):
            here = slice(i * tokens, (i + 1) * tokens), slice(behind * block, (behind + 1) * block)
            act[here] = part[behind]
    rows = pieces[0].shape[0]
    for y_behind, piece in enumerate(pieces):
        part = jnp.dot(piece[...], act[...], preferred_element_type=jnp.float32)
        part = part * (1.0 / (8 * tokens))
        at = pl.ds(pl.multiple_of(lax.rem(place[1] + 4 - y_behind, 4) * rows, rows), rows)
        for behind in range(4):
            x = lax.rem(place[0] + 4 - behind, 4)
            here = part[:, behind * block : (behind + 1) * block]
            if before:
                here = before[0][x, at, :] + here
            out[x, at, :] = here


def corrected(pieces, acts, *before):
    rows, tokens = pieces[0].shape
    block = acts[0].shape[2]
    place = jnp.stack([lax.axis_index("x"), lax.axis_index("y")]).astype(jnp.int32)
    return pl.pallas_call(
        correct_kernel,
        out_shape=jax.ShapeDtypeStruct((4, 4 * rows, block), jnp.float32),
        in_specs=[SMEM] + [VMEM] * (8 + len(before)),
        out_specs=VMEM,
        scratch_shapes=[pltpu.VMEM((tokens, 4 * block), jnp.bfloat16)],
        compiler_params=PARAMS,
        name="correct",
    )(place, *pieces, *acts, *before)


def per_device(hidden, norm_gain, gate_pre, out_grad, grad_basis, act_basis):
    act_parts, up_grad = first_partials(hidden, norm_gain, gate_pre, out_grad, act_basis)
    near, far, farthest = [shifted(up_grad, "z_lo", step) for step in (1, 2, 3)]
    near = gated(near, [far], jax.ShapeDtypeStruct)
    near_rows = [up_grad, shifted(up_grad, "core", 1), near, shifted(near, "core", 1)]
    far_rows = [far, shifted(far, "core", 1), farthest, shifted(farthest, "core", 1)]
    act_row = act_squares(act_parts)
    near_got = exchanged(grad_partials(near_rows, grad_basis))
    far_got = exchanged(gated(grad_partials(far_rows, grad_basis), act_row))
    act_own = jnp.stack(act_row)
    acts = []
    for own in [act_own] + [shifted(act_own, "z_lo", step) for step in (1, 2, 3)]:
        acts += [own, shifted(own, "core", 1)]
    near_sq = squared(near_got)
    near_pieces = [near_sq] + [shifted(near_sq, "y", step) for step in (1, 2, 3)]
    far_sq = squared(gated(far_got, acts, jax.ShapeDtypeStruct))
    far_pieces = [far_sq] + [shifted(far_sq, "y", step) for step in (1, 2, 3)]
    out = corrected(far_pieces, acts[4:], corrected(near_pieces, acts[:4]))
    out = lax.all_to_all(out, "x", 0, 0, tiled=True)
    return out.reshape(grad_basis.shape[1], -1)


def solution(mesh):
    fine = Mesh(mesh.devices.reshape(SIZES), AXES)
    placed = (
        P(TENSOR, None),
        P(),
        P(TENSOR, DP),
        P(TENSOR, DP),
        P(DP, TENSOR),
        P(DP, None),
    )
    return jax.shard_map(
        per_device, mesh=fine, in_specs=placed, out_specs=P(TENSOR, DP), check_vma=False
    )
```

```python
import jax
import jax.numpy as jnp
from jax import lax
from jax.experimental import pallas as pl
from jax.experimental.pallas import tpu as pltpu
from jax.sharding import Mesh
from jax.sharding import PartitionSpec as P

AXES = ("z_hi", "x", "y", "z_lo", "core")
SIZES = (2, 4, 4, 4, 2)
DP = ("z_hi", "x", "y")
TENSOR = ("z_lo", "core")
SMEM = pl.BlockSpec(memory_space=pltpu.SMEM)
VMEM = pl.BlockSpec(memory_space=pltpu.VMEM)
ANY = pl.BlockSpec(memory_space=pl.ANY)
PARAMS = pltpu.CompilerParams(vmem_limit_bytes=32 * 1024 * 1024)
WHOLE = pltpu.CompilerParams(vmem_limit_bytes=60 * 1024 * 1024)


def shifted(value, axis, step):
    size = SIZES[AXES.index(axis)]
    return lax.ppermute(value, axis, [(i, (i + step) % size) for i in range(size)])


def act_kernel(place, gain, hidden_at, basis_at, out_at, hidden, basis, out, sems):
    tokens, features = hidden.shape
    depth = basis.shape[0]
    strip = tokens // 4
    loads = [
        pltpu.make_async_copy(hidden_at.at[here], hidden.at[here], sems.at[i])
        for i, here in enumerate(pl.ds(at, strip) for at in range(0, tokens, strip))
    ]
    load_basis = pltpu.make_async_copy(basis_at, basis, sems.at[4])
    for load in (*loads, load_basis):
        load.start()
    stats = []
    for i, load in enumerate(loads):
        load.wait()
        squares = jnp.zeros((strip, 128), jnp.float32)
        for at in range(0, features, 128):
            wide = hidden[i * strip : (i + 1) * strip, at : at + 128].astype(jnp.float32)
            squares += wide * wide
        stats.append(jnp.sum(squares, axis=-1, keepdims=True) / features)
    stat = jnp.concatenate(stats, axis=0)
    mine = pl.ds(pl.multiple_of(place[0] * depth, depth), depth)
    scaled = hidden[:, mine].astype(jnp.float32) * lax.rsqrt(stat + 1e-05)
    normed = (scaled * gain[:, mine]).astype(jnp.bfloat16)
    load_basis.wait()
    block = basis.shape[1] // 32
    stores = []
    for x in range(4):
        for z_hi in range(2):
            at = (z_hi * 16 + x * 4) * block
            part = jnp.dot(
                normed, basis[:, at : at + 4 * block], preferred_element_type=jnp.float32
            )
            for y in range(4):
                here = part[:, y * block : (y + 1) * block]
                to = slice(z_hi * block, (z_hi + 1) * block)
                out[x * 4 + y, :, to] = here.astype(jnp.bfloat16)
        here = pl.ds(x * 4, 4)
        to = out_at.at[here, pl.ds(0, tokens)]
        stores.append(pltpu.make_async_copy(out.at[here], to, sems.at[5 + x]))
        stores[-1].start()
    for store in stores:
        store.wait()


def act_partials(hidden, norm_gain, act_basis, share):
    tokens = hidden.shape[0]
    wide = act_basis.shape[1] // 16
    place = lax.axis_index(DP).astype(jnp.int32).reshape(1)
    return pl.pallas_call(
        act_kernel,
        out_shape=pltpu.HBM((16, tokens + share, wide), jnp.bfloat16),
        in_specs=[SMEM, VMEM, ANY, ANY],
        out_specs=ANY,
        scratch_shapes=[
            pltpu.VMEM(hidden.shape, jnp.bfloat16),
            pltpu.VMEM(act_basis.shape, jnp.bfloat16),
            pltpu.VMEM((16, tokens, wide), jnp.bfloat16),
            pltpu.SemaphoreType.DMA((9,)),
        ],
        compiler_params=WHOLE,
        name="act",
    )(place, norm_gain.reshape(1, -1), hidden, act_basis)


def own_kernel(own, other, basis, filled, out_at, rows, out, sem):
    del filled
    tokens = own.shape[0]
    rows[:tokens, :] = own[...]
    rows[tokens:, :] = other[...]
    share = out.shape[1]
    for at in range(0, basis.shape[1], 256):
        part = jnp.dot(rows[...], basis[:, at : at + 256], preferred_element_type=jnp.float32)
        part = part.T.astype(jnp.bfloat16)
        for owner in range(at // share, (at + 255) // share + 1):
            low, high = max(at, owner * share), min(at + 256, (owner + 1) * share)
            to = low - owner * share
            out[owner, to : to + high - low, :] = part[low - at : high - at, :]
    store = pltpu.make_async_copy(out, out_at.at[:, pl.ds(tokens, share)], sem)
    store.start()
    store.wait()


def own_partials(filled, own, other, basis):
    tokens, depth = own.shape
    return pl.pallas_call(
        own_kernel,
        out_shape=pltpu.HBM(filled.shape, filled.dtype),
        in_specs=[VMEM, VMEM, VMEM, ANY],
        out_specs=ANY,
        scratch_shapes=[
            pltpu.VMEM((2 * tokens, depth), jnp.bfloat16),
            pltpu.VMEM((16, basis.shape[1] // 16, 2 * tokens), jnp.bfloat16),
            pltpu.SemaphoreType.DMA,
        ],
        input_output_aliases={3: 0},
        compiler_params=PARAMS,
        name="own",
    )(own, other, basis, filled)


def grad_kernel(count, *refs):
    parts, basis, out_at, rows, out, sem = refs[:count], refs[count], *refs[-4:]
    at = 0
    for part in parts:
        rows[at : at + part.shape[0], :] = part[...]
        at += part.shape[0]
    stores = []
    for at in range(0, basis.shape[1], 256):
        here = pl.ds(at, 256)
        part = jnp.dot(rows[...], basis[:, here], preferred_element_type=jnp.float32)
        out[here, :] = part.T.astype(jnp.bfloat16)
        stores.append(
            pltpu.make_async_copy(out.at[here], out_at.at[here], sem.at[at // 256])
        )
        stores[-1].start()
    for store in stores:
        store.wait()


def grad_partials(parts, basis):
    depth, columns = basis.shape
    tokens = sum(part.shape[0] for part in parts)
    shape = (columns, tokens)
    return pl.pallas_call(
        lambda *refs: grad_kernel(len(parts), *refs),
        out_shape=pltpu.HBM(shape, jnp.bfloat16),
        in_specs=[VMEM] * (len(parts) + 1),
        out_specs=ANY,
        scratch_shapes=[
            pltpu.VMEM((tokens, depth), jnp.bfloat16),
            pltpu.VMEM(shape, jnp.bfloat16),
            pltpu.SemaphoreType.DMA((columns // 256,)),
        ],
        compiler_params=PARAMS,
        name="grad",
    )(*parts, basis)


def first_sum_kernel(place, got, kept, grad, given):
    tokens, block = kept.shape
    half = tokens // 2
    act = got[0, :tokens, :].astype(jnp.float32)
    for source in range(1, got.shape[0]):
        act += got[source, :tokens, :].astype(jnp.float32)
    low, high = act[:, :block], act[:, block:]
    first = place[0] == 0
    kept[...] = jnp.where(first, low, high)
    away = jnp.where(first, high, low).astype(jnp.bfloat16)
    given[:half, :block] = away[:half]
    given[:half, block:] = away[half:]
    total = got[0, tokens:, :].astype(jnp.float32)
    for source in range(1, got.shape[0]):
        total += got[source, tokens:, :].astype(jnp.float32)
    grad[...] = total
    given[half:, :] = total.astype(jnp.bfloat16)


def square_kernel(kept, grad, got, act_sq, grad_sq):
    tokens, block = kept.shape
    half = tokens // 2
    for part in range(2):
        rows = slice(part * half, (part + 1) * half)
        total = kept[rows, :] + got[:half, part * block : (part + 1) * block].astype(jnp.float32)
        act_sq[rows, :] = (total * total).astype(jnp.bfloat16)
    total = grad[...] + got[half:, :].astype(jnp.float32)
    grad_sq[...] = (total * total).astype(jnp.bfloat16)


def first_squares(got, tokens):
    share, wide = got.shape[1] - tokens, got.shape[2]
    block = wide // 2
    place = lax.axis_index("z_hi").astype(jnp.int32).reshape(1)
    kept, grad, given = pl.pallas_call(
        first_sum_kernel,
        out_shape=(
            jax.ShapeDtypeStruct((tokens, block), jnp.float32),
            jax.ShapeDtypeStruct((share, wide), jnp.float32),
            jax.ShapeDtypeStruct((tokens // 2 + share, wide), jnp.bfloat16),
        ),
        in_specs=[SMEM, VMEM],
        out_specs=(VMEM, VMEM, VMEM),
        compiler_params=PARAMS,
        name="first_sum",
    )(place, got)
    return pl.pallas_call(
        square_kernel,
        out_shape=(
            jax.ShapeDtypeStruct((tokens, block), jnp.bfloat16),
            jax.ShapeDtypeStruct((share, wide), jnp.bfloat16),
        ),
        in_specs=[VMEM] * 3,
        out_specs=(VMEM, VMEM),
        compiler_params=PARAMS,
        name="square",
    )(kept, grad, shifted(given, "z_hi", 1))


def gate_kernel(*refs):
    del refs


def gated(value, after, place=pltpu.HBM):
    return pl.pallas_call(
        gate_kernel,
        out_shape=place(value.shape, value.dtype),
        in_specs=[ANY] * (1 + len(after)),
        out_specs=ANY,
        input_output_aliases={0: 0},
        compiler_params=PARAMS,
        name="gate",
    )(value, *after)


def exchanged(partial):
    columns, tokens = partial.shape
    return lax.all_to_all(partial.reshape(16, columns // 16, tokens), ("x", "y"), 0, 0, tiled=True)


def squared(got):
    summed = jnp.sum(got.astype(jnp.float32), axis=0)
    total = summed + shifted(summed.astype(jnp.bfloat16), "z_hi", 1).astype(jnp.float32)
    return (total * total).astype(jnp.bfloat16)


def correct_kernel(steps, place, *refs):
    pieces, acts, before, (out, act) = refs[:4], refs[4:8], refs[8:-2], refs[-2:]
    chips, cores, tokens, block = acts[0].shape
    for behind, part in enumerate(acts):
        to = slice(behind * block, (behind + 1) * block)
        for i, step in enumerate(steps):
            for core in range(cores):
                at = (i * cores + core) * tokens
                act[at : at + tokens, to] = part[step, core]
    rows = pieces[0].shape[0]
    for y_behind, piece in enumerate(pieces):
        part = jnp.dot(piece[...], act[...], preferred_element_type=jnp.float32)
        part = part * (1.0 / (chips * cores * tokens))
        at = pl.ds(pl.multiple_of(lax.rem(place[1] + 4 - y_behind, 4) * rows, rows), rows)
        for behind in range(4):
            x = lax.rem(place[0] + 4 - behind, 4)
            here = part[:, behind * block : (behind + 1) * block]
            if before:
                here = before[0][x, at, :] + here
            out[x, at, :] = here


def spread(grad_sq):
    return [grad_sq] + [shifted(grad_sq, "y", step) for step in (1, 2, 3)]


def corrected(steps, pieces, acts, *before):
    rows, tokens = pieces[0].shape
    block = acts[0].shape[3]
    place = jnp.stack([lax.axis_index("x"), lax.axis_index("y")]).astype(jnp.int32)
    return pl.pallas_call(
        lambda *refs: correct_kernel(steps, *refs),
        out_shape=jax.ShapeDtypeStruct((4, 4 * rows, block), jnp.float32),
        in_specs=[SMEM] + [VMEM] * (8 + len(before)),
        out_specs=VMEM,
        scratch_shapes=[pltpu.VMEM((tokens, 4 * block), jnp.bfloat16)],
        compiler_params=PARAMS,
        name="correct",
    )(place, *pieces, *acts, *before)


def per_device(hidden, norm_gain, gate_pre, out_grad, grad_basis, act_basis):
    tokens = hidden.shape[0]
    up_grad = (out_grad.astype(jnp.float32) * jax.nn.silu(gate_pre.astype(jnp.float32))).astype(
        jnp.bfloat16
    )
    first = act_partials(hidden, norm_gain, act_basis, grad_basis.shape[1] // 16)
    first = own_partials(first, up_grad, shifted(up_grad, "core", 1), grad_basis)
    first_got = lax.all_to_all(first, ("x", "y"), 0, 0, tiled=True)
    rows = []
    for step in (1, 2, 3):
        own = shifted(up_grad, "z_lo", step)
        rows += [own, shifted(own, "core", 1)]
    rest_got = exchanged(grad_partials(rows, grad_basis))
    act_own, first_sq = first_squares(first_got, tokens)
    act_chip = jnp.stack([act_own, shifted(act_own, "core", 1)])
    act_all = [act_chip] + [shifted(act_chip, "z_lo", step) for step in (1, 2, 3)]
    first_pieces = spread(first_sq)
    rest_sq = squared(gated(rest_got, act_all + first_pieces, jax.ShapeDtypeStruct))
    act_all = jnp.stack(act_all)
    acts = [act_all] + [shifted(act_all, "x", step) for step in (1, 2, 3)]
    out = corrected((0,), first_pieces, acts)
    out = corrected((1, 2, 3), spread(rest_sq), acts, out)
    out = lax.all_to_all(out, "x", 0, 0, tiled=True)
    return out.reshape(grad_basis.shape[1], -1)


def solution(mesh):
    fine = Mesh(mesh.devices.reshape(SIZES), AXES)
    placed = (
        P(TENSOR, None),
        P(),
        P(TENSOR, DP),
        P(TENSOR, DP),
        P(DP, TENSOR),
        P(DP, None),
    )
    return jax.shard_map(
        per_device, mesh=fine, in_specs=placed, out_specs=P(TENSOR, DP), check_vma=False
    )
```

```python
import jax
import jax.numpy as jnp
from jax import lax
from jax.experimental import pallas as pl
from jax.experimental.pallas import tpu as pltpu
from jax.sharding import Mesh
from jax.sharding import PartitionSpec as P

AXES = ("z_hi", "x", "y", "z_lo", "core")
SIZES = (2, 4, 4, 4, 2)
DP = ("z_hi", "x", "y")
TENSOR = ("z_lo", "core")
SMEM = pl.BlockSpec(memory_space=pltpu.SMEM)
VMEM = pl.BlockSpec(memory_space=pltpu.VMEM)
ANY = pl.BlockSpec(memory_space=pl.ANY)
PARAMS = pltpu.CompilerParams(vmem_limit_bytes=32 * 1024 * 1024)
WHOLE = pltpu.CompilerParams(vmem_limit_bytes=60 * 1024 * 1024)


def shifted(value, axis, step):
    size = SIZES[AXES.index(axis)]
    return lax.ppermute(value, axis, [(i, (i + step) % size) for i in range(size)])


def act_kernel(place, gain, hidden_at, basis_at, out_at, hidden, basis, out, sems):
    tokens, features = hidden.shape
    depth = basis.shape[0]
    strip = tokens // 4
    loads = [
        pltpu.make_async_copy(hidden_at.at[here], hidden.at[here], sems.at[i])
        for i, here in enumerate(pl.ds(at, strip) for at in range(0, tokens, strip))
    ]
    load_basis = pltpu.make_async_copy(basis_at, basis, sems.at[4])
    for load in (*loads, load_basis):
        load.start()
    stats = []
    for i, load in enumerate(loads):
        load.wait()
        squares = jnp.zeros((strip, 128), jnp.float32)
        for at in range(0, features, 128):
            wide = hidden[i * strip : (i + 1) * strip, at : at + 128].astype(jnp.float32)
            squares += wide * wide
        stats.append(jnp.sum(squares, axis=-1, keepdims=True) / features)
    stat = jnp.concatenate(stats, axis=0)
    mine = pl.ds(pl.multiple_of(place[0] * depth, depth), depth)
    scaled = hidden[:, mine].astype(jnp.float32) * lax.rsqrt(stat + 1e-05)
    normed = (scaled * gain[:, mine]).astype(jnp.bfloat16)
    load_basis.wait()
    block = basis.shape[1] // 32
    stores = []
    for x in range(4):
        for z_hi in range(2):
            at = (z_hi * 16 + x * 4) * block
            part = jnp.dot(
                normed, basis[:, at : at + 4 * block], preferred_element_type=jnp.float32
            )
            for y in range(4):
                here = part[:, y * block : (y + 1) * block]
                to = slice(z_hi * block, (z_hi + 1) * block)
                out[x * 4 + y, :, to] = here.astype(jnp.bfloat16)
        here = pl.ds(x * 4, 4)
        to = out_at.at[here, pl.ds(0, tokens)]
        stores.append(pltpu.make_async_copy(out.at[here], to, sems.at[5 + x]))
        stores[-1].start()
    for store in stores:
        store.wait()


def act_partials(hidden, norm_gain, act_basis, share):
    tokens = hidden.shape[0]
    wide = act_basis.shape[1] // 16
    place = lax.axis_index(DP).astype(jnp.int32).reshape(1)
    return pl.pallas_call(
        act_kernel,
        out_shape=pltpu.HBM((16, tokens + share, wide), jnp.bfloat16),
        in_specs=[SMEM, VMEM, ANY, ANY],
        out_specs=ANY,
        scratch_shapes=[
            pltpu.VMEM(hidden.shape, jnp.bfloat16),
            pltpu.VMEM(act_basis.shape, jnp.bfloat16),
            pltpu.VMEM((16, tokens, wide), jnp.bfloat16),
            pltpu.SemaphoreType.DMA((9,)),
        ],
        compiler_params=WHOLE,
        name="act",
    )(place, norm_gain.reshape(1, -1), hidden, act_basis)


def grad_kernel(count, start, *refs):
    parts, basis, (out_at, mark, rows, out, sems) = refs[:count], refs[count], refs[-5:]
    mark[...] = jnp.zeros_like(mark)
    tokens = parts[0].shape[0]
    for i, part in enumerate(parts):
        rows[i * tokens : (i + 1) * tokens, :] = part[...]
    columns = basis.shape[1]
    share = columns // 16
    stores = []
    for at in range(0, columns, 256):
        part = jnp.dot(rows[...], basis[:, at : at + 256], preferred_element_type=jnp.float32)
        part = part.T.astype(jnp.bfloat16)
        for owner in range(at // share, (at + 255) // share + 1):
            low, high = max(at, owner * share), min(at + 256, (owner + 1) * share)
            for chip in range(count // 2):
                to = chip * share + low - owner * share
                here = slice(2 * chip * tokens, 2 * (chip + 1) * tokens)
                out[owner, to : to + high - low, :] = part[low - at : high - at, here]
        while 4 * (len(stores) + 1) * share <= at + 256:
            here = pl.ds(4 * len(stores), 4)
            to = out_at.at[here, pl.ds(start, out.shape[1])]
            stores.append(pltpu.make_async_copy(out.at[here], to, sems.at[len(stores)]))
            stores[-1].start()
    for store in stores:
        store.wait()


def grad_partials(parts, basis, height, start=0, *filled):
    tokens, depth = parts[0].shape
    share = basis.shape[1] // 16
    return pl.pallas_call(
        lambda *refs: grad_kernel(len(parts), start, *refs),
        out_shape=(
            pltpu.HBM((16, height, 2 * tokens), jnp.bfloat16),
            jax.ShapeDtypeStruct((8, 128), jnp.float32),
        ),
        in_specs=[VMEM] * (len(parts) + 1) + [ANY] * len(filled),
        out_specs=(ANY, VMEM),
        scratch_shapes=[
            pltpu.VMEM((len(parts) * tokens, depth), jnp.bfloat16),
            pltpu.VMEM((16, len(parts) // 2 * share, 2 * tokens), jnp.bfloat16),
            pltpu.SemaphoreType.DMA((4,)),
        ],
        input_output_aliases={len(parts) + 1: 0} if filled else {},
        compiler_params=PARAMS,
        name="grad",
    )(*parts, basis, *filled)


def first_sum_kernel(place, got, kept, grad, given):
    tokens, block = kept.shape
    half = tokens // 2
    act = got[0, :tokens, :].astype(jnp.float32)
    for source in range(1, got.shape[0]):
        act += got[source, :tokens, :].astype(jnp.float32)
    low, high = act[:, :block], act[:, block:]
    first = place[0] == 0
    kept[...] = jnp.where(first, low, high)
    away = jnp.where(first, high, low).astype(jnp.bfloat16)
    given[:half, :block] = away[:half]
    given[:half, block:] = away[half:]
    total = got[0, tokens:, :].astype(jnp.float32)
    for source in range(1, got.shape[0]):
        total += got[source, tokens:, :].astype(jnp.float32)
    grad[...] = total
    given[half:, :] = total.astype(jnp.bfloat16)


def square_kernel(kept, grad, got, act_sq, grad_sq):
    tokens, block = kept.shape
    half = tokens // 2
    for part in range(2):
        rows = slice(part * half, (part + 1) * half)
        total = kept[rows, :] + got[:half, part * block : (part + 1) * block].astype(jnp.float32)
        act_sq[rows, :] = (total * total).astype(jnp.bfloat16)
    total = grad[...] + got[half:, :].astype(jnp.float32)
    grad_sq[...] = (total * total).astype(jnp.bfloat16)


def first_squares(got, tokens):
    share, wide = got.shape[1] - tokens, got.shape[2]
    block = wide // 2
    place = lax.axis_index("z_hi").astype(jnp.int32).reshape(1)
    kept, grad, given = pl.pallas_call(
        first_sum_kernel,
        out_shape=(
            jax.ShapeDtypeStruct((tokens, block), jnp.float32),
            jax.ShapeDtypeStruct((share, wide), jnp.float32),
            jax.ShapeDtypeStruct((tokens // 2 + share, wide), jnp.bfloat16),
        ),
        in_specs=[SMEM, VMEM],
        out_specs=(VMEM, VMEM, VMEM),
        compiler_params=PARAMS,
        name="first_sum",
    )(place, got)
    return pl.pallas_call(
        square_kernel,
        out_shape=(
            jax.ShapeDtypeStruct((tokens, block), jnp.bfloat16),
            jax.ShapeDtypeStruct((share, wide), jnp.bfloat16),
        ),
        in_specs=[VMEM] * 3,
        out_specs=(VMEM, VMEM),
        compiler_params=PARAMS,
        name="square",
    )(kept, grad, shifted(given, "z_hi", 1))


def gate_kernel(*refs):
    del refs


def gated(value, after, place=pltpu.HBM):
    return pl.pallas_call(
        gate_kernel,
        out_shape=place(value.shape, value.dtype),
        in_specs=[ANY] * (1 + len(after)),
        out_specs=ANY,
        input_output_aliases={0: 0},
        compiler_params=PARAMS,
        name="gate",
    )(value, *after)


def squared(got):
    summed = jnp.sum(got.astype(jnp.float32), axis=0)
    total = summed + shifted(summed.astype(jnp.bfloat16), "z_hi", 1).astype(jnp.float32)
    return (total * total).astype(jnp.bfloat16)


def correct_kernel(steps, place, *refs):
    pieces, acts, before, (out, act) = refs[:4], refs[4:8], refs[8:-2], refs[-2:]
    chips, cores, tokens, block = acts[0].shape
    for behind, part in enumerate(acts):
        to = slice(behind * block, (behind + 1) * block)
        for i, step in enumerate(steps):
            for core in range(cores):
                at = (i * cores + core) * tokens
                act[at : at + tokens, to] = part[step, core]
    rows = pieces[0].shape[0] // len(steps)
    wide = cores * tokens
    for y_behind, piece in enumerate(pieces):
        part = sum(
            jnp.dot(
                piece[i * rows : (i + 1) * rows, :],
                act[i * wide : (i + 1) * wide, :],
                preferred_element_type=jnp.float32,
            )
            for i in range(len(steps))
        )
        part = part * (1.0 / (chips * cores * tokens))
        at = pl.ds(pl.multiple_of(lax.rem(place[1] + 4 - y_behind, 4) * rows, rows), rows)
        for behind in range(4):
            x = lax.rem(place[0] + 4 - behind, 4)
            here = part[:, behind * block : (behind + 1) * block]
            if before:
                here = before[0][x, at, :] + here
            out[x, at, :] = here


def spread(grad_sq):
    return [grad_sq] + [shifted(grad_sq, "y", step) for step in (1, 2, 3)]


def corrected(steps, pieces, acts, *before):
    rows = pieces[0].shape[0] // len(steps)
    _, cores, tokens, block = acts[0].shape
    place = jnp.stack([lax.axis_index("x"), lax.axis_index("y")]).astype(jnp.int32)
    return pl.pallas_call(
        lambda *refs: correct_kernel(steps, *refs),
        out_shape=jax.ShapeDtypeStruct((4, 4 * rows, block), jnp.float32),
        in_specs=[SMEM] + [VMEM] * (8 + len(before)),
        out_specs=VMEM,
        scratch_shapes=[pltpu.VMEM((len(steps) * cores * tokens, 4 * block), jnp.bfloat16)],
        compiler_params=PARAMS,
        name="correct",
    )(place, *pieces, *acts, *before)


def chip_rows(own):
    return [own, shifted(own, "core", 1)]


def per_device(hidden, norm_gain, gate_pre, out_grad, grad_basis, act_basis):
    tokens = hidden.shape[0]
    share = grad_basis.shape[1] // 16
    up_grad = (out_grad.astype(jnp.float32) * jax.nn.silu(gate_pre.astype(jnp.float32))).astype(
        jnp.bfloat16
    )
    near, *far = [shifted(up_grad, "z_lo", step) for step in (1, 2, 3)]
    height = tokens + 2 * share
    first = act_partials(hidden, norm_gain, act_basis, 2 * share)
    first, mark = grad_partials(chip_rows(up_grad), grad_basis, height, tokens, first)
    near = gated(near, [mark], jax.ShapeDtypeStruct)
    first, _ = grad_partials(chip_rows(near), grad_basis, height, tokens + share, first)
    first_got = lax.all_to_all(first, ("x", "y"), 0, 0, tiled=True)
    rest, _ = grad_partials(chip_rows(far[0]) + chip_rows(far[1]), grad_basis, 2 * share)
    rest_got = lax.all_to_all(rest, ("x", "y"), 0, 0, tiled=True)
    act_own, first_sq = first_squares(first_got, tokens)
    act_chip = jnp.stack([act_own, shifted(act_own, "core", 1)])
    act_all = [act_chip] + [shifted(act_chip, "z_lo", step) for step in (1, 2, 3)]
    rest_sq = squared(gated(rest_got, act_all, jax.ShapeDtypeStruct))
    act_all = jnp.stack(act_all)
    acts = [act_all] + [shifted(act_all, "x", step) for step in (1, 2, 3)]
    out = corrected((0, 1), spread(first_sq), acts)
    out = corrected((2, 3), spread(rest_sq), acts, out)
    out = lax.all_to_all(out, "x", 0, 0, tiled=True)
    return out.reshape(grad_basis.shape[1], -1)


def solution(mesh):
    fine = Mesh(mesh.devices.reshape(SIZES), AXES)
    placed = (
        P(TENSOR, None),
        P(),
        P(TENSOR, DP),
        P(TENSOR, DP),
        P(DP, TENSOR),
        P(DP, None),
    )
    return jax.shard_map(
        per_device, mesh=fine, in_specs=placed, out_specs=P(TENSOR, DP), check_vma=False
    )
```

```python
import jax
import jax.numpy as jnp
from jax import lax
from jax.experimental import pallas as pl
from jax.experimental.pallas import tpu as pltpu
from jax.sharding import Mesh
from jax.sharding import PartitionSpec as P

AXES = ("z_hi", "x", "y", "z_lo", "core")
SIZES = (2, 4, 4, 4, 2)
DP = ("z_hi", "x", "y")
TENSOR = ("z_lo", "core")
SMEM = pl.BlockSpec(memory_space=pltpu.SMEM)
VMEM = pl.BlockSpec(memory_space=pltpu.VMEM)
ANY = pl.BlockSpec(memory_space=pl.ANY)
PARAMS = pltpu.CompilerParams(vmem_limit_bytes=32 * 1024 * 1024)
WHOLE = pltpu.CompilerParams(vmem_limit_bytes=60 * 1024 * 1024)


def shifted(value, axis, step):
    size = SIZES[AXES.index(axis)]
    return lax.ppermute(value, axis, [(i, (i + step) % size) for i in range(size)])


def first_kernel(place, gain, gate_at, grad_at, hidden_at, basis_at, out_at, up_at,
                 gate, grad, hidden, basis, out, up, sems):
    tokens, features = hidden.shape
    depth = basis.shape[0]
    strip = tokens // 4
    load_gate = pltpu.make_async_copy(gate_at, gate, sems.at[9])
    load_grad = pltpu.make_async_copy(grad_at, grad, sems.at[10])
    loads = [
        pltpu.make_async_copy(hidden_at.at[here], hidden.at[here], sems.at[i])
        for i, here in enumerate(pl.ds(at, strip) for at in range(0, tokens, strip))
    ]
    load_basis = pltpu.make_async_copy(basis_at, basis, sems.at[4])
    for load in (load_gate, load_grad, *loads, load_basis):
        load.start()
    load_gate.wait()
    load_grad.wait()
    for at in range(0, tokens, 32):
        here = slice(at, at + 32)
        wide = gate[here, :].astype(jnp.float32)
        wide = grad[here, :].astype(jnp.float32) * (wide / (1.0 + jnp.exp(-wide)))
        up[here, :] = wide.astype(jnp.bfloat16)
    store_up = pltpu.make_async_copy(up, up_at, sems.at[11])
    store_up.start()
    stats = []
    for i, load in enumerate(loads):
        load.wait()
        squares = jnp.zeros((strip, 128), jnp.float32)
        for at in range(0, features, 128):
            wide = hidden[i * strip : (i + 1) * strip, at : at + 128].astype(jnp.float32)
            squares += wide * wide
        stats.append(jnp.sum(squares, axis=-1, keepdims=True) / features)
    stat = jnp.concatenate(stats, axis=0)
    mine = pl.ds(pl.multiple_of(place[0] * depth, depth), depth)
    scaled = hidden[:, mine].astype(jnp.float32) * lax.rsqrt(stat + 1e-05)
    normed = (scaled * gain[:, mine]).astype(jnp.bfloat16)
    load_basis.wait()
    block = basis.shape[1] // 32
    stores = [store_up]
    for x in range(4):
        for z_hi in range(2):
            at = (z_hi * 16 + x * 4) * block
            part = jnp.dot(
                normed, basis[:, at : at + 4 * block], preferred_element_type=jnp.float32
            )
            for y in range(4):
                here = part[:, y * block : (y + 1) * block]
                to = slice(z_hi * block, (z_hi + 1) * block)
                out[x * 4 + y, :, to] = here.astype(jnp.bfloat16)
        here = pl.ds(x * 4, 4)
        stores.append(pltpu.make_async_copy(out.at[here], out_at.at[here], sems.at[5 + x]))
        stores[-1].start()
    for store in stores:
        store.wait()


def first_partials(hidden, norm_gain, gate_pre, out_grad, act_basis):
    tokens = hidden.shape[0]
    shape = (16, tokens, act_basis.shape[1] // 16)
    place = lax.axis_index(DP).astype(jnp.int32).reshape(1)
    return pl.pallas_call(
        first_kernel,
        out_shape=(pltpu.HBM(shape, jnp.bfloat16), pltpu.HBM(out_grad.shape, jnp.bfloat16)),
        in_specs=[SMEM, VMEM, ANY, ANY, ANY, ANY],
        out_specs=(ANY, ANY),
        scratch_shapes=[
            pltpu.VMEM(gate_pre.shape, jnp.bfloat16),
            pltpu.VMEM(out_grad.shape, jnp.bfloat16),
            pltpu.VMEM(hidden.shape, jnp.bfloat16),
            pltpu.VMEM(act_basis.shape, jnp.bfloat16),
            pltpu.VMEM(shape, jnp.bfloat16),
            pltpu.VMEM(out_grad.shape, jnp.bfloat16),
            pltpu.SemaphoreType.DMA((12,)),
        ],
        compiler_params=WHOLE,
        name="first",
    )(place, norm_gain.reshape(1, -1), gate_pre, out_grad, hidden, act_basis)


def grad_kernel(count, *refs):
    parts, basis, out_at, rows, out, sem = refs[:count], refs[count], *refs[-4:]
    at = 0
    for part in parts:
        rows[at : at + part.shape[0], :] = part[...]
        at += part.shape[0]
    stores = []
    for at in range(0, basis.shape[1], 256):
        here = pl.ds(at, 256)
        part = jnp.dot(rows[...], basis[:, here], preferred_element_type=jnp.float32)
        out[here, :] = part.T.astype(jnp.bfloat16)
        stores.append(
            pltpu.make_async_copy(out.at[here], out_at.at[here], sem.at[at // 256])
        )
        stores[-1].start()
    for store in stores:
        store.wait()


def grad_partials(parts, basis, after=(), cost=None):
    depth, columns = basis.shape
    tokens = sum(part.shape[0] for part in parts)
    shape = (columns, tokens)
    return pl.pallas_call(
        lambda *refs: grad_kernel(len(parts), *refs),
        out_shape=pltpu.HBM(shape, jnp.bfloat16),
        in_specs=[VMEM] * (len(parts) + 1) + [ANY] * len(after),
        out_specs=ANY,
        scratch_shapes=[
            pltpu.VMEM((tokens, depth), jnp.bfloat16),
            pltpu.VMEM(shape, jnp.bfloat16),
            pltpu.SemaphoreType.DMA((columns // 256,)),
        ],
        compiler_params=PARAMS,
        cost_estimate=cost,
        name="grad",
    )(*parts, basis, *after)


def act_sum_kernel(place, got, kept, given):
    total = got[0].astype(jnp.float32)
    for source in range(1, got.shape[0]):
        total += got[source].astype(jnp.float32)
    low, high = total[:, : kept.shape[1]], total[:, kept.shape[1] :]
    first = place[0] == 0
    kept[...] = jnp.where(first, low, high)
    given[...] = jnp.where(first, high, low)


def act_squares(partials):
    got = lax.all_to_all(partials, ("x", "y"), 0, 0, tiled=True)
    _, tokens, wide = got.shape
    half = jax.ShapeDtypeStruct((tokens, wide // 2), jnp.float32)
    place = lax.axis_index("z_hi").astype(jnp.int32).reshape(1)
    kept, given = pl.pallas_call(
        act_sum_kernel,
        out_shape=(half, half),
        in_specs=[SMEM, VMEM],
        out_specs=(VMEM, VMEM),
        compiler_params=PARAMS,
        name="act_sum",
    )(place, got)
    total = kept + shifted(given, "z_hi", 1)
    square = (total * total).astype(jnp.bfloat16)
    return [square] + [shifted(square, "x", step) for step in (1, 2, 3)]


def gate_kernel(*refs):
    del refs


def gated(value, after, place=pltpu.HBM):
    return pl.pallas_call(
        gate_kernel,
        out_shape=place(value.shape, value.dtype),
        in_specs=[ANY] * (1 + len(after)),
        out_specs=ANY,
        input_output_aliases={0: 0},
        compiler_params=PARAMS,
        name="gate",
    )(value, *after)


def exchanged(partial):
    columns, tokens = partial.shape
    return lax.all_to_all(partial.reshape(16, columns // 16, tokens), ("x", "y"), 0, 0, tiled=True)


def squared(got):
    summed = jnp.sum(got.astype(jnp.float32), axis=0)
    total = summed + shifted(summed.astype(jnp.bfloat16), "z_hi", 1).astype(jnp.float32)
    return (total * total).astype(jnp.bfloat16)


def correct_kernel(place, *refs):
    pieces, acts, before, (out, act) = refs[:4], refs[4:8], refs[8:-2], refs[-2:]
    _, tokens, block = acts[0].shape
    for i, part in enumerate(acts):
        for behind in range(4):
            here = slice(i * tokens, (i + 1) * tokens), slice(behind * block, (behind + 1) * block)
            act[here] = part[behind]
    rows = pieces[0].shape[0]
    for y_behind, piece in enumerate(pieces):
        part = jnp.dot(piece[...], act[...], preferred_element_type=jnp.float32)
        part = part * (1.0 / (8 * tokens))
        at = pl.ds(pl.multiple_of(lax.rem(place[1] + 4 - y_behind, 4) * rows, rows), rows)
        for behind in range(4):
            x = lax.rem(place[0] + 4 - behind, 4)
            here = part[:, behind * block : (behind + 1) * block]
            if before:
                here = before[0][x, at, :] + here
            out[x, at, :] = here


def corrected(pieces, acts, *before):
    rows, tokens = pieces[0].shape
    block = acts[0].shape[2]
    place = jnp.stack([lax.axis_index("x"), lax.axis_index("y")]).astype(jnp.int32)
    return pl.pallas_call(
        correct_kernel,
        out_shape=jax.ShapeDtypeStruct((4, 4 * rows, block), jnp.float32),
        in_specs=[SMEM] + [VMEM] * (8 + len(before)),
        out_specs=VMEM,
        scratch_shapes=[pltpu.VMEM((tokens, 4 * block), jnp.bfloat16)],
        compiler_params=PARAMS,
        name="correct",
    )(place, *pieces, *acts, *before)


def per_device(hidden, norm_gain, gate_pre, out_grad, grad_basis, act_basis):
    act_parts, up_grad = first_partials(hidden, norm_gain, gate_pre, out_grad, act_basis)
    near, far, farthest = [shifted(up_grad, "z_lo", step) for step in (1, 2, 3)]
    near = gated(near, [far, farthest], jax.ShapeDtypeStruct)
    near_rows = [up_grad, shifted(up_grad, "core", 1), near, shifted(near, "core", 1)]
    far_rows = [far, shifted(far, "core", 1), farthest, shifted(farthest, "core", 1)]
    act_row = act_squares(act_parts)
    cost = pl.CostEstimate(flops=8*10**9, bytes_accessed=10**7, transcendentals=0)
    near_got = exchanged(grad_partials(near_rows, grad_basis, (), cost))
    far_got = exchanged(gated(grad_partials(far_rows, grad_basis), act_row))
    act_own = jnp.stack(act_row)
    acts = []
    for own in [act_own] + [shifted(act_own, "z_lo", step) for step in (1, 2, 3)]:
        acts += [own, shifted(own, "core", 1)]
    near_sq = squared(near_got)
    near_pieces = [near_sq] + [shifted(near_sq, "y", step) for step in (1, 2, 3)]
    far_sq = squared(gated(far_got, acts + [near_sq], jax.ShapeDtypeStruct))
    far_pieces = [far_sq] + [shifted(far_sq, "y", step) for step in (1, 2, 3)]
    out = corrected(far_pieces, acts[4:], corrected(near_pieces, acts[:4]))
    out = lax.all_to_all(out, "x", 0, 0, tiled=True)
    return out.reshape(grad_basis.shape[1], -1)


def solution(mesh):
    fine = Mesh(mesh.devices.reshape(SIZES), AXES)
    placed = (
        P(TENSOR, None),
        P(),
        P(TENSOR, DP),
        P(TENSOR, DP),
        P(DP, TENSOR),
        P(DP, None),
    )
    return jax.shard_map(
        per_device, mesh=fine, in_specs=placed, out_specs=P(TENSOR, DP), check_vma=False
    )
```

```python
import jax
import jax.numpy as jnp
from jax import lax
from jax.experimental import pallas as pl
from jax.experimental.pallas import tpu as pltpu
from jax.sharding import Mesh
from jax.sharding import PartitionSpec as P

AXES = ("z_hi", "x", "y", "z_lo", "core")
SIZES = (2, 4, 4, 4, 2)
DP = ("z_hi", "x", "y")
TENSOR = ("z_lo", "core")
SMEM = pl.BlockSpec(memory_space=pltpu.SMEM)
VMEM = pl.BlockSpec(memory_space=pltpu.VMEM)
ANY = pl.BlockSpec(memory_space=pl.ANY)
PARAMS = pltpu.CompilerParams(vmem_limit_bytes=32 * 1024 * 1024)
WHOLE = pltpu.CompilerParams(vmem_limit_bytes=60 * 1024 * 1024)


def shifted(value, axis, step):
    size = SIZES[AXES.index(axis)]
    return lax.ppermute(value, axis, [(i, (i + step) % size) for i in range(size)])


def first_kernel(place, gain, gate_at, grad_at, hidden_at, basis_at, out_at, up_at,
                 gate, grad, hidden, basis, out, up, sems):
    tokens, features = hidden.shape
    depth = basis.shape[0]
    strip = tokens // 4
    load_gate = pltpu.make_async_copy(gate_at, gate, sems.at[9])
    load_grad = pltpu.make_async_copy(grad_at, grad, sems.at[10])
    loads = [
        pltpu.make_async_copy(hidden_at.at[here], hidden.at[here], sems.at[i])
        for i, here in enumerate(pl.ds(at, strip) for at in range(0, tokens, strip))
    ]
    load_basis = pltpu.make_async_copy(basis_at, basis, sems.at[4])
    for load in (load_gate, load_grad, *loads, load_basis):
        load.start()
    load_gate.wait()
    load_grad.wait()
    for at in range(0, tokens, 32):
        here = slice(at, at + 32)
        wide = gate[here, :].astype(jnp.float32)
        wide = grad[here, :].astype(jnp.float32) * (wide / (1.0 + jnp.exp(-wide)))
        up[here, :] = wide.astype(jnp.bfloat16)
    store_up = pltpu.make_async_copy(up, up_at, sems.at[11])
    store_up.start()
    stats = []
    for i, load in enumerate(loads):
        load.wait()
        squares = jnp.zeros((strip, 128), jnp.float32)
        for at in range(0, features, 128):
            wide = hidden[i * strip : (i + 1) * strip, at : at + 128].astype(jnp.float32)
            squares += wide * wide
        stats.append(jnp.sum(squares, axis=-1, keepdims=True) / features)
    stat = jnp.concatenate(stats, axis=0)
    mine = pl.ds(pl.multiple_of(place[0] * depth, depth), depth)
    scaled = hidden[:, mine].astype(jnp.float32) * lax.rsqrt(stat + 1e-05)
    normed = (scaled * gain[:, mine]).astype(jnp.bfloat16)
    load_basis.wait()
    block = basis.shape[1] // 32
    stores = [store_up]
    for x in range(4):
        for z_hi in range(2):
            at = (z_hi * 16 + x * 4) * block
            part = jnp.dot(
                normed, basis[:, at : at + 4 * block], preferred_element_type=jnp.float32
            )
            for y in range(4):
                here = part[:, y * block : (y + 1) * block]
                to = slice(z_hi * block, (z_hi + 1) * block)
                out[x * 4 + y, :, to] = here.astype(jnp.bfloat16)
        here = pl.ds(x * 4, 4)
        stores.append(pltpu.make_async_copy(out.at[here], out_at.at[here], sems.at[5 + x]))
        stores[-1].start()
    for store in stores:
        store.wait()


def first_partials(hidden, norm_gain, gate_pre, out_grad, act_basis):
    tokens = hidden.shape[0]
    shape = (16, tokens, act_basis.shape[1] // 16)
    place = lax.axis_index(DP).astype(jnp.int32).reshape(1)
    return pl.pallas_call(
        first_kernel,
        out_shape=(pltpu.HBM(shape, jnp.bfloat16), pltpu.HBM(out_grad.shape, jnp.bfloat16)),
        in_specs=[SMEM, VMEM, ANY, ANY, ANY, ANY],
        out_specs=(ANY, ANY),
        scratch_shapes=[
            pltpu.VMEM(gate_pre.shape, jnp.bfloat16),
            pltpu.VMEM(out_grad.shape, jnp.bfloat16),
            pltpu.VMEM(hidden.shape, jnp.bfloat16),
            pltpu.VMEM(act_basis.shape, jnp.bfloat16),
            pltpu.VMEM(shape, jnp.bfloat16),
            pltpu.VMEM(out_grad.shape, jnp.bfloat16),
            pltpu.SemaphoreType.DMA((12,)),
        ],
        compiler_params=WHOLE,
        name="first",
    )(place, norm_gain.reshape(1, -1), gate_pre, out_grad, hidden, act_basis)


def grad_kernel(count, *refs):
    parts, basis, out_at, rows, out, sem = refs[:count], refs[count], *refs[-4:]
    at = 0
    for part in parts:
        rows[at : at + part.shape[0], :] = part[...]
        at += part.shape[0]
    stores = []
    for at in range(0, basis.shape[1], 256):
        here = pl.ds(at, 256)
        part = jnp.dot(rows[...], basis[:, here], preferred_element_type=jnp.float32)
        out[here, :] = part.T.astype(jnp.bfloat16)
        stores.append(
            pltpu.make_async_copy(out.at[here], out_at.at[here], sem.at[at // 256])
        )
        stores[-1].start()
    for store in stores:
        store.wait()


def grad_partials(parts, basis, after=(), cost=None):
    depth, columns = basis.shape
    tokens = sum(part.shape[0] for part in parts)
    shape = (columns, tokens)
    return pl.pallas_call(
        lambda *refs: grad_kernel(len(parts), *refs),
        out_shape=pltpu.HBM(shape, jnp.bfloat16),
        in_specs=[VMEM] * (len(parts) + 1) + [ANY] * len(after),
        out_specs=ANY,
        scratch_shapes=[
            pltpu.VMEM((tokens, depth), jnp.bfloat16),
            pltpu.VMEM(shape, jnp.bfloat16),
            pltpu.SemaphoreType.DMA((columns // 256,)),
        ],
        compiler_params=PARAMS,
        cost_estimate=cost,
        name="grad",
    )(*parts, basis, *after)


def act_sum_kernel(place, got, kept, given):
    total = got[0].astype(jnp.float32)
    for source in range(1, got.shape[0]):
        total += got[source].astype(jnp.float32)
    low, high = total[:, : kept.shape[1]], total[:, kept.shape[1] :]
    first = place[0] == 0
    kept[...] = jnp.where(first, low, high)
    given[...] = jnp.where(first, high, low)


def act_squares(partials):
    got = lax.all_to_all(partials, ("x", "y"), 0, 0, tiled=True)
    _, tokens, wide = got.shape
    half = jax.ShapeDtypeStruct((tokens, wide // 2), jnp.float32)
    place = lax.axis_index("z_hi").astype(jnp.int32).reshape(1)
    kept, given = pl.pallas_call(
        act_sum_kernel,
        out_shape=(half, half),
        in_specs=[SMEM, VMEM],
        out_specs=(VMEM, VMEM),
        compiler_params=PARAMS,
        cost_estimate=pl.CostEstimate(flops=2*10**10, bytes_accessed=10**6, transcendentals=0),
        name="act_sum",
    )(place, got)
    total = kept + shifted(given, "z_hi", 1)
    square = (total * total).astype(jnp.bfloat16)
    return [square] + [shifted(square, "x", step) for step in (1, 2, 3)]


def gate_kernel(*refs):
    del refs


def gated(value, after, place=pltpu.HBM):
    return pl.pallas_call(
        gate_kernel,
        out_shape=place(value.shape, value.dtype),
        in_specs=[ANY] * (1 + len(after)),
        out_specs=ANY,
        input_output_aliases={0: 0},
        compiler_params=PARAMS,
        name="gate",
    )(value, *after)


def exchanged(partial):
    columns, tokens = partial.shape
    return lax.all_to_all(partial.reshape(16, columns // 16, tokens), ("x", "y"), 0, 0, tiled=True)


def squared(got):
    summed = jnp.sum(got.astype(jnp.float32), axis=0)
    total = summed + shifted(summed.astype(jnp.bfloat16), "z_hi", 1).astype(jnp.float32)
    return (total * total).astype(jnp.bfloat16)


def correct_kernel(place, *refs):
    pieces, acts, before, (out, act) = refs[:4], refs[4:8], refs[8:-2], refs[-2:]
    _, tokens, block = acts[0].shape
    for i, part in enumerate(acts):
        for behind in range(4):
            here = slice(i * tokens, (i + 1) * tokens), slice(behind * block, (behind + 1) * block)
            act[here] = part[behind]
    rows = pieces[0].shape[0]
    for y_behind, piece in enumerate(pieces):
        part = jnp.dot(piece[...], act[...], preferred_element_type=jnp.float32)
        part = part * (1.0 / (8 * tokens))
        at = pl.ds(pl.multiple_of(lax.rem(place[1] + 4 - y_behind, 4) * rows, rows), rows)
        for behind in range(4):
            x = lax.rem(place[0] + 4 - behind, 4)
            here = part[:, behind * block : (behind + 1) * block]
            if before:
                here = before[0][x, at, :] + here
            out[x, at, :] = here


def corrected(pieces, acts, *before):
    rows, tokens = pieces[0].shape
    block = acts[0].shape[2]
    place = jnp.stack([lax.axis_index("x"), lax.axis_index("y")]).astype(jnp.int32)
    return pl.pallas_call(
        correct_kernel,
        out_shape=jax.ShapeDtypeStruct((4, 4 * rows, block), jnp.float32),
        in_specs=[SMEM] + [VMEM] * (8 + len(before)),
        out_specs=VMEM,
        scratch_shapes=[pltpu.VMEM((tokens, 4 * block), jnp.bfloat16)],
        compiler_params=PARAMS,
        name="correct",
    )(place, *pieces, *acts, *before)


def per_device(hidden, norm_gain, gate_pre, out_grad, grad_basis, act_basis):
    act_parts, up_grad = first_partials(hidden, norm_gain, gate_pre, out_grad, act_basis)
    near, far, farthest = [shifted(up_grad, "z_lo", step) for step in (1, 2, 3)]
    near_rows = [up_grad, shifted(up_grad, "core", 1), near, shifted(near, "core", 1)]
    far_rows = [far, shifted(far, "core", 1), farthest, shifted(farthest, "core", 1)]
    act_row = act_squares(act_parts)
    cost = pl.CostEstimate(flops=8*10**9, bytes_accessed=10**7, transcendentals=0)
    near_got = exchanged(grad_partials(near_rows, grad_basis, (), cost))
    far_got = exchanged(gated(grad_partials(far_rows, grad_basis), act_row))
    act_own = jnp.stack(act_row)
    acts = []
    for own in [act_own] + [shifted(act_own, "z_lo", step) for step in (1, 2, 3)]:
        acts += [own, shifted(own, "core", 1)]
    near_sq = squared(near_got)
    near_pieces = [near_sq] + [shifted(near_sq, "y", step) for step in (1, 2, 3)]
    far_sq = squared(gated(far_got, acts + [near_sq], jax.ShapeDtypeStruct))
    far_pieces = [far_sq] + [shifted(far_sq, "y", step) for step in (1, 2, 3)]
    out = corrected(far_pieces, acts[4:], corrected(near_pieces, acts[:4]))
    out = lax.all_to_all(out, "x", 0, 0, tiled=True)
    return out.reshape(grad_basis.shape[1], -1)


def solution(mesh):
    fine = Mesh(mesh.devices.reshape(SIZES), AXES)
    placed = (
        P(TENSOR, None),
        P(),
        P(TENSOR, DP),
        P(TENSOR, DP),
        P(DP, TENSOR),
        P(DP, None),
    )
    return jax.shard_map(
        per_device, mesh=fine, in_specs=placed, out_specs=P(TENSOR, DP), check_vma=False
    )
```

```python
import jax
import jax.numpy as jnp
from jax import lax
from jax.experimental import pallas as pl
from jax.experimental.pallas import tpu as pltpu
from jax.sharding import Mesh
from jax.sharding import PartitionSpec as P

AXES = ("z_hi", "x", "y", "z_lo", "core")
SIZES = (2, 4, 4, 4, 2)
DP = ("z_hi", "x", "y")
TENSOR = ("z_lo", "core")
SMEM = pl.BlockSpec(memory_space=pltpu.SMEM)
VMEM = pl.BlockSpec(memory_space=pltpu.VMEM)
ANY = pl.BlockSpec(memory_space=pl.ANY)
PARAMS = pltpu.CompilerParams(vmem_limit_bytes=32 * 1024 * 1024)
WHOLE = pltpu.CompilerParams(vmem_limit_bytes=60 * 1024 * 1024)


def shifted(value, axis, step):
    size = SIZES[AXES.index(axis)]
    return lax.ppermute(value, axis, [(i, (i + step) % size) for i in range(size)])


def first_kernel(place, gain, gate_at, grad_at, hidden_at, basis_at, out_at, up_at,
                 gate, grad, hidden, basis, out, up, sems):
    tokens, features = hidden.shape
    depth = basis.shape[0]
    strip = tokens // 2
    quarter = depth // 4
    loads = [
        pltpu.make_async_copy(hidden_at.at[here], hidden.at[here], sems.at[i])
        for i, here in enumerate(pl.ds(at, strip) for at in range(0, tokens, strip))
    ]
    basis_loads = [
        pltpu.make_async_copy(basis_at.at[here], basis.at[here], sems.at[2 + i])
        for i, here in enumerate(pl.ds(at, quarter) for at in range(0, depth, quarter))
    ]
    load_gate = pltpu.make_async_copy(gate_at, gate, sems.at[10])
    load_grad = pltpu.make_async_copy(grad_at, grad, sems.at[11])
    for load in (*loads, *basis_loads, load_gate, load_grad):
        load.start()
    stats = []
    for i, load in enumerate(loads):
        load.wait()
        squares = jnp.zeros((strip, 128), jnp.float32)
        for at in range(0, features, 128):
            wide = hidden[i * strip : (i + 1) * strip, at : at + 128].astype(jnp.float32)
            squares += wide * wide
        stats.append(jnp.sum(squares, axis=-1, keepdims=True) / features)
    stat = jnp.concatenate(stats, axis=0)
    mine = pl.ds(pl.multiple_of(place[0] * depth, depth), depth)
    scaled = hidden[:, mine].astype(jnp.float32) * lax.rsqrt(stat + 1e-05)
    normed = (scaled * gain[:, mine]).astype(jnp.bfloat16)
    for load in basis_loads:
        load.wait()
    block = basis.shape[1] // 32
    stores = []
    for x in range(4):
        for z_hi in range(2):
            at = (z_hi * 16 + x * 4) * block
            part = jnp.dot(
                normed, basis[:, at : at + 4 * block], preferred_element_type=jnp.float32
            )
            for y in range(4):
                here = part[:, y * block : (y + 1) * block]
                to = slice(z_hi * block, (z_hi + 1) * block)
                out[x * 4 + y, :, to] = here.astype(jnp.bfloat16)
        here = pl.ds(x * 4, 4)
        stores.append(pltpu.make_async_copy(out.at[here], out_at.at[here], sems.at[6 + x]))
        stores[-1].start()
    load_gate.wait()
    load_grad.wait()
    for at in range(0, tokens, 32):
        here = slice(at, at + 32)
        wide = gate[here, :].astype(jnp.float32)
        wide = grad[here, :].astype(jnp.float32) * (wide / (1.0 + jnp.exp(-wide)))
        up[here, :] = wide.astype(jnp.bfloat16)
    stores.append(pltpu.make_async_copy(up, up_at, sems.at[12]))
    stores[-1].start()
    for store in stores:
        store.wait()


def first_partials(hidden, norm_gain, gate_pre, out_grad, act_basis):
    tokens = hidden.shape[0]
    shape = (16, tokens, act_basis.shape[1] // 16)
    place = lax.axis_index(DP).astype(jnp.int32).reshape(1)
    return pl.pallas_call(
        first_kernel,
        out_shape=(pltpu.HBM(shape, jnp.bfloat16), pltpu.HBM(out_grad.shape, jnp.bfloat16)),
        in_specs=[SMEM, VMEM, ANY, ANY, ANY, ANY],
        out_specs=(ANY, ANY),
        scratch_shapes=[
            pltpu.VMEM(gate_pre.shape, jnp.bfloat16),
            pltpu.VMEM(out_grad.shape, jnp.bfloat16),
            pltpu.VMEM(hidden.shape, jnp.bfloat16),
            pltpu.VMEM(act_basis.shape, jnp.bfloat16),
            pltpu.VMEM(shape, jnp.bfloat16),
            pltpu.VMEM(out_grad.shape, jnp.bfloat16),
            pltpu.SemaphoreType.DMA((13,)),
        ],
        compiler_params=WHOLE,
        name="first",
    )(place, norm_gain.reshape(1, -1), gate_pre, out_grad, hidden, act_basis)


def grad_kernel(count, *refs):
    parts, basis, out_at, rows, out, sem = refs[:count], refs[count], *refs[-4:]
    at = 0
    for part in parts:
        rows[at : at + part.shape[0], :] = part[...]
        at += part.shape[0]
    stores = []
    for at in range(0, basis.shape[1], 256):
        here = pl.ds(at, 256)
        part = jnp.dot(rows[...], basis[:, here], preferred_element_type=jnp.float32)
        out[here, :] = part.T.astype(jnp.bfloat16)
        stores.append(
            pltpu.make_async_copy(out.at[here], out_at.at[here], sem.at[at // 256])
        )
        stores[-1].start()
    for store in stores:
        store.wait()


def grad_partials(parts, basis, after=(), cost=None):
    depth, columns = basis.shape
    tokens = sum(part.shape[0] for part in parts)
    shape = (columns, tokens)
    return pl.pallas_call(
        lambda *refs: grad_kernel(len(parts), *refs),
        out_shape=pltpu.HBM(shape, jnp.bfloat16),
        in_specs=[VMEM] * (len(parts) + 1) + [ANY] * len(after),
        out_specs=ANY,
        scratch_shapes=[
            pltpu.VMEM((tokens, depth), jnp.bfloat16),
            pltpu.VMEM(shape, jnp.bfloat16),
            pltpu.SemaphoreType.DMA((columns // 256,)),
        ],
        compiler_params=PARAMS,
        cost_estimate=cost,
        name="grad",
    )(*parts, basis, *after)


def act_sum_kernel(place, got, kept, given):
    total = got[0].astype(jnp.float32)
    for source in range(1, got.shape[0]):
        total += got[source].astype(jnp.float32)
    low, high = total[:, : kept.shape[1]], total[:, kept.shape[1] :]
    first = place[0] == 0
    kept[...] = jnp.where(first, low, high)
    given[...] = jnp.where(first, high, low)


def act_squares(partials):
    got = lax.all_to_all(partials, ("x", "y"), 0, 0, tiled=True)
    _, tokens, wide = got.shape
    half = jax.ShapeDtypeStruct((tokens, wide // 2), jnp.float32)
    place = lax.axis_index("z_hi").astype(jnp.int32).reshape(1)
    kept, given = pl.pallas_call(
        act_sum_kernel,
        out_shape=(half, half),
        in_specs=[SMEM, VMEM],
        out_specs=(VMEM, VMEM),
        compiler_params=PARAMS,
        cost_estimate=pl.CostEstimate(flops=2 * 10**10, bytes_accessed=10**6, transcendentals=0),
        name="act_sum",
    )(place, got)
    total = kept + shifted(given, "z_hi", 1)
    square = (total * total).astype(jnp.bfloat16)
    return [square] + [shifted(square, "x", step) for step in (1, 2, 3)]


def gate_kernel(*refs):
    del refs


def gated(value, after, place=pltpu.HBM):
    return pl.pallas_call(
        gate_kernel,
        out_shape=place(value.shape, value.dtype),
        in_specs=[ANY] * (1 + len(after)),
        out_specs=ANY,
        input_output_aliases={0: 0},
        compiler_params=PARAMS,
        name="gate",
    )(value, *after)


def exchanged(partial):
    columns, tokens = partial.shape
    return lax.all_to_all(partial.reshape(16, columns // 16, tokens), ("x", "y"), 0, 0, tiled=True)


def squared(got):
    summed = jnp.sum(got.astype(jnp.float32), axis=0)
    total = summed + shifted(summed.astype(jnp.bfloat16), "z_hi", 1).astype(jnp.float32)
    return (total * total).astype(jnp.bfloat16)


def correct_kernel(place, *refs):
    pieces, acts, before, (out, act) = refs[:4], refs[4:8], refs[8:-2], refs[-2:]
    _, tokens, block = acts[0].shape
    for i, part in enumerate(acts):
        for behind in range(4):
            here = slice(i * tokens, (i + 1) * tokens), slice(behind * block, (behind + 1) * block)
            act[here] = part[behind]
    rows = pieces[0].shape[0]
    for y_behind, piece in enumerate(pieces):
        part = jnp.dot(piece[...], act[...], preferred_element_type=jnp.float32)
        part = part * (1.0 / (8 * tokens))
        at = pl.ds(pl.multiple_of(lax.rem(place[1] + 4 - y_behind, 4) * rows, rows), rows)
        for behind in range(4):
            x = lax.rem(place[0] + 4 - behind, 4)
            here = part[:, behind * block : (behind + 1) * block]
            if before:
                here = before[0][x, at, :] + here
            out[x, at, :] = here


def corrected(pieces, acts, *before):
    rows, tokens = pieces[0].shape
    block = acts[0].shape[2]
    place = jnp.stack([lax.axis_index("x"), lax.axis_index("y")]).astype(jnp.int32)
    return pl.pallas_call(
        correct_kernel,
        out_shape=jax.ShapeDtypeStruct((4, 4 * rows, block), jnp.float32),
        in_specs=[SMEM] + [VMEM] * (8 + len(before)),
        out_specs=VMEM,
        scratch_shapes=[pltpu.VMEM((tokens, 4 * block), jnp.bfloat16)],
        compiler_params=PARAMS,
        name="correct",
    )(place, *pieces, *acts, *before)


def per_device(hidden, norm_gain, gate_pre, out_grad, grad_basis, act_basis):
    act_parts, up_grad = first_partials(hidden, norm_gain, gate_pre, out_grad, act_basis)
    near, far, farthest = [shifted(up_grad, "z_lo", step) for step in (1, 2, 3)]
    near_rows = [up_grad, shifted(up_grad, "core", 1), near, shifted(near, "core", 1)]
    far_rows = [far, shifted(far, "core", 1), farthest, shifted(farthest, "core", 1)]
    act_row = act_squares(act_parts)
    cost = pl.CostEstimate(flops=8 * 10**9, bytes_accessed=10**7, transcendentals=0)
    near_got = exchanged(grad_partials(near_rows, grad_basis, (), cost))
    act_own = jnp.stack(act_row)
    far_got = exchanged(gated(grad_partials(far_rows, grad_basis), [act_own]))
    acts = []
    for own in [act_own] + [shifted(act_own, "z_lo", step) for step in (1, 2, 3)]:
        acts += [own, shifted(own, "core", 1)]
    near_sq = squared(near_got)
    near_pieces = [near_sq] + [shifted(near_sq, "y", step) for step in (1, 2, 3)]
    far_sq = squared(gated(far_got, acts + [near_sq], jax.ShapeDtypeStruct))
    far_pieces = [far_sq] + [shifted(far_sq, "y", step) for step in (1, 2, 3)]
    out = corrected(far_pieces, acts[4:], corrected(near_pieces, acts[:4]))
    out = lax.all_to_all(out, "x", 0, 0, tiled=True)
    return out.reshape(grad_basis.shape[1], -1)


def solution(mesh):
    fine = Mesh(mesh.devices.reshape(SIZES), AXES)
    placed = (
        P(TENSOR, None),
        P(),
        P(TENSOR, DP),
        P(TENSOR, DP),
        P(DP, TENSOR),
        P(DP, None),
    )
    return jax.shard_map(
        per_device, mesh=fine, in_specs=placed, out_specs=P(TENSOR, DP), check_vma=False
    )
```

```python
import jax
import jax.numpy as jnp
from jax import lax
from jax.experimental import pallas as pl
from jax.experimental.pallas import tpu as pltpu
from jax.sharding import Mesh
from jax.sharding import PartitionSpec as P

AXES = ("z_hi", "x", "y", "z_lo", "core")
SIZES = (2, 4, 4, 4, 2)
DP = ("z_hi", "x", "y")
TENSOR = ("z_lo", "core")
Y_STEPS = (2, 1, 3)
SMEM = pl.BlockSpec(memory_space=pltpu.SMEM)
VMEM = pl.BlockSpec(memory_space=pltpu.VMEM)
ANY = pl.BlockSpec(memory_space=pl.ANY)
PARAMS = pltpu.CompilerParams(vmem_limit_bytes=32 * 1024 * 1024)
WHOLE = pltpu.CompilerParams(vmem_limit_bytes=60 * 1024 * 1024)


def shifted(value, axis, step):
    size = SIZES[AXES.index(axis)]
    return lax.ppermute(value, axis, [(i, (i + step) % size) for i in range(size)])


def first_kernel(place, gain, gate_at, grad_at, hidden_at, basis_at, out_at, up_at,
                 gate, grad, hidden, basis, out, up, sems):
    tokens, features = hidden.shape
    depth = basis.shape[0]
    strip = tokens // 2
    quarter = depth // 4
    loads = [
        pltpu.make_async_copy(hidden_at.at[here], hidden.at[here], sems.at[i])
        for i, here in enumerate(pl.ds(at, strip) for at in range(0, tokens, strip))
    ]
    basis_loads = [
        pltpu.make_async_copy(basis_at.at[here], basis.at[here], sems.at[2 + i])
        for i, here in enumerate(pl.ds(at, quarter) for at in range(0, depth, quarter))
    ]
    load_gate = pltpu.make_async_copy(gate_at, gate, sems.at[10])
    load_grad = pltpu.make_async_copy(grad_at, grad, sems.at[11])
    for load in (*loads, *basis_loads, load_gate, load_grad):
        load.start()
    stats = []
    for i, load in enumerate(loads):
        load.wait()
        squares = jnp.zeros((strip, 128), jnp.float32)
        for at in range(0, features, 128):
            wide = hidden[i * strip : (i + 1) * strip, at : at + 128].astype(jnp.float32)
            squares += wide * wide
        stats.append(jnp.sum(squares, axis=-1, keepdims=True) / features)
    stat = jnp.concatenate(stats, axis=0)
    mine = pl.ds(pl.multiple_of(place[0] * depth, depth), depth)
    scaled = hidden[:, mine].astype(jnp.float32) * lax.rsqrt(stat + 1e-05)
    normed = (scaled * gain[:, mine]).astype(jnp.bfloat16)
    for load in basis_loads:
        load.wait()
    block = basis.shape[1] // 32
    stores = []
    for x in range(4):
        for z_hi in range(2):
            at = (z_hi * 16 + x * 4) * block
            part = jnp.dot(
                normed, basis[:, at : at + 4 * block], preferred_element_type=jnp.float32
            )
            for y in range(4):
                here = part[:, y * block : (y + 1) * block]
                to = slice(z_hi * block, (z_hi + 1) * block)
                out[x * 4 + y, :, to] = here.astype(jnp.bfloat16)
        here = pl.ds(x * 4, 4)
        stores.append(pltpu.make_async_copy(out.at[here], out_at.at[here], sems.at[6 + x]))
        stores[-1].start()
    load_gate.wait()
    load_grad.wait()
    for at in range(0, tokens, 32):
        here = slice(at, at + 32)
        wide = gate[here, :].astype(jnp.float32)
        wide = grad[here, :].astype(jnp.float32) * (wide / (1.0 + jnp.exp(-wide)))
        up[here, :] = wide.astype(jnp.bfloat16)
    stores.append(pltpu.make_async_copy(up, up_at, sems.at[12]))
    stores[-1].start()
    for store in stores:
        store.wait()


def first_partials(hidden, norm_gain, gate_pre, out_grad, act_basis):
    tokens = hidden.shape[0]
    shape = (16, tokens, act_basis.shape[1] // 16)
    place = lax.axis_index(DP).astype(jnp.int32).reshape(1)
    return pl.pallas_call(
        first_kernel,
        out_shape=(pltpu.HBM(shape, jnp.bfloat16), pltpu.HBM(out_grad.shape, jnp.bfloat16)),
        in_specs=[SMEM, VMEM, ANY, ANY, ANY, ANY],
        out_specs=(ANY, ANY),
        scratch_shapes=[
            pltpu.VMEM(gate_pre.shape, jnp.bfloat16),
            pltpu.VMEM(out_grad.shape, jnp.bfloat16),
            pltpu.VMEM(hidden.shape, jnp.bfloat16),
            pltpu.VMEM(act_basis.shape, jnp.bfloat16),
            pltpu.VMEM(shape, jnp.bfloat16),
            pltpu.VMEM(out_grad.shape, jnp.bfloat16),
            pltpu.SemaphoreType.DMA((13,)),
        ],
        compiler_params=WHOLE,
        name="first",
    )(place, norm_gain.reshape(1, -1), gate_pre, out_grad, hidden, act_basis)


def grad_kernel(count, *refs):
    parts, basis, out_at, rows, out, sem = refs[:count], refs[count], *refs[-4:]
    at = 0
    for part in parts:
        rows[at : at + part.shape[0], :] = part[...]
        at += part.shape[0]
    stores = []
    for at in range(0, basis.shape[1], 256):
        here = pl.ds(at, 256)
        part = jnp.dot(rows[...], basis[:, here], preferred_element_type=jnp.float32)
        out[here, :] = part.T.astype(jnp.bfloat16)
        stores.append(
            pltpu.make_async_copy(out.at[here], out_at.at[here], sem.at[at // 256])
        )
        stores[-1].start()
    for store in stores:
        store.wait()


def grad_partials(parts, basis, after=(), cost=None):
    depth, columns = basis.shape
    tokens = sum(part.shape[0] for part in parts)
    shape = (columns, tokens)
    return pl.pallas_call(
        lambda *refs: grad_kernel(len(parts), *refs),
        out_shape=pltpu.HBM(shape, jnp.bfloat16),
        in_specs=[VMEM] * (len(parts) + 1) + [ANY] * len(after),
        out_specs=ANY,
        scratch_shapes=[
            pltpu.VMEM((tokens, depth), jnp.bfloat16),
            pltpu.VMEM(shape, jnp.bfloat16),
            pltpu.SemaphoreType.DMA((columns // 256,)),
        ],
        compiler_params=PARAMS,
        cost_estimate=cost,
        name="grad",
    )(*parts, basis, *after)


def act_sum_kernel(place, got, kept, given):
    total = got[0].astype(jnp.float32)
    for source in range(1, got.shape[0]):
        total += got[source].astype(jnp.float32)
    low, high = total[:, : kept.shape[1]], total[:, kept.shape[1] :]
    first = place[0] == 0
    kept[...] = jnp.where(first, low, high)
    given[...] = jnp.where(first, high, low)


def act_squares(partials):
    got = lax.all_to_all(partials, ("x", "y"), 0, 0, tiled=True)
    _, tokens, wide = got.shape
    half = jax.ShapeDtypeStruct((tokens, wide // 2), jnp.float32)
    place = lax.axis_index("z_hi").astype(jnp.int32).reshape(1)
    kept, given = pl.pallas_call(
        act_sum_kernel,
        out_shape=(half, half),
        in_specs=[SMEM, VMEM],
        out_specs=(VMEM, VMEM),
        compiler_params=PARAMS,
        cost_estimate=pl.CostEstimate(flops=2 * 10**10, bytes_accessed=10**6, transcendentals=0),
        name="act_sum",
    )(place, got)
    total = kept + shifted(given, "z_hi", 1)
    square = (total * total).astype(jnp.bfloat16)
    return [square] + [shifted(square, "x", step) for step in (1, 2, 3)]


def gate_kernel(*refs):
    del refs


def gated(value, after, place=pltpu.HBM):
    return pl.pallas_call(
        gate_kernel,
        out_shape=place(value.shape, value.dtype),
        in_specs=[ANY] * (1 + len(after)),
        out_specs=ANY,
        input_output_aliases={0: 0},
        compiler_params=PARAMS,
        name="gate",
    )(value, *after)


def exchanged(partial):
    columns, tokens = partial.shape
    return lax.all_to_all(partial.reshape(16, columns // 16, tokens), ("x", "y"), 0, 0, tiled=True)


def squared(got):
    summed = jnp.sum(got.astype(jnp.float32), axis=0)
    total = summed + shifted(summed.astype(jnp.bfloat16), "z_hi", 1).astype(jnp.float32)
    return (total * total).astype(jnp.bfloat16)


def correct_kernel(place, *refs):
    pieces, acts, before, (out, act, both) = refs[:4], refs[4:8], refs[8:-3], refs[-3:]
    _, tokens, block = acts[0].shape
    for i, part in enumerate(acts):
        for behind in range(4):
            here = slice(i * tokens, (i + 1) * tokens), slice(behind * block, (behind + 1) * block)
            act[here] = part[behind]
    rows = pieces[0].shape[0]
    for i, piece in enumerate(pieces):
        both[i * rows : (i + 1) * rows, :] = piece[...]
    every = jnp.dot(both[...], act[...], preferred_element_type=jnp.float32)
    every = every * (1.0 / (8 * tokens))
    for i, y_behind in enumerate((0, *Y_STEPS)):
        at = pl.ds(pl.multiple_of(lax.rem(place[1] + 4 - y_behind, 4) * rows, rows), rows)
        for behind in range(4):
            x = lax.rem(place[0] + 4 - behind, 4)
            here = every[i * rows : (i + 1) * rows, behind * block : (behind + 1) * block]
            if before:
                here = before[0][x, at, :] + here
            out[x, at, :] = here


def corrected(pieces, acts, *before):
    rows, tokens = pieces[0].shape
    block = acts[0].shape[2]
    place = jnp.stack([lax.axis_index("x"), lax.axis_index("y")]).astype(jnp.int32)
    return pl.pallas_call(
        correct_kernel,
        out_shape=jax.ShapeDtypeStruct((4, 4 * rows, block), jnp.float32),
        in_specs=[SMEM] + [VMEM] * (8 + len(before)),
        out_specs=VMEM,
        scratch_shapes=[
            pltpu.VMEM((tokens, 4 * block), jnp.bfloat16),
            pltpu.VMEM((4 * rows, tokens), jnp.bfloat16),
        ],
        compiler_params=PARAMS,
        name="correct",
    )(place, *pieces, *acts, *before)


def per_device(hidden, norm_gain, gate_pre, out_grad, grad_basis, act_basis):
    act_parts, up_grad = first_partials(hidden, norm_gain, gate_pre, out_grad, act_basis)
    near, far, farthest = [shifted(up_grad, "z_lo", step) for step in (1, 2, 3)]
    near_rows = [up_grad, shifted(up_grad, "core", 1), near, shifted(near, "core", 1)]
    far_rows = [far, shifted(far, "core", 1), farthest, shifted(farthest, "core", 1)]
    act_row = act_squares(act_parts)
    cost = pl.CostEstimate(flops=8 * 10**9, bytes_accessed=10**7, transcendentals=0)
    near_got = exchanged(grad_partials(near_rows, grad_basis, (), cost))
    act_own = jnp.stack(act_row)
    far_got = exchanged(gated(grad_partials(far_rows, grad_basis), [act_own]))
    acts = []
    for own in [act_own] + [shifted(act_own, "z_lo", step) for step in (1, 2, 3)]:
        acts += [own, shifted(own, "core", 1)]
    near_sq = squared(near_got)
    near_pieces = [near_sq] + [shifted(near_sq, "y", step) for step in Y_STEPS]
    far_sq = squared(gated(far_got, acts + [near_sq], jax.ShapeDtypeStruct))
    far_pieces = [far_sq] + [shifted(far_sq, "y", step) for step in Y_STEPS]
    out = corrected(far_pieces, acts[4:], corrected(near_pieces, acts[:4]))
    out = lax.all_to_all(out, "x", 0, 0, tiled=True)
    return out.reshape(grad_basis.shape[1], -1)


def solution(mesh):
    fine = Mesh(mesh.devices.reshape(SIZES), AXES)
    placed = (
        P(TENSOR, None),
        P(),
        P(TENSOR, DP),
        P(TENSOR, DP),
        P(DP, TENSOR),
        P(DP, None),
    )
    return jax.shard_map(
        per_device, mesh=fine, in_specs=placed, out_specs=P(TENSOR, DP), check_vma=False
    )
```

```python
import jax
import jax.numpy as jnp
from jax import lax
from jax.experimental import pallas as pl
from jax.experimental.pallas import tpu as pltpu
from jax.sharding import Mesh
from jax.sharding import PartitionSpec as P

AXES = ("z_hi", "x", "y", "z_lo", "core")
SIZES = (2, 4, 4, 4, 2)
DP = ("z_hi", "x", "y")
TENSOR = ("z_lo", "core")
ROW_STEPS = (2, 1, 3)
SMEM = pl.BlockSpec(memory_space=pltpu.SMEM)
VMEM = pl.BlockSpec(memory_space=pltpu.VMEM)
ANY = pl.BlockSpec(memory_space=pl.ANY)
PARAMS = pltpu.CompilerParams(vmem_limit_bytes=32 * 1024 * 1024)
WHOLE = pltpu.CompilerParams(vmem_limit_bytes=60 * 1024 * 1024)


def shifted(value, axis, step):
    size = SIZES[AXES.index(axis)]
    return lax.ppermute(value, axis, [(i, (i + step) % size) for i in range(size)])


def shifted_by_core(value, axis, step):
    pairs = []
    for x in range(4):
        for y in range(4):
            for core in range(2):
                along_x = (axis == "x") == (core == 0)
                to_x, to_y = ((x + step) % 4, y) if along_x else (x, (y + step) % 4)
                pairs.append((x * 8 + y * 2 + core, to_x * 8 + to_y * 2 + core))
    return lax.ppermute(value, ("x", "y", "core"), pairs)


def swapped_by_core(value):
    groups = [[x * 8 + y * 2 for x in range(4)] for y in range(4)]
    groups += [[x * 8 + y * 2 + 1 for y in range(4)] for x in range(4)]
    return lax.all_to_all(
        value, ("x", "y", "core"), 0, 0, tiled=True, axis_index_groups=groups
    )


def first_kernel(place, gain, gate_at, grad_at, hidden_at, basis_at, out_at, up_at,
                 gate, grad, hidden, basis, out, up, sems):
    tokens, features = hidden.shape
    depth = basis.shape[0]
    strip = tokens // 2
    quarter = depth // 4
    loads = [
        pltpu.make_async_copy(hidden_at.at[here], hidden.at[here], sems.at[i])
        for i, here in enumerate(pl.ds(at, strip) for at in range(0, tokens, strip))
    ]
    basis_loads = [
        pltpu.make_async_copy(basis_at.at[here], basis.at[here], sems.at[2 + i])
        for i, here in enumerate(pl.ds(at, quarter) for at in range(0, depth, quarter))
    ]
    load_gate = pltpu.make_async_copy(gate_at, gate, sems.at[10])
    load_grad = pltpu.make_async_copy(grad_at, grad, sems.at[11])
    for load in (*loads, *basis_loads, load_gate, load_grad):
        load.start()
    stats = []
    for i, load in enumerate(loads):
        load.wait()
        squares = jnp.zeros((strip, 128), jnp.float32)
        for at in range(0, features, 128):
            wide = hidden[i * strip : (i + 1) * strip, at : at + 128].astype(jnp.float32)
            squares += wide * wide
        stats.append(jnp.sum(squares, axis=-1, keepdims=True) / features)
    stat = jnp.concatenate(stats, axis=0)
    mine = pl.ds(pl.multiple_of(place[0] * depth, depth), depth)
    scaled = hidden[:, mine].astype(jnp.float32) * lax.rsqrt(stat + 1e-05)
    normed = (scaled * gain[:, mine]).astype(jnp.bfloat16)
    for load in basis_loads:
        load.wait()
    block = basis.shape[1] // 32
    stores = []
    for x in range(4):
        for z_hi in range(2):
            at = (z_hi * 16 + x * 4) * block
            part = jnp.dot(
                normed, basis[:, at : at + 4 * block], preferred_element_type=jnp.float32
            )
            for y in range(4):
                here = part[:, y * block : (y + 1) * block]
                to = slice(z_hi * block, (z_hi + 1) * block)
                out[x * 4 + y, :, to] = here.astype(jnp.bfloat16)
        here = pl.ds(x * 4, 4)
        stores.append(pltpu.make_async_copy(out.at[here], out_at.at[here], sems.at[6 + x]))
        stores[-1].start()
    load_gate.wait()
    load_grad.wait()
    for at in range(0, tokens, 32):
        here = slice(at, at + 32)
        wide = gate[here, :].astype(jnp.float32)
        wide = grad[here, :].astype(jnp.float32) * (wide / (1.0 + jnp.exp(-wide)))
        up[here, :] = wide.astype(jnp.bfloat16)
    stores.append(pltpu.make_async_copy(up, up_at, sems.at[12]))
    stores[-1].start()
    for store in stores:
        store.wait()


def first_partials(hidden, norm_gain, gate_pre, out_grad, act_basis):
    tokens = hidden.shape[0]
    shape = (16, tokens, act_basis.shape[1] // 16)
    place = lax.axis_index(DP).astype(jnp.int32).reshape(1)
    return pl.pallas_call(
        first_kernel,
        out_shape=(pltpu.HBM(shape, jnp.bfloat16), pltpu.HBM(out_grad.shape, jnp.bfloat16)),
        in_specs=[SMEM, VMEM, ANY, ANY, ANY, ANY],
        out_specs=(ANY, ANY),
        scratch_shapes=[
            pltpu.VMEM(gate_pre.shape, jnp.bfloat16),
            pltpu.VMEM(out_grad.shape, jnp.bfloat16),
            pltpu.VMEM(hidden.shape, jnp.bfloat16),
            pltpu.VMEM(act_basis.shape, jnp.bfloat16),
            pltpu.VMEM(shape, jnp.bfloat16),
            pltpu.VMEM(out_grad.shape, jnp.bfloat16),
            pltpu.SemaphoreType.DMA((13,)),
        ],
        compiler_params=WHOLE,
        name="first",
    )(place, norm_gain.reshape(1, -1), gate_pre, out_grad, hidden, act_basis)


def grad_kernel(count, *refs):
    parts, basis, out_at, rows, out, sem = refs[:count], refs[count], *refs[-4:]
    at = 0
    for part in parts:
        rows[at : at + part.shape[0], :] = part[...]
        at += part.shape[0]
    stores = []
    for at in range(0, basis.shape[1], 256):
        here = pl.ds(at, 256)
        part = jnp.dot(rows[...], basis[:, here], preferred_element_type=jnp.float32)
        out[here, :] = part.T.astype(jnp.bfloat16)
        stores.append(
            pltpu.make_async_copy(out.at[here], out_at.at[here], sem.at[at // 256])
        )
        stores[-1].start()
    for store in stores:
        store.wait()


def grad_partials(parts, basis, after=(), cost=None):
    depth, columns = basis.shape
    tokens = sum(part.shape[0] for part in parts)
    shape = (columns, tokens)
    return pl.pallas_call(
        lambda *refs: grad_kernel(len(parts), *refs),
        out_shape=pltpu.HBM(shape, jnp.bfloat16),
        in_specs=[VMEM] * (len(parts) + 1) + [ANY] * len(after),
        out_specs=ANY,
        scratch_shapes=[
            pltpu.VMEM((tokens, depth), jnp.bfloat16),
            pltpu.VMEM(shape, jnp.bfloat16),
            pltpu.SemaphoreType.DMA((columns // 256,)),
        ],
        compiler_params=PARAMS,
        cost_estimate=cost,
        name="grad",
    )(*parts, basis, *after)


def act_sum_kernel(place, got, kept, given):
    total = got[0].astype(jnp.float32)
    for source in range(1, got.shape[0]):
        total += got[source].astype(jnp.float32)
    low, high = total[:, : kept.shape[1]], total[:, kept.shape[1] :]
    first = place[0] == 0
    kept[...] = jnp.where(first, low, high)
    given[...] = jnp.where(first, high, low)


def act_squares(partials):
    got = lax.all_to_all(partials, ("x", "y"), 0, 0, tiled=True)
    _, tokens, wide = got.shape
    half = jax.ShapeDtypeStruct((tokens, wide // 2), jnp.float32)
    place = lax.axis_index("z_hi").astype(jnp.int32).reshape(1)
    kept, given = pl.pallas_call(
        act_sum_kernel,
        out_shape=(half, half),
        in_specs=[SMEM, VMEM],
        out_specs=(VMEM, VMEM),
        compiler_params=PARAMS,
        cost_estimate=pl.CostEstimate(flops=2 * 10**10, bytes_accessed=10**6, transcendentals=0),
        name="act_sum",
    )(place, got)
    total = kept + shifted(given, "z_hi", 1)
    square = (total * total).astype(jnp.bfloat16)
    return square


def gate_kernel(*refs):
    del refs


def gated(value, after, place=pltpu.HBM):
    return pl.pallas_call(
        gate_kernel,
        out_shape=place(value.shape, value.dtype),
        in_specs=[ANY] * (1 + len(after)),
        out_specs=ANY,
        input_output_aliases={0: 0},
        compiler_params=PARAMS,
        name="gate",
    )(value, *after)


def exchanged(partial):
    columns, tokens = partial.shape
    return lax.all_to_all(partial.reshape(16, columns // 16, tokens), ("x", "y"), 0, 0, tiled=True)


def doubled(summed):
    total = summed + shifted(summed.astype(jnp.bfloat16), "z_hi", 1).astype(jnp.float32)
    return (total * total).astype(jnp.bfloat16)


def squared(got):
    return doubled(jnp.sum(got.astype(jnp.float32), axis=0))


def correct_kernel(steps, place, *refs):
    pieces, acts, before, (out, act, both) = refs[:4], refs[4:8], refs[8:-3], refs[-3:]
    chips, cores, tokens, block = acts[0].shape
    for behind, part in enumerate(acts):
        to = slice(behind * block, (behind + 1) * block)
        for i, step in enumerate(steps):
            for core in range(cores):
                at = (i * cores + core) * tokens
                act[at : at + tokens, to] = part[step, core]
    rows = pieces[0].shape[0]
    for i, piece in enumerate(pieces):
        both[i * rows : (i + 1) * rows, :] = piece[...]
    every = jnp.dot(both[...], act[...], preferred_element_type=jnp.float32)
    every = every * (1.0 / (chips * cores * tokens))
    for i, row_behind in enumerate((0, *ROW_STEPS)):
        at = pl.ds(pl.multiple_of(lax.rem(place[1] + 4 - row_behind, 4) * rows, rows), rows)
        for behind in range(4):
            owner = lax.rem(place[0] + 4 - behind, 4)
            here = every[i * rows : (i + 1) * rows, behind * block : (behind + 1) * block]
            if before:
                here = before[0][owner, at, :] + here
            out[owner, at, :] = here


def spread(grad_sq):
    return [grad_sq] + [shifted_by_core(grad_sq, "y", step) for step in ROW_STEPS]


def corrected(steps, place, pieces, acts, *before):
    rows, tokens = pieces[0].shape
    block = acts[0].shape[3]
    return pl.pallas_call(
        lambda *refs: correct_kernel(steps, *refs),
        out_shape=jax.ShapeDtypeStruct((4, 4 * rows, block), jnp.float32),
        in_specs=[SMEM] + [VMEM] * (8 + len(before)),
        out_specs=VMEM,
        scratch_shapes=[
            pltpu.VMEM((tokens, 4 * block), jnp.bfloat16),
            pltpu.VMEM((4 * rows, tokens), jnp.bfloat16),
        ],
        compiler_params=PARAMS,
        name="correct",
    )(place, *pieces, *acts, *before)


def order_kernel(place, got, out, sems):
    rows = got.shape[1] // 4
    copies = []
    for sender in range(4):
        for piece in range(4):
            to = jnp.where(place[2] == 0, sender * 4 + piece, piece * 4 + sender) * rows
            copies.append(
                pltpu.make_async_copy(
                    got.at[sender, pl.ds(piece * rows, rows)],
                    out.at[pl.ds(pl.multiple_of(to, rows), rows)],
                    sems.at[sender * 4 + piece],
                )
            )
            copies[-1].start()
    for copy in copies:
        copy.wait()


def ordered(place, got):
    return pl.pallas_call(
        order_kernel,
        out_shape=jax.ShapeDtypeStruct((4 * got.shape[1], got.shape[2]), got.dtype),
        in_specs=[SMEM, ANY],
        out_specs=ANY,
        scratch_shapes=[pltpu.SemaphoreType.DMA((16,))],
        compiler_params=PARAMS,
        name="order",
    )(place, got)


def per_device(hidden, norm_gain, gate_pre, out_grad, grad_basis, act_basis):
    x, y, core = [lax.axis_index(axis) for axis in ("x", "y", "core")]
    on_first = core == 0
    place = jnp.stack([jnp.where(on_first, x, y), jnp.where(on_first, y, x), core])
    place = place.astype(jnp.int32)
    act_parts, up_grad = first_partials(hidden, norm_gain, gate_pre, out_grad, act_basis)
    near, far, farthest = [shifted(up_grad, "z_lo", step) for step in (1, 2, 3)]
    near_rows = [up_grad, shifted(up_grad, "core", 1), near, shifted(near, "core", 1)]
    far_rows = [far, shifted(far, "core", 1), farthest, shifted(farthest, "core", 1)]
    act_own = act_squares(act_parts)
    cost = pl.CostEstimate(flops=8 * 10**9, bytes_accessed=10**7, transcendentals=0)
    near_got = exchanged(grad_partials(near_rows, grad_basis, (), cost))
    act_chip = jnp.stack([act_own, shifted(act_own, "core", 1)])
    act_all = jnp.stack(
        [act_chip] + [shifted(act_chip, "z_lo", step) for step in (1, 2, 3)]
    )
    far_got = exchanged(gated(grad_partials(far_rows, grad_basis), [act_all]))
    near_sq = squared(near_got)
    far_got = gated(far_got, [near_sq], jax.ShapeDtypeStruct)
    far_sum = jnp.sum(far_got.astype(jnp.float32), axis=0)
    far_sq = doubled(far_sum)
    act_all = gated(act_all, [far_sum], jax.ShapeDtypeStruct)
    acts = [act_all] + [shifted_by_core(act_all, "x", step) for step in (1, 2, 3)]
    out = corrected((0, 1), place, spread(near_sq), acts)
    out = corrected((2, 3), place, spread(far_sq), acts, out)
    return ordered(place, swapped_by_core(out))


def solution(mesh):
    fine = Mesh(mesh.devices.reshape(SIZES), AXES)
    placed = (
        P(TENSOR, None),
        P(),
        P(TENSOR, DP),
        P(TENSOR, DP),
        P(DP, TENSOR),
        P(DP, None),
    )
    return jax.shard_map(
        per_device, mesh=fine, in_specs=placed, out_specs=P(TENSOR, DP), check_vma=False
    )
```

```python
import jax
import jax.numpy as jnp
from jax import lax
from jax.experimental import pallas as pl
from jax.experimental.pallas import tpu as pltpu
from jax.sharding import Mesh
from jax.sharding import PartitionSpec as P

AXES = ("z_hi", "x", "y", "z_lo", "core")
SIZES = (2, 4, 4, 4, 2)
DP = ("z_hi", "x", "y")
TENSOR = ("z_lo", "core")
Y_STEPS = (2, 1, 3)
SMEM = pl.BlockSpec(memory_space=pltpu.SMEM)
VMEM = pl.BlockSpec(memory_space=pltpu.VMEM)
ANY = pl.BlockSpec(memory_space=pl.ANY)
PARAMS = pltpu.CompilerParams(vmem_limit_bytes=32 * 1024 * 1024)
WHOLE = pltpu.CompilerParams(vmem_limit_bytes=60 * 1024 * 1024)


def shifted(value, axis, step):
    size = SIZES[AXES.index(axis)]
    return lax.ppermute(value, axis, [(i, (i + step) % size) for i in range(size)])


def first_kernel(place, gain, gate_at, grad_at, hidden_at, basis_at, out_at, up_at,
                 gate, grad, hidden, basis, out, up, sems):
    tokens, features = hidden.shape
    depth = basis.shape[0]
    strip = tokens // 2
    quarter = depth // 4
    loads = [
        pltpu.make_async_copy(hidden_at.at[here], hidden.at[here], sems.at[i])
        for i, here in enumerate(pl.ds(at, strip) for at in range(0, tokens, strip))
    ]
    basis_loads = [
        pltpu.make_async_copy(basis_at.at[here], basis.at[here], sems.at[2 + i])
        for i, here in enumerate(pl.ds(at, quarter) for at in range(0, depth, quarter))
    ]
    load_gate = pltpu.make_async_copy(gate_at, gate, sems.at[10])
    load_grad = pltpu.make_async_copy(grad_at, grad, sems.at[11])
    for load in (*loads, *basis_loads, load_gate, load_grad):
        load.start()
    stats = []
    for i, load in enumerate(loads):
        load.wait()
        squares = jnp.zeros((strip, 128), jnp.float32)
        for at in range(0, features, 128):
            wide = hidden[i * strip : (i + 1) * strip, at : at + 128].astype(jnp.float32)
            squares += wide * wide
        stats.append(jnp.sum(squares, axis=-1, keepdims=True) / features)
    stat = jnp.concatenate(stats, axis=0)
    mine = pl.ds(pl.multiple_of(place[0] * depth, depth), depth)
    scaled = hidden[:, mine].astype(jnp.float32) * lax.rsqrt(stat + 1e-05)
    normed = (scaled * gain[:, mine]).astype(jnp.bfloat16)
    for load in basis_loads:
        load.wait()
    block = basis.shape[1] // 32
    stores = []
    for x in range(4):
        for z_hi in range(2):
            at = (z_hi * 16 + x * 4) * block
            part = jnp.dot(
                normed, basis[:, at : at + 4 * block], preferred_element_type=jnp.float32
            )
            for y in range(4):
                here = part[:, y * block : (y + 1) * block]
                to = slice(z_hi * block, (z_hi + 1) * block)
                out[x * 4 + y, :, to] = here.astype(jnp.bfloat16)
        here = pl.ds(x * 4, 4)
        stores.append(pltpu.make_async_copy(out.at[here], out_at.at[here], sems.at[6 + x]))
        stores[-1].start()
    load_gate.wait()
    load_grad.wait()
    for at in range(0, tokens, 32):
        here = slice(at, at + 32)
        wide = gate[here, :].astype(jnp.float32)
        wide = grad[here, :].astype(jnp.float32) * (wide / (1.0 + jnp.exp(-wide)))
        up[here, :] = wide.astype(jnp.bfloat16)
    stores.append(pltpu.make_async_copy(up, up_at, sems.at[12]))
    stores[-1].start()
    for store in stores:
        store.wait()


def first_partials(hidden, norm_gain, gate_pre, out_grad, act_basis):
    tokens = hidden.shape[0]
    shape = (16, tokens, act_basis.shape[1] // 16)
    place = lax.axis_index(DP).astype(jnp.int32).reshape(1)
    return pl.pallas_call(
        first_kernel,
        out_shape=(pltpu.HBM(shape, jnp.bfloat16), pltpu.HBM(out_grad.shape, jnp.bfloat16)),
        in_specs=[SMEM, VMEM, ANY, ANY, ANY, ANY],
        out_specs=(ANY, ANY),
        scratch_shapes=[
            pltpu.VMEM(gate_pre.shape, jnp.bfloat16),
            pltpu.VMEM(out_grad.shape, jnp.bfloat16),
            pltpu.VMEM(hidden.shape, jnp.bfloat16),
            pltpu.VMEM(act_basis.shape, jnp.bfloat16),
            pltpu.VMEM(shape, jnp.bfloat16),
            pltpu.VMEM(out_grad.shape, jnp.bfloat16),
            pltpu.SemaphoreType.DMA((13,)),
        ],
        compiler_params=WHOLE,
        name="first",
    )(place, norm_gain.reshape(1, -1), gate_pre, out_grad, hidden, act_basis)


def grad_kernel(count, *refs):
    parts, basis, out_at, rows, out, sem = refs[:count], refs[count], *refs[-4:]
    at = 0
    for part in parts:
        rows[at : at + part.shape[0], :] = part[...]
        at += part.shape[0]
    stores = []
    for at in range(0, basis.shape[1], 256):
        here = pl.ds(at, 256)
        part = jnp.dot(rows[...], basis[:, here], preferred_element_type=jnp.float32)
        out[here, :] = part.T.astype(jnp.bfloat16)
        stores.append(
            pltpu.make_async_copy(out.at[here], out_at.at[here], sem.at[at // 256])
        )
        stores[-1].start()
    for store in stores:
        store.wait()


def grad_partials(parts, basis, after=(), cost=None):
    depth, columns = basis.shape
    tokens = sum(part.shape[0] for part in parts)
    shape = (columns, tokens)
    return pl.pallas_call(
        lambda *refs: grad_kernel(len(parts), *refs),
        out_shape=pltpu.HBM(shape, jnp.bfloat16),
        in_specs=[VMEM] * (len(parts) + 1) + [ANY] * len(after),
        out_specs=ANY,
        scratch_shapes=[
            pltpu.VMEM((tokens, depth), jnp.bfloat16),
            pltpu.VMEM(shape, jnp.bfloat16),
            pltpu.SemaphoreType.DMA((columns // 256,)),
        ],
        compiler_params=PARAMS,
        cost_estimate=cost,
        name="grad",
    )(*parts, basis, *after)


def act_sum_kernel(place, got, kept, given):
    total = got[0].astype(jnp.float32)
    for source in range(1, got.shape[0]):
        total += got[source].astype(jnp.float32)
    low, high = total[:, : kept.shape[1]], total[:, kept.shape[1] :]
    first = place[0] == 0
    kept[...] = jnp.where(first, low, high)
    given[...] = jnp.where(first, high, low)


def act_squares(partials):
    got = lax.all_to_all(partials, ("x", "y"), 0, 0, tiled=True)
    _, tokens, wide = got.shape
    half = jax.ShapeDtypeStruct((tokens, wide // 2), jnp.float32)
    place = lax.axis_index("z_hi").astype(jnp.int32).reshape(1)
    kept, given = pl.pallas_call(
        act_sum_kernel,
        out_shape=(half, half),
        in_specs=[SMEM, VMEM],
        out_specs=(VMEM, VMEM),
        compiler_params=PARAMS,
        cost_estimate=pl.CostEstimate(flops=2 * 10**10, bytes_accessed=10**6, transcendentals=0),
        name="act_sum",
    )(place, got)
    total = kept + shifted(given, "z_hi", 1)
    square = (total * total).astype(jnp.bfloat16)
    return [square] + [shifted(square, "x", step) for step in (1, 2, 3)]


def gate_kernel(*refs):
    del refs


def gated(value, after, place=pltpu.HBM):
    return pl.pallas_call(
        gate_kernel,
        out_shape=place(value.shape, value.dtype),
        in_specs=[ANY] * (1 + len(after)),
        out_specs=ANY,
        input_output_aliases={0: 0},
        compiler_params=PARAMS,
        name="gate",
    )(value, *after)


def exchanged(partial):
    columns, tokens = partial.shape
    return lax.all_to_all(partial.reshape(16, columns // 16, tokens), ("x", "y"), 0, 0, tiled=True)


def squared(got):
    summed = jnp.sum(got.astype(jnp.float32), axis=0)
    total = summed + shifted(summed.astype(jnp.bfloat16), "z_hi", 1).astype(jnp.float32)
    return (total * total).astype(jnp.bfloat16)


def correct_kernel(place, *refs):
    pieces, acts, before, (out, act, both) = refs[:4], refs[4:8], refs[8:-3], refs[-3:]
    _, tokens, block = acts[0].shape
    for i, part in enumerate(acts):
        for behind in range(4):
            here = slice(i * tokens, (i + 1) * tokens), slice(behind * block, (behind + 1) * block)
            act[here] = part[behind]
    rows = pieces[0].shape[0]
    for i, piece in enumerate(pieces):
        both[i * rows : (i + 1) * rows, :] = piece[...]
    every = jnp.dot(both[...], act[...], preferred_element_type=jnp.float32)
    every = every * (1.0 / (8 * tokens))
    for i, y_behind in enumerate((0, *Y_STEPS)):
        at = pl.ds(pl.multiple_of(lax.rem(place[1] + 4 - y_behind, 4) * rows, rows), rows)
        for behind in range(4):
            x = lax.rem(place[0] + 4 - behind, 4)
            here = every[i * rows : (i + 1) * rows, behind * block : (behind + 1) * block]
            if before:
                here = before[0][x, at, :] + here
            out[x, at, :] = here


def corrected(pieces, acts, *before):
    rows, tokens = pieces[0].shape
    block = acts[0].shape[2]
    place = jnp.stack([lax.axis_index("x"), lax.axis_index("y")]).astype(jnp.int32)
    return pl.pallas_call(
        correct_kernel,
        out_shape=jax.ShapeDtypeStruct((4, 4 * rows, block), jnp.float32),
        in_specs=[SMEM] + [VMEM] * (8 + len(before)),
        out_specs=VMEM,
        scratch_shapes=[
            pltpu.VMEM((tokens, 4 * block), jnp.bfloat16),
            pltpu.VMEM((4 * rows, tokens), jnp.bfloat16),
        ],
        compiler_params=PARAMS,
        name="correct",
    )(place, *pieces, *acts, *before)


def per_device(hidden, norm_gain, gate_pre, out_grad, grad_basis, act_basis):
    act_parts, up_grad = first_partials(hidden, norm_gain, gate_pre, out_grad, act_basis)
    near, far, farthest = [shifted(up_grad, "z_lo", step) for step in (1, 2, 3)]
    near_rows = [up_grad, shifted(up_grad, "core", 1), near, shifted(near, "core", 1)]
    far_rows = [far, shifted(far, "core", 1), farthest, shifted(farthest, "core", 1)]
    act_row = act_squares(act_parts)
    cost = pl.CostEstimate(flops=5 * 10**9, bytes_accessed=10**7, transcendentals=0)
    near_got = exchanged(grad_partials(near_rows, grad_basis, (), cost))
    act_own = jnp.stack(act_row)
    far_got = exchanged(gated(grad_partials(far_rows, grad_basis), [act_own]))
    acts = []
    for own in [act_own] + [shifted(act_own, "z_lo", step) for step in (1, 2, 3)]:
        acts += [own, shifted(own, "core", 1)]
    near_sq = squared(near_got)
    near_pieces = [near_sq] + [shifted(near_sq, "y", step) for step in Y_STEPS]
    far_sq = squared(gated(far_got, acts + [near_sq], jax.ShapeDtypeStruct))
    far_pieces = [far_sq] + [shifted(far_sq, "y", step) for step in Y_STEPS]
    out = corrected(far_pieces, acts[4:], corrected(near_pieces, acts[:4]))
    out = lax.all_to_all(out, "x", 0, 0, tiled=True)
    return out.reshape(grad_basis.shape[1], -1)


def solution(mesh):
    fine = Mesh(mesh.devices.reshape(SIZES), AXES)
    placed = (
        P(TENSOR, None),
        P(),
        P(TENSOR, DP),
        P(TENSOR, DP),
        P(DP, TENSOR),
        P(DP, None),
    )
    return jax.shard_map(
        per_device, mesh=fine, in_specs=placed, out_specs=P(TENSOR, DP), check_vma=False
    )
```

```python
import jax
import jax.numpy as jnp
from jax import lax
from jax.experimental import pallas as pl
from jax.experimental.pallas import tpu as pltpu
from jax.sharding import Mesh
from jax.sharding import PartitionSpec as P

AXES = ("z_hi", "x", "y", "z_lo", "core")
SIZES = (2, 4, 4, 4, 2)
DP = ("z_hi", "x", "y")
TENSOR = ("z_lo", "core")
Y_STEPS = (2, 1, 3)
SMEM = pl.BlockSpec(memory_space=pltpu.SMEM)
VMEM = pl.BlockSpec(memory_space=pltpu.VMEM)
ANY = pl.BlockSpec(memory_space=pl.ANY)
PARAMS = pltpu.CompilerParams(vmem_limit_bytes=32 * 1024 * 1024)
WHOLE = pltpu.CompilerParams(vmem_limit_bytes=60 * 1024 * 1024)


def shifted(value, axis, step):
    size = SIZES[AXES.index(axis)]
    return lax.ppermute(value, axis, [(i, (i + step) % size) for i in range(size)])


def first_kernel(place, gain, gate_at, grad_at, hidden_at, basis_at, out_at, up_at,
                 gate, grad, hidden, basis, out, up, sems):
    tokens, features = hidden.shape
    depth = basis.shape[0]
    strip = tokens // 2
    quarter = depth // 4
    loads = [
        pltpu.make_async_copy(hidden_at.at[here], hidden.at[here], sems.at[i])
        for i, here in enumerate(pl.ds(at, strip) for at in range(0, tokens, strip))
    ]
    basis_loads = [
        pltpu.make_async_copy(basis_at.at[here], basis.at[here], sems.at[2 + i])
        for i, here in enumerate(pl.ds(at, quarter) for at in range(0, depth, quarter))
    ]
    load_gate = pltpu.make_async_copy(gate_at, gate, sems.at[10])
    load_grad = pltpu.make_async_copy(grad_at, grad, sems.at[11])
    for load in (*loads, *basis_loads, load_gate, load_grad):
        load.start()
    stats = []
    for i, load in enumerate(loads):
        load.wait()
        squares = jnp.zeros((strip, 128), jnp.float32)
        for at in range(0, features, 128):
            wide = hidden[i * strip : (i + 1) * strip, at : at + 128].astype(jnp.float32)
            squares += wide * wide
        stats.append(jnp.sum(squares, axis=-1, keepdims=True) / features)
    stat = jnp.concatenate(stats, axis=0)
    mine = pl.ds(pl.multiple_of(place[0] * depth, depth), depth)
    scaled = hidden[:, mine].astype(jnp.float32) * lax.rsqrt(stat + 1e-05)
    normed = (scaled * gain[:, mine]).astype(jnp.bfloat16)
    for load in basis_loads:
        load.wait()
    block = basis.shape[1] // 32
    stores = []
    for x in range(4):
        for z_hi in range(2):
            at = (z_hi * 16 + x * 4) * block
            part = jnp.dot(
                normed, basis[:, at : at + 4 * block], preferred_element_type=jnp.float32
            )
            for y in range(4):
                here = part[:, y * block : (y + 1) * block]
                to = slice(z_hi * block, (z_hi + 1) * block)
                out[x * 4 + y, :, to] = here.astype(jnp.bfloat16)
        here = pl.ds(x * 4, 4)
        stores.append(pltpu.make_async_copy(out.at[here], out_at.at[here], sems.at[6 + x]))
        stores[-1].start()
    load_gate.wait()
    load_grad.wait()
    for at in range(0, tokens, 32):
        here = slice(at, at + 32)
        wide = gate[here, :].astype(jnp.float32)
        wide = grad[here, :].astype(jnp.float32) * (wide / (1.0 + jnp.exp(-wide)))
        up[here, :] = wide.astype(jnp.bfloat16)
    stores.append(pltpu.make_async_copy(up, up_at, sems.at[12]))
    stores[-1].start()
    for store in stores:
        store.wait()


def first_partials(hidden, norm_gain, gate_pre, out_grad, act_basis):
    tokens = hidden.shape[0]
    shape = (16, tokens, act_basis.shape[1] // 16)
    place = lax.axis_index(DP).astype(jnp.int32).reshape(1)
    return pl.pallas_call(
        first_kernel,
        out_shape=(pltpu.HBM(shape, jnp.bfloat16), pltpu.HBM(out_grad.shape, jnp.bfloat16)),
        in_specs=[SMEM, VMEM, ANY, ANY, ANY, ANY],
        out_specs=(ANY, ANY),
        scratch_shapes=[
            pltpu.VMEM(gate_pre.shape, jnp.bfloat16),
            pltpu.VMEM(out_grad.shape, jnp.bfloat16),
            pltpu.VMEM(hidden.shape, jnp.bfloat16),
            pltpu.VMEM(act_basis.shape, jnp.bfloat16),
            pltpu.VMEM(shape, jnp.bfloat16),
            pltpu.VMEM(out_grad.shape, jnp.bfloat16),
            pltpu.SemaphoreType.DMA((13,)),
        ],
        compiler_params=WHOLE,
        name="first",
    )(place, norm_gain.reshape(1, -1), gate_pre, out_grad, hidden, act_basis)


def grad_kernel(count, *refs):
    parts, basis, out_at, rows, out, sem = refs[:count], refs[count], *refs[-4:]
    at = 0
    for part in parts:
        rows[at : at + part.shape[0], :] = part[...]
        at += part.shape[0]
    stores = []
    for at in range(0, basis.shape[1], 256):
        here = pl.ds(at, 256)
        part = jnp.dot(rows[...], basis[:, here], preferred_element_type=jnp.float32)
        out[here, :] = part.T.astype(jnp.bfloat16)
        stores.append(
            pltpu.make_async_copy(out.at[here], out_at.at[here], sem.at[at // 256])
        )
        stores[-1].start()
    for store in stores:
        store.wait()


def grad_partials(parts, basis, after=(), cost=None):
    depth, columns = basis.shape
    tokens = sum(part.shape[0] for part in parts)
    shape = (columns, tokens)
    return pl.pallas_call(
        lambda *refs: grad_kernel(len(parts), *refs),
        out_shape=pltpu.HBM(shape, jnp.bfloat16),
        in_specs=[VMEM] * (len(parts) + 1) + [ANY] * len(after),
        out_specs=ANY,
        scratch_shapes=[
            pltpu.VMEM((tokens, depth), jnp.bfloat16),
            pltpu.VMEM(shape, jnp.bfloat16),
            pltpu.SemaphoreType.DMA((columns // 256,)),
        ],
        compiler_params=PARAMS,
        cost_estimate=cost,
        name="grad",
    )(*parts, basis, *after)


def act_sum_kernel(place, got, kept, given):
    total = got[0].astype(jnp.float32)
    for source in range(1, got.shape[0]):
        total += got[source].astype(jnp.float32)
    low, high = total[:, : kept.shape[1]], total[:, kept.shape[1] :]
    first = place[0] == 0
    kept[...] = jnp.where(first, low, high)
    given[...] = jnp.where(first, high, low)


def act_squares(partials):
    got = lax.all_to_all(partials, ("x", "y"), 0, 0, tiled=True)
    _, tokens, wide = got.shape
    half = jax.ShapeDtypeStruct((tokens, wide // 2), jnp.float32)
    place = lax.axis_index("z_hi").astype(jnp.int32).reshape(1)
    kept, given = pl.pallas_call(
        act_sum_kernel,
        out_shape=(half, half),
        in_specs=[SMEM, VMEM],
        out_specs=(VMEM, VMEM),
        compiler_params=PARAMS,
        cost_estimate=pl.CostEstimate(flops=2 * 10**10, bytes_accessed=10**6, transcendentals=0),
        name="act_sum",
    )(place, got)
    total = kept + shifted(given, "z_hi", 1)
    square = (total * total).astype(jnp.bfloat16)
    return [square] + [shifted(square, "x", step) for step in (1, 2, 3)]


def gate_kernel(*refs):
    del refs


def gated(value, after, place=pltpu.HBM):
    return pl.pallas_call(
        gate_kernel,
        out_shape=place(value.shape, value.dtype),
        in_specs=[ANY] * (1 + len(after)),
        out_specs=ANY,
        input_output_aliases={0: 0},
        compiler_params=PARAMS,
        name="gate",
    )(value, *after)


def exchanged(partial):
    columns, tokens = partial.shape
    return lax.all_to_all(partial.reshape(16, columns // 16, tokens), ("x", "y"), 0, 0, tiled=True)


def squared(got):
    summed = jnp.sum(got.astype(jnp.float32), axis=0)
    total = summed + shifted(summed.astype(jnp.bfloat16), "z_hi", 1).astype(jnp.float32)
    return (total * total).astype(jnp.bfloat16)


def correct_kernel(place, *refs):
    pieces, acts, before, (out, act, both) = refs[:4], refs[4:8], refs[8:-3], refs[-3:]
    _, tokens, block = acts[0].shape
    for i, part in enumerate(acts):
        for behind in range(4):
            here = slice(i * tokens, (i + 1) * tokens), slice(behind * block, (behind + 1) * block)
            act[here] = part[behind]
    rows = pieces[0].shape[0]
    for i, piece in enumerate(pieces):
        both[i * rows : (i + 1) * rows, :] = piece[...]
    every = jnp.dot(both[...], act[...], preferred_element_type=jnp.float32)
    every = every * (1.0 / (8 * tokens))
    for i, y_behind in enumerate((0, *Y_STEPS)):
        at = pl.ds(pl.multiple_of(lax.rem(place[1] + 4 - y_behind, 4) * rows, rows), rows)
        for behind in range(4):
            x = lax.rem(place[0] + 4 - behind, 4)
            here = every[i * rows : (i + 1) * rows, behind * block : (behind + 1) * block]
            if before:
                here = before[0][x, at, :] + here
            out[x, at, :] = here


def corrected(pieces, acts, *before):
    rows, tokens = pieces[0].shape
    block = acts[0].shape[2]
    place = jnp.stack([lax.axis_index("x"), lax.axis_index("y")]).astype(jnp.int32)
    return pl.pallas_call(
        correct_kernel,
        out_shape=jax.ShapeDtypeStruct((4, 4 * rows, block), jnp.float32),
        in_specs=[SMEM] + [VMEM] * (8 + len(before)),
        out_specs=VMEM,
        scratch_shapes=[
            pltpu.VMEM((tokens, 4 * block), jnp.bfloat16),
            pltpu.VMEM((4 * rows, tokens), jnp.bfloat16),
        ],
        compiler_params=PARAMS,
        name="correct",
    )(place, *pieces, *acts, *before)


def per_device(hidden, norm_gain, gate_pre, out_grad, grad_basis, act_basis):
    act_parts, up_grad = first_partials(hidden, norm_gain, gate_pre, out_grad, act_basis)
    near, far, farthest = [shifted(up_grad, "z_lo", step) for step in (1, 2, 3)]
    near_rows = [up_grad, shifted(up_grad, "core", 1), near, shifted(near, "core", 1)]
    far_rows = [far, shifted(far, "core", 1), farthest, shifted(farthest, "core", 1)]
    act_row = act_squares(act_parts)
    cost = pl.CostEstimate(flops=8 * 10**9, bytes_accessed=10**7, transcendentals=0)
    near_got = exchanged(grad_partials(near_rows, grad_basis, (), cost))
    act_own = jnp.stack(act_row)
    far_got = exchanged(gated(grad_partials(far_rows, grad_basis), [act_own]))
    acts = []
    for own in [act_own] + [shifted(act_own, "z_lo", step) for step in (1, 2, 3)]:
        acts += [own, shifted(own, "core", 1)]
    near_sq = squared(near_got)
    near_pieces = [near_sq] + [shifted(near_sq, "y", step) for step in Y_STEPS]
    far_got = gated(far_got, acts + [near_sq], jax.ShapeDtypeStruct)
    summed = jnp.sum(far_got.astype(jnp.float32), axis=0)
    other = shifted(summed.astype(jnp.bfloat16), "z_hi", 1)
    total = summed + gated(other, near_pieces, jax.ShapeDtypeStruct).astype(jnp.float32)
    far_sq = (total * total).astype(jnp.bfloat16)
    far_pieces = [far_sq] + [shifted(far_sq, "y", step) for step in Y_STEPS]
    out = corrected(far_pieces, acts[4:], corrected(near_pieces, acts[:4]))
    out = lax.all_to_all(out, "x", 0, 0, tiled=True)
    return out.reshape(grad_basis.shape[1], -1)


def solution(mesh):
    fine = Mesh(mesh.devices.reshape(SIZES), AXES)
    placed = (
        P(TENSOR, None),
        P(),
        P(TENSOR, DP),
        P(TENSOR, DP),
        P(DP, TENSOR),
        P(DP, None),
    )
    return jax.shard_map(
        per_device, mesh=fine, in_specs=placed, out_specs=P(TENSOR, DP), check_vma=False
    )
```

```python
import jax
import jax.numpy as jnp
from jax import lax
from jax.experimental import pallas as pl
from jax.experimental.pallas import tpu as pltpu
from jax.sharding import Mesh
from jax.sharding import PartitionSpec as P

AXES = ("z_hi", "x", "y", "z_lo", "core")
SIZES = (2, 4, 4, 4, 2)
DP = ("z_hi", "x", "y")
TENSOR = ("z_lo", "core")
Y_STEPS = (2, 1, 3)
SMEM = pl.BlockSpec(memory_space=pltpu.SMEM)
VMEM = pl.BlockSpec(memory_space=pltpu.VMEM)
ANY = pl.BlockSpec(memory_space=pl.ANY)
PARAMS = pltpu.CompilerParams(vmem_limit_bytes=32 * 1024 * 1024)
WHOLE = pltpu.CompilerParams(vmem_limit_bytes=60 * 1024 * 1024)


def shifted(value, axis, step):
    size = SIZES[AXES.index(axis)]
    return lax.ppermute(value, axis, [(i, (i + step) % size) for i in range(size)])


def first_kernel(place, gain, gate_at, grad_at, hidden_at, basis_at, out_at, up_at,
                 gate, grad, hidden, basis, out, up, sems):
    tokens, features = hidden.shape
    depth = basis.shape[0]
    strip = tokens // 2
    quarter = depth // 4
    loads = [
        pltpu.make_async_copy(hidden_at.at[here], hidden.at[here], sems.at[i])
        for i, here in enumerate(pl.ds(at, strip) for at in range(0, tokens, strip))
    ]
    basis_loads = [
        pltpu.make_async_copy(basis_at.at[here], basis.at[here], sems.at[2 + i])
        for i, here in enumerate(pl.ds(at, quarter) for at in range(0, depth, quarter))
    ]
    load_gate = pltpu.make_async_copy(gate_at, gate, sems.at[10])
    load_grad = pltpu.make_async_copy(grad_at, grad, sems.at[11])
    for load in (*loads, *basis_loads, load_gate, load_grad):
        load.start()
    stats = []
    for i, load in enumerate(loads):
        load.wait()
        squares = jnp.zeros((strip, 128), jnp.float32)
        for at in range(0, features, 128):
            wide = hidden[i * strip : (i + 1) * strip, at : at + 128].astype(jnp.float32)
            squares += wide * wide
        stats.append(jnp.sum(squares, axis=-1, keepdims=True) / features)
    stat = jnp.concatenate(stats, axis=0)
    mine = pl.ds(pl.multiple_of(place[0] * depth, depth), depth)
    scaled = hidden[:, mine].astype(jnp.float32) * lax.rsqrt(stat + 1e-05)
    normed = (scaled * gain[:, mine]).astype(jnp.bfloat16)
    for load in basis_loads:
        load.wait()
    block = basis.shape[1] // 32
    stores = []
    for x in range(4):
        for z_hi in range(2):
            at = (z_hi * 16 + x * 4) * block
            part = jnp.dot(
                normed, basis[:, at : at + 4 * block], preferred_element_type=jnp.float32
            )
            for y in range(4):
                here = part[:, y * block : (y + 1) * block]
                to = slice(z_hi * block, (z_hi + 1) * block)
                out[x * 4 + y, :, to] = here.astype(jnp.bfloat16)
        here = pl.ds(x * 4, 4)
        stores.append(pltpu.make_async_copy(out.at[here], out_at.at[here], sems.at[6 + x]))
        stores[-1].start()
    load_gate.wait()
    load_grad.wait()
    for at in range(0, tokens, 32):
        here = slice(at, at + 32)
        wide = gate[here, :].astype(jnp.float32)
        wide = grad[here, :].astype(jnp.float32) * (wide / (1.0 + jnp.exp(-wide)))
        up[here, :] = wide.astype(jnp.bfloat16)
    stores.append(pltpu.make_async_copy(up, up_at, sems.at[12]))
    stores[-1].start()
    for store in stores:
        store.wait()


def first_partials(hidden, norm_gain, gate_pre, out_grad, act_basis):
    tokens = hidden.shape[0]
    shape = (16, tokens, act_basis.shape[1] // 16)
    place = lax.axis_index(DP).astype(jnp.int32).reshape(1)
    return pl.pallas_call(
        first_kernel,
        out_shape=(pltpu.HBM(shape, jnp.bfloat16), pltpu.HBM(out_grad.shape, jnp.bfloat16)),
        in_specs=[SMEM, VMEM, ANY, ANY, ANY, ANY],
        out_specs=(ANY, ANY),
        scratch_shapes=[
            pltpu.VMEM(gate_pre.shape, jnp.bfloat16),
            pltpu.VMEM(out_grad.shape, jnp.bfloat16),
            pltpu.VMEM(hidden.shape, jnp.bfloat16),
            pltpu.VMEM(act_basis.shape, jnp.bfloat16),
            pltpu.VMEM(shape, jnp.bfloat16),
            pltpu.VMEM(out_grad.shape, jnp.bfloat16),
            pltpu.SemaphoreType.DMA((13,)),
        ],
        compiler_params=WHOLE,
        name="first",
    )(place, norm_gain.reshape(1, -1), gate_pre, out_grad, hidden, act_basis)


def grad_kernel(count, *refs):
    parts, basis, out_at, rows, out, sem = refs[:count], refs[count], *refs[-4:]
    at = 0
    for part in parts:
        rows[at : at + part.shape[0], :] = part[...]
        at += part.shape[0]
    stores = []
    for at in range(0, basis.shape[1], 256):
        here = pl.ds(at, 256)
        part = jnp.dot(rows[...], basis[:, here], preferred_element_type=jnp.float32)
        out[here, :] = part.T.astype(jnp.bfloat16)
        stores.append(
            pltpu.make_async_copy(out.at[here], out_at.at[here], sem.at[at // 256])
        )
        stores[-1].start()
    for store in stores:
        store.wait()


def grad_partials(parts, basis, after=(), cost=None):
    depth, columns = basis.shape
    tokens = sum(part.shape[0] for part in parts)
    shape = (columns, tokens)
    return pl.pallas_call(
        lambda *refs: grad_kernel(len(parts), *refs),
        out_shape=pltpu.HBM(shape, jnp.bfloat16),
        in_specs=[VMEM] * (len(parts) + 1) + [ANY] * len(after),
        out_specs=ANY,
        scratch_shapes=[
            pltpu.VMEM((tokens, depth), jnp.bfloat16),
            pltpu.VMEM(shape, jnp.bfloat16),
            pltpu.SemaphoreType.DMA((columns // 256,)),
        ],
        compiler_params=PARAMS,
        cost_estimate=cost,
        name="grad",
    )(*parts, basis, *after)


def act_sum_kernel(place, got, kept, given):
    total = got[0].astype(jnp.float32)
    for source in range(1, got.shape[0]):
        total += got[source].astype(jnp.float32)
    low, high = total[:, : kept.shape[1]], total[:, kept.shape[1] :]
    first = place[0] == 0
    kept[...] = jnp.where(first, low, high)
    given[...] = jnp.where(first, high, low)


def act_squares(partials):
    got = lax.all_to_all(partials, ("x", "y"), 0, 0, tiled=True)
    _, tokens, wide = got.shape
    half = jax.ShapeDtypeStruct((tokens, wide // 2), jnp.float32)
    place = lax.axis_index("z_hi").astype(jnp.int32).reshape(1)
    kept, given = pl.pallas_call(
        act_sum_kernel,
        out_shape=(half, half),
        in_specs=[SMEM, VMEM],
        out_specs=(VMEM, VMEM),
        compiler_params=PARAMS,
        cost_estimate=pl.CostEstimate(flops=2 * 10**10, bytes_accessed=10**6, transcendentals=0),
        name="act_sum",
    )(place, got)
    total = kept + shifted(given, "z_hi", 1)
    square = (total * total).astype(jnp.bfloat16)
    return [square] + [shifted(square, "x", step) for step in (1, 2, 3)]


def gate_kernel(*refs):
    del refs


def gated(value, after, place=pltpu.HBM):
    return pl.pallas_call(
        gate_kernel,
        out_shape=place(value.shape, value.dtype),
        in_specs=[ANY] * (1 + len(after)),
        out_specs=ANY,
        input_output_aliases={0: 0},
        compiler_params=PARAMS,
        name="gate",
    )(value, *after)


def exchanged(partial):
    columns, tokens = partial.shape
    return lax.all_to_all(partial.reshape(16, columns // 16, tokens), ("x", "y"), 0, 0, tiled=True)


def squared(got):
    summed = jnp.sum(got.astype(jnp.float32), axis=0)
    total = summed + shifted(summed.astype(jnp.bfloat16), "z_hi", 1).astype(jnp.float32)
    return (total * total).astype(jnp.bfloat16)


def correct_kernel(place, *refs):
    pieces, acts, before, (out, act, both) = refs[:4], refs[4:8], refs[8:-3], refs[-3:]
    _, tokens, block = acts[0].shape
    for i, part in enumerate(acts):
        for behind in range(4):
            here = slice(i * tokens, (i + 1) * tokens), slice(behind * block, (behind + 1) * block)
            act[here] = part[behind]
    rows = pieces[0].shape[0]
    for i, piece in enumerate(pieces):
        both[i * rows : (i + 1) * rows, :] = piece[...]
    every = jnp.dot(both[...], act[...], preferred_element_type=jnp.float32)
    every = every * (1.0 / (8 * tokens))
    for i, y_behind in enumerate((0, *Y_STEPS)):
        at = pl.ds(pl.multiple_of(lax.rem(place[1] + 4 - y_behind, 4) * rows, rows), rows)
        for behind in range(4):
            x = lax.rem(place[0] + 4 - behind, 4)
            here = every[i * rows : (i + 1) * rows, behind * block : (behind + 1) * block]
            if before:
                here = before[0][x, at, :] + here
            out[x, at, :] = here


def corrected(pieces, acts, *before):
    rows, tokens = pieces[0].shape
    block = acts[0].shape[2]
    place = jnp.stack([lax.axis_index("x"), lax.axis_index("y")]).astype(jnp.int32)
    return pl.pallas_call(
        correct_kernel,
        out_shape=jax.ShapeDtypeStruct((4, 4 * rows, block), jnp.float32),
        in_specs=[SMEM] + [VMEM] * (8 + len(before)),
        out_specs=VMEM,
        scratch_shapes=[
            pltpu.VMEM((tokens, 4 * block), jnp.bfloat16),
            pltpu.VMEM((4 * rows, tokens), jnp.bfloat16),
        ],
        compiler_params=PARAMS,
        name="correct",
    )(place, *pieces, *acts, *before)


def per_device(hidden, norm_gain, gate_pre, out_grad, grad_basis, act_basis):
    act_parts, up_grad = first_partials(hidden, norm_gain, gate_pre, out_grad, act_basis)
    near, far, farthest = [shifted(up_grad, "z_lo", step) for step in (1, 2, 3)]
    near_rows = [up_grad, shifted(up_grad, "core", 1), near, shifted(near, "core", 1)]
    far_rows = [far, shifted(far, "core", 1), farthest, shifted(farthest, "core", 1)]
    act_row = act_squares(act_parts)
    cost = pl.CostEstimate(flops=8 * 10**9, bytes_accessed=10**7, transcendentals=0)
    near_got = exchanged(grad_partials(near_rows, grad_basis, (), cost))
    act_own = jnp.stack(act_row)
    far_got = exchanged(gated(grad_partials(far_rows, grad_basis), [act_own]))
    acts = []
    for own in [act_own] + [shifted(act_own, "z_lo", step) for step in (1, 2, 3)]:
        acts += [own, shifted(own, "core", 1)]
    near_sq = squared(near_got)
    near_pieces = [near_sq] + [shifted(near_sq, "y", step) for step in Y_STEPS]
    far_got = gated(far_got, acts + [near_sq], jax.ShapeDtypeStruct)
    summed = jnp.sum(far_got.astype(jnp.float32), axis=0)
    other = shifted(summed.astype(jnp.bfloat16), "z_hi", 1)
    total = summed + gated(other, near_pieces[1:2], jax.ShapeDtypeStruct).astype(jnp.float32)
    far_sq = (total * total).astype(jnp.bfloat16)
    far_pieces = [far_sq] + [shifted(far_sq, "y", step) for step in Y_STEPS]
    out = corrected(far_pieces, acts[4:], corrected(near_pieces, acts[:4]))
    out = lax.all_to_all(out, "x", 0, 0, tiled=True)
    return out.reshape(grad_basis.shape[1], -1)


def solution(mesh):
    fine = Mesh(mesh.devices.reshape(SIZES), AXES)
    placed = (
        P(TENSOR, None),
        P(),
        P(TENSOR, DP),
        P(TENSOR, DP),
        P(DP, TENSOR),
        P(DP, None),
    )
    return jax.shard_map(
        per_device, mesh=fine, in_specs=placed, out_specs=P(TENSOR, DP), check_vma=False
    )
```

```python
import jax
import jax.numpy as jnp
from jax import lax
from jax.experimental import pallas as pl
from jax.experimental.pallas import tpu as pltpu
from jax.sharding import Mesh
from jax.sharding import PartitionSpec as P

AXES = ("z_hi", "x", "y", "z_lo", "core")
SIZES = (2, 4, 4, 4, 2)
DP = ("z_hi", "x", "y")
TENSOR = ("z_lo", "core")
Y_STEPS = (2, 1, 3)
SMEM = pl.BlockSpec(memory_space=pltpu.SMEM)
VMEM = pl.BlockSpec(memory_space=pltpu.VMEM)
ANY = pl.BlockSpec(memory_space=pl.ANY)
PARAMS = pltpu.CompilerParams(vmem_limit_bytes=32 * 1024 * 1024)
WHOLE = pltpu.CompilerParams(vmem_limit_bytes=60 * 1024 * 1024)


def shifted(value, axis, step):
    size = SIZES[AXES.index(axis)]
    return lax.ppermute(value, axis, [(i, (i + step) % size) for i in range(size)])


def first_kernel(place, gain, gate_at, grad_at, hidden_at, basis_at, out_at, up_at,
                 gate, grad, hidden, basis, out, up, sems):
    tokens, features = hidden.shape
    depth = basis.shape[0]
    strip = tokens // 2
    quarter = depth // 4
    loads = [
        pltpu.make_async_copy(hidden_at.at[here], hidden.at[here], sems.at[i])
        for i, here in enumerate(pl.ds(at, strip) for at in range(0, tokens, strip))
    ]
    basis_loads = [
        pltpu.make_async_copy(basis_at.at[here], basis.at[here], sems.at[2 + i])
        for i, here in enumerate(pl.ds(at, quarter) for at in range(0, depth, quarter))
    ]
    load_gate = pltpu.make_async_copy(gate_at, gate, sems.at[10])
    load_grad = pltpu.make_async_copy(grad_at, grad, sems.at[11])
    for load in (*loads, *basis_loads, load_gate, load_grad):
        load.start()
    stats = []
    for i, load in enumerate(loads):
        load.wait()
        squares = jnp.zeros((strip, 128), jnp.float32)
        for at in range(0, features, 128):
            wide = hidden[i * strip : (i + 1) * strip, at : at + 128].astype(jnp.float32)
            squares += wide * wide
        stats.append(jnp.sum(squares, axis=-1, keepdims=True) / features)
    stat = jnp.concatenate(stats, axis=0)
    mine = pl.ds(pl.multiple_of(place[0] * depth, depth), depth)
    scaled = hidden[:, mine].astype(jnp.float32) * lax.rsqrt(stat + 1e-05)
    normed = (scaled * gain[:, mine]).astype(jnp.bfloat16)
    for load in basis_loads:
        load.wait()
    block = basis.shape[1] // 32
    stores = []
    for x in range(4):
        for z_hi in range(2):
            at = (z_hi * 16 + x * 4) * block
            part = jnp.dot(
                normed, basis[:, at : at + 4 * block], preferred_element_type=jnp.float32
            )
            for y in range(4):
                here = part[:, y * block : (y + 1) * block]
                to = slice(z_hi * block, (z_hi + 1) * block)
                out[x * 4 + y, :, to] = here.astype(jnp.bfloat16)
        here = pl.ds(x * 4, 4)
        stores.append(pltpu.make_async_copy(out.at[here], out_at.at[here], sems.at[6 + x]))
        stores[-1].start()
    load_gate.wait()
    load_grad.wait()
    for at in range(0, tokens, 32):
        here = slice(at, at + 32)
        wide = gate[here, :].astype(jnp.float32)
        wide = grad[here, :].astype(jnp.float32) * (wide / (1.0 + jnp.exp(-wide)))
        up[here, :] = wide.astype(jnp.bfloat16)
    stores.append(pltpu.make_async_copy(up, up_at, sems.at[12]))
    stores[-1].start()
    for store in stores:
        store.wait()


def first_partials(hidden, norm_gain, gate_pre, out_grad, act_basis):
    tokens = hidden.shape[0]
    shape = (16, tokens, act_basis.shape[1] // 16)
    place = lax.axis_index(DP).astype(jnp.int32).reshape(1)
    return pl.pallas_call(
        first_kernel,
        out_shape=(pltpu.HBM(shape, jnp.bfloat16), pltpu.HBM(out_grad.shape, jnp.bfloat16)),
        in_specs=[SMEM, VMEM, ANY, ANY, ANY, ANY],
        out_specs=(ANY, ANY),
        scratch_shapes=[
            pltpu.VMEM(gate_pre.shape, jnp.bfloat16),
            pltpu.VMEM(out_grad.shape, jnp.bfloat16),
            pltpu.VMEM(hidden.shape, jnp.bfloat16),
            pltpu.VMEM(act_basis.shape, jnp.bfloat16),
            pltpu.VMEM(shape, jnp.bfloat16),
            pltpu.VMEM(out_grad.shape, jnp.bfloat16),
            pltpu.SemaphoreType.DMA((13,)),
        ],
        compiler_params=WHOLE,
        name="first",
    )(place, norm_gain.reshape(1, -1), gate_pre, out_grad, hidden, act_basis)


def grad_kernel(count, *refs):
    parts, basis, out_at, rows, out, sem = refs[:count], refs[count], *refs[-4:]
    at = 0
    for part in parts:
        rows[at : at + part.shape[0], :] = part[...]
        at += part.shape[0]
    stores = []
    for at in range(0, basis.shape[1], 256):
        here = pl.ds(at, 256)
        part = jnp.dot(rows[...], basis[:, here], preferred_element_type=jnp.float32)
        out[here, :] = part.T.astype(jnp.bfloat16)
        stores.append(
            pltpu.make_async_copy(out.at[here], out_at.at[here], sem.at[at // 256])
        )
        stores[-1].start()
    for store in stores:
        store.wait()


def grad_partials(parts, basis, after=(), cost=None):
    depth, columns = basis.shape
    tokens = sum(part.shape[0] for part in parts)
    shape = (columns, tokens)
    return pl.pallas_call(
        lambda *refs: grad_kernel(len(parts), *refs),
        out_shape=pltpu.HBM(shape, jnp.bfloat16),
        in_specs=[VMEM] * (len(parts) + 1) + [ANY] * len(after),
        out_specs=ANY,
        scratch_shapes=[
            pltpu.VMEM((tokens, depth), jnp.bfloat16),
            pltpu.VMEM(shape, jnp.bfloat16),
            pltpu.SemaphoreType.DMA((columns // 256,)),
        ],
        compiler_params=PARAMS,
        cost_estimate=cost,
        name="grad",
    )(*parts, basis, *after)


def act_sum_kernel(place, got, kept, given):
    total = got[0].astype(jnp.float32)
    for source in range(1, got.shape[0]):
        total += got[source].astype(jnp.float32)
    low, high = total[:, : kept.shape[1]], total[:, kept.shape[1] :]
    first = place[0] == 0
    kept[...] = jnp.where(first, low, high)
    given[...] = jnp.where(first, high, low)


def act_squares(partials):
    got = lax.all_to_all(partials, ("x", "y"), 0, 0, tiled=True)
    _, tokens, wide = got.shape
    half = jax.ShapeDtypeStruct((tokens, wide // 2), jnp.float32)
    place = lax.axis_index("z_hi").astype(jnp.int32).reshape(1)
    kept, given = pl.pallas_call(
        act_sum_kernel,
        out_shape=(half, half),
        in_specs=[SMEM, VMEM],
        out_specs=(VMEM, VMEM),
        compiler_params=PARAMS,
        cost_estimate=pl.CostEstimate(flops=2 * 10**10, bytes_accessed=10**6, transcendentals=0),
        name="act_sum",
    )(place, got)
    total = kept + shifted(given, "z_hi", 1)
    square = (total * total).astype(jnp.bfloat16)
    return [square] + [shifted(square, "x", step) for step in (1, 2, 3)]


def gate_kernel(*refs):
    del refs


def gated(value, after, place=pltpu.HBM):
    return pl.pallas_call(
        gate_kernel,
        out_shape=place(value.shape, value.dtype),
        in_specs=[ANY] * (1 + len(after)),
        out_specs=ANY,
        input_output_aliases={0: 0},
        compiler_params=PARAMS,
        name="gate",
    )(value, *after)


def exchanged(partial):
    columns, tokens = partial.shape
    return lax.all_to_all(partial.reshape(16, columns // 16, tokens), ("x", "y"), 0, 0, tiled=True)


def squared(got):
    summed = jnp.sum(got.astype(jnp.float32), axis=0)
    total = summed + shifted(summed.astype(jnp.bfloat16), "z_hi", 1).astype(jnp.float32)
    return (total * total).astype(jnp.bfloat16)


def correct_kernel(place, *refs):
    pieces, acts, before, (out, act, both) = refs[:4], refs[4:8], refs[8:-3], refs[-3:]
    _, tokens, block = acts[0].shape
    for i, part in enumerate(acts):
        for behind in range(4):
            here = slice(i * tokens, (i + 1) * tokens), slice(behind * block, (behind + 1) * block)
            act[here] = part[behind]
    rows = pieces[0].shape[0]
    for i, piece in enumerate(pieces):
        both[i * rows : (i + 1) * rows, :] = piece[...]
    every = jnp.dot(both[...], act[...], preferred_element_type=jnp.float32)
    every = every * (1.0 / (8 * tokens))
    for i, y_behind in enumerate((0, *Y_STEPS)):
        at = pl.ds(pl.multiple_of(lax.rem(place[1] + 4 - y_behind, 4) * rows, rows), rows)
        for behind in range(4):
            x = lax.rem(place[0] + 4 - behind, 4)
            here = every[i * rows : (i + 1) * rows, behind * block : (behind + 1) * block]
            if before:
                here = before[0][x, at, :] + here
            out[x, at, :] = here


def corrected(pieces, acts, *before):
    rows, tokens = pieces[0].shape
    block = acts[0].shape[2]
    place = jnp.stack([lax.axis_index("x"), lax.axis_index("y")]).astype(jnp.int32)
    return pl.pallas_call(
        correct_kernel,
        out_shape=jax.ShapeDtypeStruct((4, 4 * rows, block), jnp.float32),
        in_specs=[SMEM] + [VMEM] * (8 + len(before)),
        out_specs=VMEM,
        scratch_shapes=[
            pltpu.VMEM((tokens, 4 * block), jnp.bfloat16),
            pltpu.VMEM((4 * rows, tokens), jnp.bfloat16),
        ],
        compiler_params=PARAMS,
        name="correct",
    )(place, *pieces, *acts, *before)


def per_device(hidden, norm_gain, gate_pre, out_grad, grad_basis, act_basis):
    act_parts, up_grad = first_partials(hidden, norm_gain, gate_pre, out_grad, act_basis)
    near, far, farthest = [shifted(up_grad, "z_lo", step) for step in (1, 2, 3)]
    near_rows = [up_grad, shifted(up_grad, "core", 1), near, shifted(near, "core", 1)]
    far_rows = [far, shifted(far, "core", 1), farthest, shifted(farthest, "core", 1)]
    act_row = act_squares(act_parts)
    cost = pl.CostEstimate(flops=8 * 10**9, bytes_accessed=10**7, transcendentals=0)
    near_got = exchanged(grad_partials(near_rows, grad_basis, (), cost))
    act_own = jnp.stack(act_row)
    far_got = exchanged(gated(grad_partials(far_rows, grad_basis), [act_own]))
    near_sum = jnp.sum(near_got.astype(jnp.float32), axis=0)
    act_own = gated(act_own, [near_sum], jax.ShapeDtypeStruct)
    acts = []
    for own in [act_own] + [shifted(act_own, "z_lo", step) for step in (1, 2, 3)]:
        acts += [own, shifted(own, "core", 1)]
    total = near_sum + shifted(near_sum.astype(jnp.bfloat16), "z_hi", 1).astype(jnp.float32)
    near_sq = (total * total).astype(jnp.bfloat16)
    near_pieces = [near_sq] + [shifted(near_sq, "y", step) for step in Y_STEPS]
    far_got = gated(far_got, acts + [near_sq], jax.ShapeDtypeStruct)
    summed = jnp.sum(far_got.astype(jnp.float32), axis=0)
    other = shifted(summed.astype(jnp.bfloat16), "z_hi", 1)
    total = summed + gated(other, near_pieces[1:2], jax.ShapeDtypeStruct).astype(jnp.float32)
    far_sq = (total * total).astype(jnp.bfloat16)
    far_pieces = [far_sq] + [shifted(far_sq, "y", step) for step in Y_STEPS]
    out = corrected(far_pieces, acts[4:], corrected(near_pieces, acts[:4]))
    out = lax.all_to_all(out, "x", 0, 0, tiled=True)
    return out.reshape(grad_basis.shape[1], -1)


def solution(mesh):
    fine = Mesh(mesh.devices.reshape(SIZES), AXES)
    placed = (
        P(TENSOR, None),
        P(),
        P(TENSOR, DP),
        P(TENSOR, DP),
        P(DP, TENSOR),
        P(DP, None),
    )
    return jax.shard_map(
        per_device, mesh=fine, in_specs=placed, out_specs=P(TENSOR, DP), check_vma=False
    )
```
